128 devices in a mesh: tensor: 8 (over z, x_hi), tokens: 16 (over y, x_lo, core).
Axes of the slice: x: 4 (x_hi: 2, x_lo: 2; x = x_hi * 2 + x_lo), y: 4, z: 4, core: 2. Of those that a mesh axis runs over, the one named last changes fastest.
Arguments:
- hidden: bfloat16 [4096, 8192], P('tokens', 'tensor'), may hold values from -24 to 24
- w_query: bfloat16 [8192, 8192], P(None, 'tensor'), may hold values from -0.0625 to 0.0625
- w_key: bfloat16 [8192, 1024], P(None, 'tensor'), may hold values from -0.0625 to 0.0625
- w_value: bfloat16 [8192, 1024], P(None, 'tensor'), may hold values from -0.0625 to 0.0625
- key_codes: int32 [4096, 1024], P('tokens', 'tensor'), may hold values from 0 to 15
- codebook: float32 [1024, 16], P('tensor'), may hold values from -24 to 24
- positions: int32 [4096], P('tokens'), may hold values from 0 to 3071, as said below
- cotangent: bfloat16 [4096, 8192], P('tokens', 'tensor'), may hold values from -6 to 6
Outputs:
- attention_out: bfloat16 [4096, 8192], P('tokens', 'tensor')
- codebook_grad: float32 [1024, 16], P('tensor')
The draws below stay inside these ranges and needn't reach their ends.
Inputs may be any that keep to these rules, and one draw needn't show every extreme that they name: positions are 0 at the first token of each packed document and rise by one within it; exactly one document has 3072 tokens and every other is shorter.
All inputs are finite; a program needn't handle non-finite values.
Results may differ from the reference program's by a relative error of at most 0.0095.
The reference program's roundings to bfloat16 on the way count: a program that leaves them out, or rounds other values in their place, can miss the bound.
Values may be sent and summed in bfloat16 or wider, within the bound.
No kernel may reach another device: no remote copies, remote signals or barrier semaphores. Data moves between devices by JAX's collectives and lax.ppermute only.
A program may use at most 128 MiB of HBM per device.

```python
import math
import jax
import jax.numpy as jnp
from jax import lax

D = 8192
HD = 128
LEVELS = 16
QH = 64
KVH = 8
SEQ = 4096


def draw_hidden(key, part):
    base = jnp.clip(jax.random.normal(jax.random.fold_in(key, 11), (SEQ, D), jnp.float32), -4.0, 4.0)
    shared = jax.random.normal(jax.random.fold_in(key, 13), (1, D), jnp.float32)
    lower, upper = (math.log(0.5), math.log(2.0))
    shared = jnp.clip(shared, -3.0, 3.0)
    row_scale = jnp.exp(jax.random.uniform(jax.random.fold_in(key, 12), (SEQ, 1), jnp.float32, lower, upper))
    return (base * row_scale + shared).astype(jnp.bfloat16)


def draw_codebook(key, part):
    base = jnp.clip(jax.random.normal(jax.random.fold_in(key, 21), (KVH * HD, LEVELS), jnp.float32), -4.0, 4.0)
    lower, upper = (math.log(0.5), math.log(2.0))
    channel_scale = jnp.exp(jax.random.uniform(jax.random.fold_in(key, 22), (KVH * HD, 1), jnp.float32, lower, upper))
    return base * channel_scale


def draw_positions(key, part):
    longest = 3 * SEQ // 4
    first = jax.random.randint(jax.random.fold_in(key, 31), (), 0, SEQ - longest + 1)
    index = jnp.arange(SEQ).astype(jnp.int32)
    spacing = max(4, SEQ // 32)
    marks = jax.random.randint(jax.random.fold_in(key, 32), (SEQ,), 0, spacing) == 0
    inside = (index > first) & (index < first + longest)
    marks = marks & jnp.logical_not(inside) | (index == 0) | (index == first) | (index == first + longest)
    starts = lax.cummax(jnp.where(marks, index, 0), axis=0)
    return (index - starts).astype(jnp.int32)


def with_ends(values, own_key, smallest, largest):
    place = [jax.random.randint(jax.random.fold_in(own_key, axis), (), 0, length) for axis, length in enumerate(values.shape)]
    widest = values.shape.index(max(values.shape))
    neighbour = place[:widest] + [(place[widest] + 1) % values.shape[widest]] + place[widest + 1:]
    return values.at[tuple(place)].set(smallest).at[tuple(neighbour)].set(largest)


def block_levels(key, shape, cuts, smallest, high):
    factor_of, own = 1.0, jax.random.fold_in(key, 6)
    for axis_at, shards_of in cuts:
        heights = jnp.exp(jax.random.uniform(jax.random.fold_in(own, axis_at), (shards_of,), jnp.float32, smallest / len(cuts), high / len(cuts)))
        factor_of = factor_of * jnp.repeat(heights, shape[axis_at] // shards_of).reshape([-1 if axis == axis_at else 1 for axis in range(len(shape))])
    return factor_of


def centred(own_key, dims, deviation, reach, split=(), kind=jnp.bfloat16):
    array = jax.random.normal(own_key, dims, jnp.float32) * deviation
    if len(split) > 0:
        array = block_levels(own_key, dims, split, -0.22, 0.18) * array
    return jnp.clip(array, min=-reach, max=reach).astype(kind)


def setup_inputs(seed: int = 0) -> dict:
    key_of = jax.random.split(jax.random.key(seed), 9)
    return {
        "hidden": draw_hidden(jax.random.fold_in(key_of[8], 71), 0),
        "w_query": centred(key_of[1], (D, QH * HD), D ** -0.5, 0.0625, ((1, 8),)),
        "w_key": centred(key_of[2], (D, KVH * HD), D ** -0.5, 0.0625, ((1, 8),)),
        "w_value": centred(key_of[3], (D, KVH * HD), D ** -0.5, 0.0625, ((1, 8),)),
        "key_codes": with_ends(jax.random.randint(key_of[4], (SEQ, KVH * HD), 0, LEVELS), jax.random.fold_in(key_of[4], 1), 0, LEVELS - 1).astype(jnp.int32),
        "codebook": draw_codebook(jax.random.fold_in(key_of[8], 71), 0),
        "positions": draw_positions(jax.random.fold_in(key_of[8], 71), 0),
        "cotangent": centred(key_of[7], (SEQ, QH * HD), 1.0, 6.0, ((0, 16), (1, 8))),
    }


ROPE_BASE = 500000.0
NEG_BIG = -1e+30

def rope_tables(positions, width):
    index = jnp.arange(width // 2).astype(jnp.float32)
    inverse = jnp.exp(index * (-2.0 * math.log(ROPE_BASE) / width))
    angle = positions.astype(jnp.float32)[:, None] * inverse[None, :]
    return (jnp.cos(angle), jnp.sin(angle))

def rotate(values, cosine, sine):
    half = values.shape[-1] // 2
    first = values[..., :half]
    second = values[..., half:]
    return jnp.concatenate([first * cosine - second * sine, second * cosine + first * sine], axis=-1)

def unrotate(grads, cosine, sine):
    half = grads.shape[-1] // 2
    first = grads[..., :half]
    second = grads[..., half:]
    return jnp.concatenate([first * cosine + second * sine, second * cosine - first * sine], axis=-1)

def reference(hidden, w_query, w_key, w_value, key_codes, codebook, positions, cotangent):
    query_pre = jnp.dot(hidden, w_query, preferred_element_type=jnp.float32)
    key_true = jnp.dot(hidden, w_key, preferred_element_type=jnp.float32)
    value_all = jnp.dot(hidden, w_value, preferred_element_type=jnp.float32).astype(jnp.bfloat16)
    channels = jnp.arange(KVH * HD).astype(jnp.int32)
    key_deq = codebook[channels[None, :], key_codes]
    cosine, sine = rope_tables(positions, HD)
    query_rot = rotate(query_pre.reshape(SEQ, QH, HD).transpose(1, 0, 2), cosine, sine).astype(jnp.bfloat16)
    key_rot = rotate(key_deq.reshape(SEQ, KVH, HD).transpose(1, 0, 2), cosine, sine).astype(jnp.bfloat16)
    values = value_all.reshape(SEQ, KVH, HD).transpose(1, 0, 2)
    cot = cotangent.reshape(SEQ, QH, HD).transpose(1, 0, 2)
    index = jnp.arange(SEQ).astype(jnp.int32)
    spacing = index[:, None] - index[None, :]
    visible = (spacing >= 0) & (spacing <= positions[:, None])
    scale = 1.0 / math.sqrt(HD)
    group = QH // KVH

    def one_head(head):
        kv_head = head // group
        query = query_rot[head]
        keys = key_rot[kv_head]
        vals = values[kv_head]
        grad_out = cot[head]
        scores = jnp.dot(query, keys.T, preferred_element_type=jnp.float32) * scale
        masked = jnp.where(visible, scores, NEG_BIG)
        peak = lax.optimization_barrier(jnp.max(masked, axis=1))
        mass = lax.optimization_barrier(jnp.sum(jnp.where(visible, jnp.exp(masked - peak[:, None]), 0.0), axis=1))
        log_total = peak + jnp.log(mass)
        probs = jnp.where(visible, jnp.exp(masked - log_total[:, None]), 0.0)
        output = jnp.dot(probs.astype(jnp.bfloat16), vals, preferred_element_type=jnp.float32).astype(jnp.bfloat16)
        delta = lax.optimization_barrier(jnp.sum(grad_out.astype(jnp.float32) * output.astype(jnp.float32), axis=1))
        dprobs = jnp.dot(grad_out, vals.T, preferred_element_type=jnp.float32)
        dscores = (probs * (dprobs - delta[:, None])).astype(jnp.bfloat16)
        dkey = jnp.dot(dscores.T, query, preferred_element_type=jnp.float32) * scale
        return (output, dkey)
    outputs, dkeys = lax.map(one_head, jnp.arange(QH).astype(jnp.int32))
    attention_out = outputs.transpose(1, 0, 2).reshape(SEQ, QH * HD)
    key_grad_rot = lax.optimization_barrier(jnp.sum(dkeys.reshape(KVH, group, SEQ, HD), axis=1))
    key_grad_pre = unrotate(key_grad_rot, cosine, sine).transpose(1, 0, 2).reshape(SEQ, KVH * HD)
    entry_grad = key_grad_pre + LEVELS / SEQ * (key_deq - key_true)
    codebook_grad = jnp.zeros((KVH * HD, LEVELS), jnp.float32).at[jnp.broadcast_to(channels[None, :], key_codes.shape), key_codes].add(entry_grad)
    return (attention_out, codebook_grad)
```

```python
import functools
import math

import jax
import jax.numpy as jnp
from jax import lax
from jax.experimental import pallas as pl
from jax.experimental.pallas import tpu as pltpu
from jax.sharding import PartitionSpec as P

HD = 128
ROPE_BASE = 500000.0
NEG_BIG = -1e30
LOG2E = math.log2(math.e)
SCALE = 1.0 / math.sqrt(HD)
BLOCK = 512
NN = (((1,), (0,)), ((), ()))
TN = (((0,), (0,)), ((), ()))
TAIL = 16


def rope_tables(positions, width):
    index = jnp.arange(width // 2).astype(jnp.float32)
    inverse = jnp.exp(index * (-2.0 * math.log(ROPE_BASE) / width))
    angle = positions.astype(jnp.float32)[:, None] * inverse[None, :]
    cosine, sine = jnp.cos(angle), jnp.sin(angle)
    return (
        jnp.concatenate([cosine, cosine], axis=1),
        jnp.concatenate([-sine, sine], axis=1),
    )


def visible_block(base, block, own, earliest, rows):
    key = base + lax.broadcasted_iota(jnp.int32, (block, rows), 0)
    query = own + lax.broadcasted_iota(jnp.int32, (block, rows), 1)
    return (key <= query) & (key >= earliest)


def over_blocks(info, rows, body):
    own, first, edge = info[0], info[1], info[2]
    last = (own + rows + BLOCK - 1) // BLOCK

    @pl.loop(first, last)
    def _(b):
        masked = (b * BLOCK < edge) | (b * BLOCK + BLOCK > own)

        @pl.when(masked)
        def _():
            body(b, True)

        @pl.when(jnp.logical_not(masked))
        def _():
            body(b, False)


def stats_kernel(
    heads, rows, levels, weight,
    info, q_pre, cos_q, sin_q, keys, early, true, codes, book,
    q_rot, q_t, log_total, bins, peak_s, mass_s,
):
    own = info[0]
    for h in range(heads):
        x = q_pre[:, h * HD : (h + 1) * HD]
        turned = (x * cos_q[...] + pltpu.roll(x, HD // 2, 1) * sin_q[...]).astype(jnp.bfloat16)
        q_rot[h] = turned
        q_t[h] = turned.T
    code = codes[...]
    for level in range(levels):
        entry = weight * (book[level : level + 1, :] - true[...])
        bins[level : level + 1, :] = jnp.sum(
            jnp.where(code == level, entry, 0.0), axis=0, keepdims=True
        )
    peak_s[...] = jnp.full_like(peak_s, NEG_BIG)
    mass_s[...] = jnp.zeros_like(mass_s)

    def body(b, masked):
        base = pl.multiple_of(b * BLOCK, BLOCK)
        k = keys[pl.ds(base, BLOCK), :]
        if masked:
            seen = visible_block(base, BLOCK, own, early[...], rows)
        for h in range(heads):
            t = lax.dot_general(k, q_t[h], NN, preferred_element_type=jnp.float32)
            t = t * (SCALE * LOG2E)
            if masked:
                t = jnp.where(seen, t, NEG_BIG)
            old = peak_s[h : h + 1, :]
            new = jnp.maximum(old, jnp.max(t, axis=0, keepdims=True))
            fresh = jnp.sum(jnp.exp2(t - new), axis=0, keepdims=True)
            mass_s[h : h + 1, :] = mass_s[h : h + 1, :] * jnp.exp2(old - new) + fresh
            peak_s[h : h + 1, :] = new

    over_blocks(info, rows, body)
    log_total[...] = peak_s[...] + jnp.log(mass_s[...]) * LOG2E


def grad_kernel(
    heads, rows, levels, spare,
    info, q_rot, q_t, log_total, keys, early, cot, cot_t, cos_k, sin_k, codes, init,
    v_own, v_x, v_y1, v_y2, v_y3, v_core,
    out, bins, probs_s, out_s, delta_s, acc_s, values,
):
    own, first, me = info[0], info[1], info[3]

    def place(slot, ref, at):
        start = pl.multiple_of((me ^ slot) * rows, rows)
        values[pl.ds(start, rows), :] = ref[at * rows : (at + 1) * rows, :]

    place(0, v_own, 0)
    place(2, v_x, 0)
    for y, ref in ((1, v_y1), (2, v_y2), (3, v_y3)):
        place(4 * y, ref, 0)
        place(4 * y + 2, ref, 1)
    for j in range(8):
        place(2 * j + 1, v_core, j)
    out_s[...] = jnp.zeros_like(out_s)

    def forward(b, masked):
        base = pl.multiple_of(b * BLOCK, BLOCK)
        k = keys[pl.ds(base, BLOCK), :]
        v = values[pl.ds(base, BLOCK), :]
        if masked:
            seen = visible_block(base, BLOCK, own, early[...], rows)
        for h in range(heads):
            s = lax.dot_general(k, q_t[h], NN, preferred_element_type=jnp.float32)
            p = jnp.exp2(s * (SCALE * LOG2E) - log_total[h : h + 1, :])
            if masked:
                p = jnp.where(seen, p, 0.0)
            probs_s[b - first, h] = p
            out_s[h] += lax.dot_general(
                p.astype(jnp.bfloat16), v, TN, preferred_element_type=jnp.float32
            )

    over_blocks(info, rows, forward)
    for h in range(heads):
        o = out_s[h].astype(jnp.bfloat16)
        out[:, h * HD : (h + 1) * HD] = o
        prod = cot[:, h * HD : (h + 1) * HD].astype(jnp.float32) * o.astype(jnp.float32)
        delta_s[h : h + 1, :] = jnp.sum(prod.T, axis=0, keepdims=True)
    acc_s[...] = jnp.zeros_like(acc_s)
    last = (own + rows + BLOCK - 1) // BLOCK
    stride = rows + spare

    @pl.loop(first, last)
    def _(b):
        base = pl.multiple_of(b * BLOCK, BLOCK)
        v = values[pl.ds(base, BLOCK), :]
        dk = jnp.zeros((BLOCK, HD), jnp.float32)
        for h in range(heads):
            dp = lax.dot_general(v, cot_t[h], NN, preferred_element_type=jnp.float32)
            ds = (probs_s[b - first, h] * (dp - delta_s[h : h + 1, :])).astype(jnp.bfloat16)
            dk = dk + lax.dot_general(ds, q_rot[h], NN, preferred_element_type=jnp.float32)
        dk = dk * SCALE
        g = dk * cos_k[pl.ds(base, BLOCK), :] - pltpu.roll(dk, HD // 2, 1) * sin_k[pl.ds(base, BLOCK), :]
        for part in range(BLOCK // rows):
            at = pl.multiple_of((b * (BLOCK // rows) + part) * stride, TAIL)
            code = codes[pl.ds(at, rows), :].astype(jnp.float32)
            piece = g[part * rows : (part + 1) * rows, :]
            for level in range(levels):
                chosen = jnp.where(code == level, piece, 0.0)
                acc_s[level] += jnp.sum(chosen.reshape(rows // 8, 8, HD), axis=0)

    bins[...] = init[...] + jnp.sum(acc_s[...], axis=1)


def vmem():
    return pl.BlockSpec(memory_space=pltpu.VMEM)


def smem():
    return pl.BlockSpec(memory_space=pltpu.SMEM)


def cost(flops, size):
    return pl.CostEstimate(flops=flops, bytes_accessed=size, transcendentals=0)


def shards(hidden, w_query, w_key, w_value, key_codes, codebook, positions, cotangent):
    rows, part = hidden.shape
    width = w_query.shape[1]
    heads = width // HD
    levels = codebook.shape[1]
    ranks = lax.axis_size("tokens")
    total = rows * ranks
    group = lax.axis_size("tensor")
    rank = lax.axis_index("tensor")
    me = lax.axis_index("tokens")
    own = me * rows
    bf16, f32 = jnp.bfloat16, jnp.float32

    digits = jnp.stack([positions // 64, positions % 64]).reshape(2 * rows // HD, HD)
    digits = jnp.pad(digits, ((0, TAIL - digits.shape[0]), (0, 0)))
    packed = jnp.concatenate([key_codes, digits], axis=0).astype(bf16)
    packed = lax.all_gather(packed, "tokens", axis=0, tiled=True)
    by_rank = packed.reshape(ranks, rows + TAIL, HD)
    digits = by_rank[:, rows : rows + 2 * rows // HD].reshape(ranks, 2, rows).astype(f32)
    every = (digits[:, 0] * 64.0 + digits[:, 1]).reshape(total)
    cos_k, sin_k = rope_tables(every, HD)
    cos_q, sin_q = rope_tables(positions, HD)
    book = codebook.T
    codes = by_rank[:, :rows].reshape(total, HD).astype(f32)
    deq = jnp.zeros((total, HD), f32)
    for level in range(levels):
        deq = jnp.where(codes == level, book[level][None, :], deq)
    half = HD // 2
    keys = (deq * cos_k + jnp.concatenate([deq[:, half:], deq[:, :half]], axis=1) * sin_k).astype(bf16)
    cot_t = cotangent.reshape(rows, heads, HD).transpose(1, 2, 0)

    flip = [(i, i ^ 1) for i in range(group)]
    up = [(i, (i + 2) % group) for i in range(group)]
    down = [(i, (i - 2) % group) for i in range(group)]
    send = functools.partial(lax.ppermute, axis_name="tensor")

    def weights_of(shard):
        start = shard * part
        return tuple(lax.dynamic_slice_in_dim(w, start, part, 0) for w in (w_query, w_key, w_value))

    def project(piece, shard, sums):
        out = []
        for w, s in zip(weights_of(shard), sums):
            term = jnp.dot(piece, w, preferred_element_type=f32)
            out.append(term if s is None else s + term)
        return tuple(out)

    other = send(hidden, perm=flip)
    sums = project(hidden, rank, (None, None, None))
    n = rows // 2
    lanes = []
    for base, here in ((hidden, rank), (other, rank ^ 1)):
        low = send(base, perm=up)
        high = send(base, perm=down)
        far = jnp.concatenate([send(low[:n], perm=up), send(high[n:], perm=down)], axis=0)
        lanes.append((base, here, low, high, far))
    base, here, low, high, far = lanes[0]
    sums = project(low, (here - 2) % group, sums)
    sums = project(high, (here + 2) % group, sums)
    sums = project(lanes[1][0], rank ^ 1, sums)
    sums = project(far, (here + 4) % group, sums)
    base, here, low, high, far = lanes[1]
    sums = project(low, (here - 2) % group, sums)
    sums = project(high, (here + 2) % group, sums)
    query_pre, key_true, value_sum = project(far, (here + 4) % group, sums)
    value = value_sum.astype(bf16)

    cross = lambda x, d: lax.ppermute(x, "tokens", [(i, i ^ d) for i in range(ranks)])
    v_x = cross(value, 2)
    pair = jnp.concatenate([value, v_x], axis=0)
    v_y = [cross(pair, 4 * y) for y in (1, 2, 3)]
    v_core = cross(jnp.concatenate([pair] + v_y, axis=0), 1)

    index = own + jnp.arange(rows)
    early = (index - positions).astype(jnp.int32)
    info = jnp.stack([own, jnp.min(early) // BLOCK, jnp.max(early), me]).astype(jnp.int32)
    early = early[None, :]

    q_rot, q_t, log_total, init = pl.pallas_call(
        functools.partial(stats_kernel, heads, rows, levels, levels / total),
        out_shape=(
            jax.ShapeDtypeStruct((heads, rows, HD), bf16),
            jax.ShapeDtypeStruct((heads, HD, rows), bf16),
            jax.ShapeDtypeStruct((heads, rows), f32),
            jax.ShapeDtypeStruct((levels, HD), f32),
        ),
        in_specs=[smem()] + [vmem()] * 8,
        out_specs=(vmem(),) * 4,
        scratch_shapes=[pltpu.VMEM((heads, rows), f32)] * 2,
        compiler_params=pltpu.CompilerParams(vmem_limit_bytes=40 << 20),
        cost_estimate=cost(2 * rows * width * total, 4 << 20),
        name="stats",
    )(info, query_pre, cos_q, sin_q, keys, early, key_true, key_codes, book)

    most = total // BLOCK
    attention_out, local = pl.pallas_call(
        functools.partial(grad_kernel, heads, rows, levels, TAIL),
        out_shape=(
            jax.ShapeDtypeStruct((rows, width), bf16),
            jax.ShapeDtypeStruct((levels, HD), f32),
        ),
        in_specs=[smem()] + [vmem()] * 17,
        out_specs=(vmem(),) * 2,
        scratch_shapes=[
            pltpu.VMEM((min(most, 7), heads, BLOCK, rows), f32),
            pltpu.VMEM((heads, rows, HD), f32),
            pltpu.VMEM((heads, rows), f32),
            pltpu.VMEM((levels, 8, HD), f32),
            pltpu.VMEM((total, HD), bf16),
        ],
        compiler_params=pltpu.CompilerParams(vmem_limit_bytes=58 << 20),
        cost_estimate=cost(8 * rows * width * total, 8 << 20),
        name="grad",
    )(
        info, q_rot, q_t, log_total, keys, early, cotangent, cot_t, cos_k, sin_k, packed, init,
        value, v_x, *v_y, v_core,
    )
    for d in (1, 2, 4, 8):
        local = local + cross(local, d)
    return (attention_out, local.T)


def solution(mesh):
    placed = (
        P("tokens", "tensor"),
        P(None, "tensor"),
        P(None, "tensor"),
        P(None, "tensor"),
        P("tokens", "tensor"),
        P("tensor", None),
        P("tokens"),
        P("tokens", "tensor"),
    )
    return jax.shard_map(
        shards,
        mesh=mesh,
        in_specs=placed,
        out_specs=(P("tokens", "tensor"), P("tensor", None)),
        check_vma=False,
    )
```

```python
import functools
import math

import jax
import jax.numpy as jnp
from jax import lax
from jax.experimental import pallas as pl
from jax.experimental.pallas import tpu as pltpu
from jax.sharding import PartitionSpec as P

HD = 128
ROPE_BASE = 500000.0
NEG_BIG = -1e30
LOG2E = math.log2(math.e)
SCALE = 1.0 / math.sqrt(HD)
BLOCK = 512
NN = (((1,), (0,)), ((), ()))
TN = (((0,), (0,)), ((), ()))
TAIL = 16


def sincos(angle):
    turns = jnp.floor(angle * (2.0 / math.pi) + 0.5)
    r = angle - turns * 1.5703125
    r = r - turns * 4.837512969970703125e-4
    r = r - turns * 7.54978995489188216e-8
    z = r * r
    s = ((-1.9515295891e-4 * z + 8.3321608736e-3) * z - 1.6666654611e-1) * z * r + r
    c = ((2.443315711809948e-5 * z - 1.388731625493765e-3) * z + 4.166664568298827e-2) * z * z
    c = c - 0.5 * z + 1.0
    quadrant = turns.astype(jnp.int32)
    odd = (quadrant & 1) == 1
    sine = jnp.where(odd, c, s)
    cosine = jnp.where(odd, s, c)
    sine = jnp.where((quadrant & 2) == 0, sine, -sine)
    cosine = jnp.where(((quadrant + 1) & 2) == 0, cosine, -cosine)
    return sine, cosine


def slots(pieces):
    own, x, y1, y2, y3, core = pieces
    found = [(0, own, 0), (2, x, 0)]
    for y, ref in ((1, y1), (2, y2), (3, y3)):
        found += [(4 * y, ref, 0), (4 * y + 2, ref, 1)]
    return found + [(2 * j + 1, core, j) for j in range(8)]


def prep_kernel(
    rows, ranks, levels, heads,
    info, inverse, book, cot, p_own, p_x, p_y1, p_y2, p_y3, p_core,
    keys, cos_k, sin_k, codes, cot_t, packed_s,
):
    me = info[3]
    tall = rows + TAIL
    for bits, ref, at in slots((p_own, p_x, p_y1, p_y2, p_y3, p_core)):
        start = pl.multiple_of((me ^ bits) * tall, TAIL)
        packed_s[pl.ds(start, tall), :] = ref[at * tall : (at + 1) * tall, :]
    for h in range(heads):
        cot_t[h] = cot[:, h * HD : (h + 1) * HD].T
    eye = lax.broadcasted_iota(jnp.int32, (HD, HD), 0) == lax.broadcasted_iota(
        jnp.int32, (HD, HD), 1
    )
    lane = lax.broadcasted_iota(jnp.int32, (HD, HD), 1)
    ones = jnp.ones((2 * HD, HD), jnp.bfloat16)

    @pl.loop(0, ranks)
    def _(i):
        source = pl.multiple_of(i * tall, TAIL)
        tail = packed_s[pl.ds(source + rows, TAIL), :].astype(jnp.float32)
        for part in range(rows // HD):
            target = pl.multiple_of(i * rows + part * HD, HD)
            high = jnp.where(eye, tail[part : part + 1, :], 0.0)
            low = jnp.where(eye, tail[rows // HD + part : rows // HD + part + 1, :], 0.0)
            digits = jnp.concatenate([high, low], axis=1).astype(jnp.bfloat16)
            place = lax.dot_general(digits, ones, NN, preferred_element_type=jnp.float32)
            sine, cosine = sincos(place * inverse[...])
            sine = jnp.where(lane < HD // 2, -sine, sine)
            cos_k[pl.ds(target, HD), :] = cosine
            sin_k[pl.ds(target, HD), :] = sine
            raw = packed_s[pl.ds(source + part * HD, HD), :]
            codes[pl.ds(target, HD), :] = raw
            code = raw.astype(jnp.float32).astype(jnp.int32)
            layer = [book[e : e + 1, :] for e in range(levels)]
            bit = 1
            while len(layer) > 1:
                on = (code & bit) != 0
                layer = [jnp.where(on, layer[j + 1], layer[j]) for j in range(0, len(layer), 2)]
                bit *= 2
            deq = layer[0]
            turned = deq * cosine + pltpu.roll(deq, HD // 2, 1) * sine
            keys[pl.ds(target, HD), :] = turned.astype(jnp.bfloat16)


def project_kernel(count, names, started, place, *refs):
    pieces, refs = refs[:count], refs[count:]
    weights, refs = refs[: len(names)], refs[len(names) :]
    before, after = (refs[: len(names)], refs[len(names) :]) if started else ((), refs)
    step = pl.program_id(0)
    chunk = weights[0].shape[0]
    per = pieces[0].shape[1] // chunk

    @pl.when(step == 0)
    def _():
        for j, ref in enumerate(after):
            ref[...] = before[j][...] if started else jnp.zeros_like(ref)

    for n in range(count):
        @pl.when(step // per == n)
        def _():
            at = pl.multiple_of((step % per) * chunk, chunk)
            x = pieces[n][:, pl.ds(at, chunk)]
            for w, ref in zip(weights, after):
                ref[...] += jnp.dot(x, w[...], preferred_element_type=jnp.float32)


def visible_block(base, block, own, earliest, rows):
    key = base + lax.broadcasted_iota(jnp.int32, (block, rows), 0)
    query = own + lax.broadcasted_iota(jnp.int32, (block, rows), 1)
    return (key <= query) & (key >= earliest)


def over_blocks(info, rows, body):
    own, first, edge = info[0], info[1], info[2]
    last = (own + rows + BLOCK - 1) // BLOCK

    @pl.loop(first, last)
    def _(b):
        masked = (b * BLOCK < edge) | (b * BLOCK + BLOCK > own)

        @pl.when(masked)
        def _():
            body(b, True)

        @pl.when(jnp.logical_not(masked))
        def _():
            body(b, False)


def stats_kernel(
    heads, rows, levels, weight,
    info, q_pre, cos_k, sin_k, keys, early, true, codes, book,
    q_rot, q_t, log_total, bins, peak_s, mass_s,
):
    own = info[0]
    mine = pl.ds(pl.multiple_of(own, rows), rows)
    cos_q, sin_q = cos_k[mine, :], sin_k[mine, :]
    for h in range(heads):
        x = q_pre[:, h * HD : (h + 1) * HD]
        turned = (x * cos_q + pltpu.roll(x, HD // 2, 1) * sin_q).astype(jnp.bfloat16)
        q_rot[h] = turned
        q_t[h] = turned.T
    code = codes[...]
    for level in range(levels):
        entry = weight * (book[level : level + 1, :] - true[...])
        bins[level : level + 1, :] = jnp.sum(
            jnp.where(code == level, entry, 0.0), axis=0, keepdims=True
        )
    peak_s[...] = jnp.full_like(peak_s, NEG_BIG)
    mass_s[...] = jnp.zeros_like(mass_s)

    def body(b, masked):
        base = pl.multiple_of(b * BLOCK, BLOCK)
        k = keys[pl.ds(base, BLOCK), :]
        if masked:
            seen = visible_block(base, BLOCK, own, early[...], rows)
        for h in range(heads):
            t = lax.dot_general(k, q_t[h], NN, preferred_element_type=jnp.float32)
            t = t * (SCALE * LOG2E)
            if masked:
                t = jnp.where(seen, t, NEG_BIG)
            old = peak_s[h : h + 1, :]
            new = jnp.maximum(old, jnp.max(t, axis=0, keepdims=True))
            fresh = jnp.sum(jnp.exp2(t - new), axis=0, keepdims=True)
            mass_s[h : h + 1, :] = mass_s[h : h + 1, :] * jnp.exp2(old - new) + fresh
            peak_s[h : h + 1, :] = new

    over_blocks(info, rows, body)
    log_total[...] = peak_s[...] + jnp.log(mass_s[...]) * LOG2E


def grad_kernel(
    heads, rows, levels,
    info, q_rot, q_t, log_total, keys, early, cot, cot_t, cos_k, sin_k, codes, init,
    v_own, v_x, v_y1, v_y2, v_y3, v_core,
    out, bins, probs_s, out_s, delta_s, acc_s, values,
):
    own, first, me = info[0], info[1], info[3]

    for bits, ref, at in slots((v_own, v_x, v_y1, v_y2, v_y3, v_core)):
        start = pl.multiple_of((me ^ bits) * rows, rows)
        values[pl.ds(start, rows), :] = ref[at * rows : (at + 1) * rows, :]
    out_s[...] = jnp.zeros_like(out_s)

    def forward(b, masked):
        base = pl.multiple_of(b * BLOCK, BLOCK)
        k = keys[pl.ds(base, BLOCK), :]
        v = values[pl.ds(base, BLOCK), :]
        if masked:
            seen = visible_block(base, BLOCK, own, early[...], rows)
        for h in range(heads):
            s = lax.dot_general(k, q_t[h], NN, preferred_element_type=jnp.float32)
            p = jnp.exp2(s * (SCALE * LOG2E) - log_total[h : h + 1, :])
            if masked:
                p = jnp.where(seen, p, 0.0)
            probs_s[b - first, h] = p
            out_s[h] += lax.dot_general(
                p.astype(jnp.bfloat16), v, TN, preferred_element_type=jnp.float32
            )

    over_blocks(info, rows, forward)
    for h in range(heads):
        o = out_s[h].astype(jnp.bfloat16)
        out[:, h * HD : (h + 1) * HD] = o
        prod = cot[:, h * HD : (h + 1) * HD].astype(jnp.float32) * o.astype(jnp.float32)
        delta_s[h : h + 1, :] = jnp.sum(prod.T, axis=0, keepdims=True)
    acc_s[...] = jnp.zeros_like(acc_s)
    last = (own + rows + BLOCK - 1) // BLOCK

    @pl.loop(first, last)
    def _(b):
        base = pl.multiple_of(b * BLOCK, BLOCK)
        v = values[pl.ds(base, BLOCK), :]
        dk = jnp.zeros((BLOCK, HD), jnp.float32)
        for h in range(heads):
            dp = lax.dot_general(v, cot_t[h], NN, preferred_element_type=jnp.float32)
            ds = (probs_s[b - first, h] * (dp - delta_s[h : h + 1, :])).astype(jnp.bfloat16)
            dk = dk + lax.dot_general(ds, q_rot[h], NN, preferred_element_type=jnp.float32)
        dk = dk * SCALE
        g = dk * cos_k[pl.ds(base, BLOCK), :] - pltpu.roll(dk, HD // 2, 1) * sin_k[pl.ds(base, BLOCK), :]
        code = codes[pl.ds(base, BLOCK), :].astype(jnp.float32)
        for level in range(levels):
            chosen = jnp.where(code == level, g, 0.0)
            acc_s[level] += jnp.sum(chosen.reshape(BLOCK // 8, 8, HD), axis=0)

    bins[...] = init[...] + jnp.sum(acc_s[...], axis=1)


def vmem():
    return pl.BlockSpec(memory_space=pltpu.VMEM)


def smem():
    return pl.BlockSpec(memory_space=pltpu.SMEM)


def cost(flops, size):
    return pl.CostEstimate(flops=flops, bytes_accessed=size, transcendentals=0)


def shards(hidden, w_query, w_key, w_value, key_codes, codebook, positions, cotangent):
    rows, part = hidden.shape
    width = w_query.shape[1]
    heads = width // HD
    levels = codebook.shape[1]
    ranks = lax.axis_size("tokens")
    total = rows * ranks
    group = lax.axis_size("tensor")
    rank = lax.axis_index("tensor")
    me = lax.axis_index("tokens")
    own = me * rows
    bf16, f32 = jnp.bfloat16, jnp.float32

    cross = lambda x, d: lax.ppermute(x, "tokens", [(i, i ^ d) for i in range(ranks)])

    def everyone(x):
        x_side = cross(x, 2)
        pair = jnp.concatenate([x, x_side], axis=0)
        y_side = [cross(pair, 4 * y) for y in (1, 2, 3)]
        core = cross(jnp.concatenate([pair] + y_side, axis=0), 1)
        return (x, x_side, *y_side, core)

    flip = [(i, i ^ 1) for i in range(group)]
    up = [(i, (i + 2) % group) for i in range(group)]
    down = [(i, (i - 2) % group) for i in range(group)]
    send = functools.partial(lax.ppermute, axis_name="tensor")
    n = rows // 2
    other = send(hidden, perm=flip)
    low = send(hidden, perm=up)
    high = send(hidden, perm=down)
    far = jnp.concatenate([send(low[:n], perm=up), send(high[n:], perm=down)], axis=0)
    other_low = send(other, perm=up)
    other_high = send(other, perm=down)
    other_far = send(far, perm=flip)

    digits = jnp.stack([positions // 64 * 64, positions % 64]).reshape(2 * rows // HD, HD)
    digits = jnp.pad(digits, ((0, TAIL - digits.shape[0]), (0, 0)))
    packed = everyone(jnp.concatenate([key_codes, digits], axis=0).astype(bf16))
    index = own + jnp.arange(rows)
    early = (index - positions).astype(jnp.int32)
    info = jnp.stack([own, jnp.min(early) // BLOCK, jnp.max(early), me]).astype(jnp.int32)
    early = early[None, :]
    book = codebook.T
    inverse = jnp.exp((jnp.arange(HD) % (HD // 2)).astype(f32) * (-2.0 * math.log(ROPE_BASE) / HD))

    keys, cos_k, sin_k, codes, cot_t = pl.pallas_call(
        functools.partial(prep_kernel, rows, ranks, levels, heads),
        out_shape=(
            jax.ShapeDtypeStruct((total, HD), bf16),
            jax.ShapeDtypeStruct((total, HD), f32),
            jax.ShapeDtypeStruct((total, HD), f32),
            jax.ShapeDtypeStruct((total, HD), bf16),
            jax.ShapeDtypeStruct((heads, HD, rows), bf16),
        ),
        in_specs=[smem()] + [vmem()] * 9,
        out_specs=(vmem(),) * 5,
        scratch_shapes=[pltpu.VMEM((ranks * (rows + TAIL), HD), bf16)],
        compiler_params=pltpu.CompilerParams(vmem_limit_bytes=16 << 20),
        cost_estimate=cost(1 << 32, 16 << 20),
        name="prep",
    )(info, inverse[None, :], book, cotangent, *packed)

    def project(pieces, weights, sums, chunk):
        count, names = len(pieces), range(len(weights))
        per = part // chunk
        place = jnp.stack([shard for _, shard in pieces]).astype(jnp.int32)
        whole = lambda shape: pl.BlockSpec(shape, lambda i, place: (0, 0))
        sizes = [(rows, w.shape[1]) for w in weights]
        return pl.pallas_call(
            functools.partial(project_kernel, count, names, sums is not None),
            out_shape=[jax.ShapeDtypeStruct(size, f32) for size in sizes],
            grid_spec=pltpu.PrefetchScalarGridSpec(
                num_scalar_prefetch=1,
                grid=(count * per,),
                in_specs=[whole((rows, part))] * count
                + [
                    pl.BlockSpec((chunk, w.shape[1]), lambda i, place: (place[i // per] * per + i % per, 0))
                    for w in weights
                ]
                + ([whole(size) for size in sizes] if sums is not None else []),
                out_specs=[whole(size) for size in sizes],
            ),
            compiler_params=pltpu.CompilerParams(vmem_limit_bytes=20 << 20),
            cost_estimate=cost(
                2 * rows * part * count * sum(w.shape[1] for w in weights),
                part * count * sum(w.shape[1] for w in weights) * 2,
            ),
            name="project",
        )(place, *[piece for piece, _ in pieces], *weights, *(sums if sums is not None else ()))

    everything = (w_query, w_key, w_value)
    mate = rank ^ 1
    sums = project([(hidden, rank)], everything, None, part // 2)
    sums = project([(low, (rank - 2) % group), (high, (rank + 2) % group), (other, mate)], everything, sums, part // 2)
    rest = [
        (far, (rank + 4) % group),
        (other_low, (mate - 2) % group),
        (other_high, (mate + 2) % group),
        (other_far, (mate + 4) % group),
    ]
    (value_sum,) = project(rest, (w_value,), sums[2:], part)
    query_pre, key_true = project(rest, (w_query, w_key), sums[:2], part // 2)
    values = everyone(value_sum.astype(bf16))

    def log_totals(first, count):
        return pl.pallas_call(
            functools.partial(stats_kernel, count, rows, levels, levels / total),
            out_shape=(
                jax.ShapeDtypeStruct((count, rows, HD), bf16),
                jax.ShapeDtypeStruct((count, HD, rows), bf16),
                jax.ShapeDtypeStruct((count, rows), f32),
                jax.ShapeDtypeStruct((levels, HD), f32),
            ),
            in_specs=[smem()] + [vmem()] * 8,
            out_specs=(vmem(),) * 4,
            scratch_shapes=[pltpu.VMEM((count, rows), f32)] * 2,
            compiler_params=pltpu.CompilerParams(vmem_limit_bytes=16 << 20),
            cost_estimate=cost(2 * rows * width * total, 4 << 20),
            name="stats",
        )(info, query_pre, cos_k, sin_k, keys, early, key_true, key_codes, book)

    q_rot, q_t, log_total, init = log_totals(0, heads)

    most = total // BLOCK
    attention_out, local = pl.pallas_call(
        functools.partial(grad_kernel, heads, rows, levels),
        out_shape=(
            jax.ShapeDtypeStruct((rows, width), bf16),
            jax.ShapeDtypeStruct((levels, HD), f32),
        ),
        in_specs=[smem()] + [vmem()] * 17,
        out_specs=(vmem(),) * 2,
        scratch_shapes=[
            pltpu.VMEM((min(most, 7), heads, BLOCK, rows), f32),
            pltpu.VMEM((heads, rows, HD), f32),
            pltpu.VMEM((heads, rows), f32),
            pltpu.VMEM((levels, 8, HD), f32),
            pltpu.VMEM((total, HD), bf16),
        ],
        compiler_params=pltpu.CompilerParams(vmem_limit_bytes=42 << 20),
        cost_estimate=cost(8 * rows * width * total, 8 << 20),
        name="grad",
    )(info, q_rot, q_t, log_total, keys, early, cotangent, cot_t, cos_k, sin_k, codes, init, *values)
    for d in (1, 2, 4, 8):
        local = local + cross(local, d)
    return (attention_out, local.T)


def solution(mesh):
    placed = (
        P("tokens", "tensor"),
        P(None, "tensor"),
        P(None, "tensor"),
        P(None, "tensor"),
        P("tokens", "tensor"),
        P("tensor", None),
        P("tokens"),
        P("tokens", "tensor"),
    )
    return jax.shard_map(
        shards,
        mesh=mesh,
        in_specs=placed,
        out_specs=(P("tokens", "tensor"), P("tensor", None)),
        check_vma=False,
    )
```

```python
import functools
import math

import jax
import jax.numpy as jnp
from jax import lax
from jax.experimental import pallas as pl
from jax.experimental.pallas import tpu as pltpu
from jax.sharding import PartitionSpec as P

HD = 128
ROPE_BASE = 500000.0
NEG_BIG = -1e30
LOG2E = math.log2(math.e)
SCALE = 1.0 / math.sqrt(HD)
BLOCK = 512
NN = (((1,), (0,)), ((), ()))
TN = (((0,), (0,)), ((), ()))
TAIL = 16


def sincos(angle):
    turns = jnp.floor(angle * (2.0 / math.pi) + 0.5)
    r = angle - turns * 1.5703125
    r = r - turns * 4.837512969970703125e-4
    r = r - turns * 7.54978995489188216e-8
    z = r * r
    s = ((-1.9515295891e-4 * z + 8.3321608736e-3) * z - 1.6666654611e-1) * z * r + r
    c = ((2.443315711809948e-5 * z - 1.388731625493765e-3) * z + 4.166664568298827e-2) * z * z
    c = c - 0.5 * z + 1.0
    quadrant = turns.astype(jnp.int32)
    odd = (quadrant & 1) == 1
    sine = jnp.where(odd, c, s)
    cosine = jnp.where(odd, s, c)
    sine = jnp.where((quadrant & 2) == 0, sine, -sine)
    cosine = jnp.where(((quadrant + 1) & 2) == 0, cosine, -cosine)
    return sine, cosine


def slots(pieces):
    own, x, y1, y2, y3, core = pieces
    found = [(0, own, 0), (2, x, 0)]
    for y, ref in ((1, y1), (2, y2), (3, y3)):
        found += [(4 * y, ref, 0), (4 * y + 2, ref, 1)]
    return found + [(2 * j + 1, core, j) for j in range(8)]


def token_rank():
    return lax.axis_index("tokens")


def pack_kernel(rows, key_codes, positions, packed, early, info):
    packed[:rows, :] = key_codes[...].astype(jnp.float32).astype(jnp.bfloat16)
    place = positions[...]
    high, low = place & ~63, place & 63
    wide = [x[:, j * HD : (j + 1) * HD] for x in (high, low) for j in range(rows // HD)]
    blank = jnp.zeros((TAIL - len(wide), HD), jnp.int32)
    tail = jnp.concatenate(wide + [blank], axis=0)
    packed[rows:, :] = tail.astype(jnp.float32).astype(jnp.bfloat16)
    index = token_rank() * rows + lax.broadcasted_iota(jnp.int32, (1, rows), 1)
    first = index - place
    early[...] = first
    first = first.astype(jnp.float32)
    info[0] = jnp.min(first).astype(jnp.int32) // BLOCK
    info[1] = jnp.max(first).astype(jnp.int32)


def prep_kernel(
    rows, ranks, levels, heads,
    inverse, book, cot, p_own, p_x, p_y1, p_y2, p_y3, p_core,
    keys, cos_k, sin_k, codes, cot_t, packed_s, sems,
):
    me = token_rank()
    tall = rows + TAIL
    copies = []
    for j, (bits, ref, at) in enumerate(slots((p_own, p_x, p_y1, p_y2, p_y3, p_core))):
        start = pl.multiple_of((me ^ bits) * tall, TAIL)
        copies.append(
            pltpu.make_async_copy(
                ref.at[at * tall : (at + 1) * tall, :], packed_s.at[pl.ds(start, tall), :], sems.at[j]
            )
        )
    for copy in copies:
        copy.start()
    for h in range(heads):
        cot_t[h] = cot[:, h * HD : (h + 1) * HD].T
    for copy in copies:
        copy.wait()
    eye = lax.broadcasted_iota(jnp.int32, (HD, HD), 0) == lax.broadcasted_iota(
        jnp.int32, (HD, HD), 1
    )
    lane = lax.broadcasted_iota(jnp.int32, (HD, HD), 1)
    ones = jnp.ones((2 * HD, HD), jnp.bfloat16)

    @pl.loop(0, ranks)
    def _(i):
        source = pl.multiple_of(i * tall, TAIL)
        tail = packed_s[pl.ds(source + rows, TAIL), :].astype(jnp.float32)
        for part in range(rows // HD):
            target = pl.multiple_of(i * rows + part * HD, HD)
            high = jnp.where(eye, tail[part : part + 1, :], 0.0)
            low = jnp.where(eye, tail[rows // HD + part : rows // HD + part + 1, :], 0.0)
            digits = jnp.concatenate([high, low], axis=1).astype(jnp.bfloat16)
            place = lax.dot_general(digits, ones, NN, preferred_element_type=jnp.float32)
            sine, cosine = sincos(place * inverse[...])
            sine = jnp.where(lane < HD // 2, -sine, sine)
            cos_k[pl.ds(target, HD), :] = cosine
            sin_k[pl.ds(target, HD), :] = sine
            raw = packed_s[pl.ds(source + part * HD, HD), :]
            codes[pl.ds(target, HD), :] = raw
            code = raw.astype(jnp.float32).astype(jnp.int32)
            layer = [book[e : e + 1, :] for e in range(levels)]
            bit = 1
            while len(layer) > 1:
                on = (code & bit) != 0
                layer = [jnp.where(on, layer[j + 1], layer[j]) for j in range(0, len(layer), 2)]
                bit *= 2
            deq = layer[0]
            turned = deq * cosine + pltpu.roll(deq, HD // 2, 1) * sine
            keys[pl.ds(target, HD), :] = turned.astype(jnp.bfloat16)


def project_kernel(pieces_at, chunk, count, started, place, *refs):
    pieces, refs = refs[: len(pieces_at)], refs[len(pieces_at) :]
    weights, refs = refs[:count], refs[count:]
    before, after = (refs[:count], refs[count:]) if started else ((), refs)
    step = pl.program_id(0)

    @pl.when(step == 0)
    def _():
        for j, ref in enumerate(after):
            ref[...] = before[j][...] if started else jnp.zeros_like(ref)

    for piece, (start, stop) in zip(pieces, pieces_at):
        @pl.when((step >= start) & (step < stop))
        def _():
            at = pl.multiple_of((step - start) * chunk, chunk)
            x = piece[:, pl.ds(at, chunk)]
            for w, ref in zip(weights, after):
                ref[...] += jnp.dot(x, w[...], preferred_element_type=jnp.float32)


def value_kernel(first, chunk, place, w, before, *refs):
    pieces, value = refs[:-1], refs[-1]
    total = before[...]
    step = first
    for piece in pieces:
        for at in range(0, piece.shape[1], chunk):
            start = pl.multiple_of(place[step] * chunk, chunk)
            total += jnp.dot(
                piece[:, at : at + chunk], w[pl.ds(start, chunk), :], preferred_element_type=jnp.float32
            )
            step += 1
    value[...] = total.astype(jnp.bfloat16)


def visible_block(base, block, own, earliest, rows):
    key = base + lax.broadcasted_iota(jnp.int32, (block, rows), 0)
    query = own + lax.broadcasted_iota(jnp.int32, (block, rows), 1)
    return (key <= query) & (key >= earliest)


def over_blocks(own, info, rows, body):
    first, edge = info[0], info[1]
    last = (own + rows + BLOCK - 1) // BLOCK

    @pl.loop(first, last)
    def _(b):
        masked = (b * BLOCK < edge) | (b * BLOCK + BLOCK > own)

        @pl.when(masked)
        def _():
            body(b, True)

        @pl.when(jnp.logical_not(masked))
        def _():
            body(b, False)


def stats_kernel(
    begin, heads, rows, levels, weight,
    info, q_pre, early, true, codes, book, cos_k, sin_k, keys_k,
    q_rot, q_t, log_total, bins, peak_s, mass_s, cos_q, sin_q, keys, sems,
):
    own = token_rank() * rows
    mine = pl.ds(pl.multiple_of(own, rows), rows)
    copies = [
        pltpu.make_async_copy(cos_k.at[mine, :], cos_q, sems.at[0]),
        pltpu.make_async_copy(sin_k.at[mine, :], sin_q, sems.at[1]),
        pltpu.make_async_copy(keys_k, keys, sems.at[2]),
    ]
    for copy in copies:
        copy.start()
    if begin == 0:
        code = codes[...]
        for level in range(levels):
            entry = weight * (book[level : level + 1, :] - true[...])
            bins[level : level + 1, :] = jnp.sum(
                jnp.where(code == level, entry, 0.0), axis=0, keepdims=True
            )
    else:
        bins[...] = jnp.zeros_like(bins)
    peak_s[...] = jnp.full_like(peak_s, NEG_BIG)
    mass_s[...] = jnp.zeros_like(mass_s)
    copies[0].wait()
    copies[1].wait()
    for h in range(heads):
        x = q_pre[:, (begin + h) * HD : (begin + h + 1) * HD]
        turned = (x * cos_q[...] + pltpu.roll(x, HD // 2, 1) * sin_q[...]).astype(jnp.bfloat16)
        q_rot[h] = turned
        q_t[h] = turned.T
    copies[2].wait()

    def body(b, masked):
        base = pl.multiple_of(b * BLOCK, BLOCK)
        k = keys[pl.ds(base, BLOCK), :]
        if masked:
            seen = visible_block(base, BLOCK, own, early[...], rows)
        for h in range(heads):
            t = lax.dot_general(k, q_t[h], NN, preferred_element_type=jnp.float32)
            t = t * (SCALE * LOG2E)
            if masked:
                t = jnp.where(seen, t, NEG_BIG)
            old = peak_s[h : h + 1, :]
            new = jnp.maximum(old, jnp.max(t, axis=0, keepdims=True))
            fresh = jnp.sum(jnp.exp2(t - new), axis=0, keepdims=True)
            mass_s[h : h + 1, :] = mass_s[h : h + 1, :] * jnp.exp2(old - new) + fresh
            peak_s[h : h + 1, :] = new

    over_blocks(own, info, rows, body)
    log_total[...] = peak_s[...] + jnp.log(mass_s[...]) * LOG2E


def grad_kernel(
    heads, rows, levels,
    info, q_rot_0, q_t_0, log_total_0, q_rot_1, q_t_1, log_total_1, early, cot, cot_t, init,
    keys_k, cos_f, sin_f, codes_f, v_own, v_x, v_y1, v_y2, v_y3, v_core,
    out, bins, probs_s, out_s, delta_s, acc_s, values, keys, cos_k, sin_k, codes, sems,
):
    me = token_rank()
    own, first = me * rows, info[0]
    part = heads // 2
    q_rot = [q_rot_0.at[h] for h in range(part)] + [q_rot_1.at[h] for h in range(part)]
    q_t = [q_t_0.at[h] for h in range(part)] + [q_t_1.at[h] for h in range(part)]
    log_total = [ref.at[h : h + 1, :] for ref in (log_total_0, log_total_1) for h in range(part)]
    copies = [pltpu.make_async_copy(keys_k, keys, sems.at[0])]
    for j, (bits, ref, at) in enumerate(slots((v_own, v_x, v_y1, v_y2, v_y3, v_core))):
        start = pl.multiple_of((me ^ bits) * rows, rows)
        copies.append(
            pltpu.make_async_copy(
                ref.at[at * rows : (at + 1) * rows, :], values.at[pl.ds(start, rows), :], sems.at[1 + j]
            )
        )
    late = [
        pltpu.make_async_copy(cos_f, cos_k, sems.at[17]),
        pltpu.make_async_copy(sin_f, sin_k, sems.at[18]),
        pltpu.make_async_copy(codes_f, codes, sems.at[19]),
    ]
    for copy in copies + late:
        copy.start()
    out_s[...] = jnp.zeros_like(out_s)
    for copy in copies:
        copy.wait()

    def forward(b, masked):
        base = pl.multiple_of(b * BLOCK, BLOCK)
        k = keys[pl.ds(base, BLOCK), :]
        v = values[pl.ds(base, BLOCK), :]
        if masked:
            seen = visible_block(base, BLOCK, own, early[...], rows)
        for h in range(heads):
            s = lax.dot_general(k, q_t[h][...], NN, preferred_element_type=jnp.float32)
            p = jnp.exp2(s * (SCALE * LOG2E) - log_total[h][...])
            if masked:
                p = jnp.where(seen, p, 0.0)
            probs_s[b - first, h] = p
            out_s[h] += lax.dot_general(
                p.astype(jnp.bfloat16), v, TN, preferred_element_type=jnp.float32
            )

    over_blocks(own, info, rows, forward)
    for h in range(heads):
        o = out_s[h].astype(jnp.bfloat16)
        out[:, h * HD : (h + 1) * HD] = o
        prod = cot[:, h * HD : (h + 1) * HD].astype(jnp.float32) * o.astype(jnp.float32)
        delta_s[h : h + 1, :] = jnp.sum(prod.T, axis=0, keepdims=True)
    acc_s[...] = jnp.zeros_like(acc_s)
    last = (own + rows + BLOCK - 1) // BLOCK
    for copy in late:
        copy.wait()

    @pl.loop(first, last)
    def _(b):
        base = pl.multiple_of(b * BLOCK, BLOCK)
        v = values[pl.ds(base, BLOCK), :]
        dk = jnp.zeros((BLOCK, HD), jnp.float32)
        for h in range(heads):
            dp = lax.dot_general(v, cot_t[h], NN, preferred_element_type=jnp.float32)
            ds = (probs_s[b - first, h] * (dp - delta_s[h : h + 1, :])).astype(jnp.bfloat16)
            dk = dk + lax.dot_general(ds, q_rot[h][...], NN, preferred_element_type=jnp.float32)
        dk = dk * SCALE
        g = dk * cos_k[pl.ds(base, BLOCK), :] - pltpu.roll(dk, HD // 2, 1) * sin_k[pl.ds(base, BLOCK), :]
        code = codes[pl.ds(base, BLOCK), :].astype(jnp.float32)
        for level in range(levels):
            chosen = jnp.where(code == level, g, 0.0)
            acc_s[level] += jnp.sum(chosen.reshape(BLOCK // 8, 8, HD), axis=0)

    bins[...] = init[...] + jnp.sum(acc_s[...], axis=1)


def anywhere():
    return pl.BlockSpec(memory_space=pl.ANY)


def vmem():
    return pl.BlockSpec(memory_space=pltpu.VMEM)


def smem():
    return pl.BlockSpec(memory_space=pltpu.SMEM)


def cost(flops, size):
    return pl.CostEstimate(flops=flops, bytes_accessed=size, transcendentals=0)


def shards(hidden, w_query, w_key, w_value, key_codes, codebook, positions, cotangent):
    rows, part = hidden.shape
    width = w_query.shape[1]
    heads = width // HD
    levels = codebook.shape[1]
    ranks = lax.axis_size("tokens")
    total = rows * ranks
    group = lax.axis_size("tensor")
    rank = lax.axis_index("tensor")
    me = lax.axis_index("tokens")
    own = me * rows
    bf16, f32 = jnp.bfloat16, jnp.float32

    cross = lambda x, d: lax.ppermute(x, "tokens", [(i, i ^ d) for i in range(ranks)])

    def everyone(x, second=lambda v: v, third=lambda v: v):
        x_side = cross(x, 2)
        pair = second(jnp.concatenate([x, x_side], axis=0))
        y_side = [cross(pair, 4 * y) for y in (1, 2, 3)]
        core = cross(third(jnp.concatenate([pair] + y_side, axis=0)), 1)
        return (x, x_side, *y_side, core)

    def after(*others):
        return lambda v: lax.optimization_barrier((v, others))[0]

    flip = [(i, i ^ 1) for i in range(group)]
    up = [(i, (i + 2) % group) for i in range(group)]
    down = [(i, (i - 2) % group) for i in range(group)]
    send = functools.partial(lax.ppermute, axis_name="tensor")
    n = part // 2
    low = send(hidden, perm=up)
    high = send(hidden, perm=down)
    other = send(hidden, perm=flip)
    places = positions[None, :]
    packed, early, info = pl.pallas_call(
        functools.partial(pack_kernel, rows),
        out_shape=(
            jax.ShapeDtypeStruct((rows + TAIL, HD), bf16),
            jax.ShapeDtypeStruct((1, rows), jnp.int32),
            jax.ShapeDtypeStruct((2,), jnp.int32),
        ),
        in_specs=[vmem()] * 2,
        out_specs=(vmem(), vmem(), smem()),
        name="pack",
    )(key_codes, places)
    book = codebook.T
    inverse = jnp.exp((jnp.arange(HD) % (HD // 2)).astype(f32) * (-2.0 * math.log(ROPE_BASE) / HD))

    mate = rank ^ 1
    turn = lambda x, by: (x + by) % group
    shard = [rank, turn(rank, -2), turn(rank, 2), mate, turn(rank, 4)]
    shard += [turn(mate, -2), turn(mate, 2), turn(mate, 4)]
    place = jnp.stack([2 * x + j for x in shard for j in (0, 1)]).astype(jnp.int32)

    def project(pieces, first, weights, sums, share=1.0):
        steps, at = [], 0
        for piece in pieces:
            steps.append((at, at + piece.shape[1] // n))
            at = steps[-1][1]
        count = len(weights)
        whole = lambda shape: pl.BlockSpec(shape, lambda i, place: (0, 0))
        sizes = [(rows, w.shape[1]) for w in weights]
        flops = 2 * rows * n * at * sum(w.shape[1] for w in weights)
        return pl.pallas_call(
            functools.partial(project_kernel, steps, n, count, sums is not None),
            out_shape=[jax.ShapeDtypeStruct(size, f32) for size in sizes],
            grid_spec=pltpu.PrefetchScalarGridSpec(
                num_scalar_prefetch=1,
                grid=(at,),
                in_specs=[whole(piece.shape) for piece in pieces]
                + [pl.BlockSpec((n, w.shape[1]), lambda i, place: (place[first + i], 0)) for w in weights]
                + ([whole(size) for size in sizes] if sums is not None else []),
                out_specs=[whole(size) for size in sizes],
            ),
            compiler_params=pltpu.CompilerParams(vmem_limit_bytes=50 << 20),
            cost_estimate=cost(int(flops * share), int(flops * share) // rows),
            name="project",
        )(place, *pieces, *weights, *(sums if sums is not None else ()))

    everything = (w_query, w_key, w_value)
    sums = project([hidden], 0, everything, None)
    x_side = after(sums[0])(cross(packed, 2))
    pair = jnp.concatenate([packed, x_side], axis=0)
    y_side = [cross(pair, 4 * y) for y in (1, 2, 3)]
    low, high, other = after(*y_side)((low, high, other))
    far_a = send(low[:, :n], perm=up)
    far_b = send(high[:, n:], perm=down)
    other_low = send(other, perm=up)
    other_high = send(other, perm=down)
    other_far_a = send(far_a, perm=flip)
    other_far_b = send(far_b, perm=flip)
    sums = project([low, high, other], 2, everything, sums, 16.0)
    core = cross(jnp.concatenate([pair] + y_side, axis=0), 1)
    packed = (packed, x_side, *y_side, core)

    keys, cos_k, sin_k, codes, cot_t = pl.pallas_call(
        functools.partial(prep_kernel, rows, ranks, levels, heads),
        out_shape=(
            jax.ShapeDtypeStruct((total, HD), bf16),
            jax.ShapeDtypeStruct((total, HD), f32),
            jax.ShapeDtypeStruct((total, HD), f32),
            jax.ShapeDtypeStruct((total, HD), bf16),
            jax.ShapeDtypeStruct((heads, HD, rows), bf16),
        ),
        in_specs=[vmem()] * 3 + [anywhere()] * 6,
        out_specs=(vmem(),) * 5,
        scratch_shapes=[
            pltpu.VMEM((ranks * (rows + TAIL), HD), bf16),
            pltpu.SemaphoreType.DMA((ranks,)),
        ],
        compiler_params=pltpu.CompilerParams(vmem_limit_bytes=16 << 20),
        cost_estimate=cost(0, 0),
        name="prep",
    )(inverse[None, :], book, cotangent, *packed)

    sums, keys = lax.optimization_barrier((sums, keys))
    sums = project([far_a, far_b], 8, everything, sums, 0.0)
    rest = [other_low, other_high, other_far_a, other_far_b]
    value = pl.pallas_call(
        functools.partial(value_kernel, 10, n),
        out_shape=jax.ShapeDtypeStruct((rows, HD), bf16),
        in_specs=[smem()] + [vmem()] * (2 + len(rest)),
        out_specs=vmem(),
        compiler_params=pltpu.CompilerParams(vmem_limit_bytes=16 << 20),
        cost_estimate=cost(0, 0),
        name="value",
    )(place, w_value, sums[2], *rest)
    query_pre, key_true = project(rest, 10, (w_query, w_key), sums[:2])

    def log_totals(begin, count, query_pre):
        return pl.pallas_call(
            functools.partial(stats_kernel, begin, count, rows, levels, levels / total),
            out_shape=(
                jax.ShapeDtypeStruct((count, rows, HD), bf16),
                jax.ShapeDtypeStruct((count, HD, rows), bf16),
                jax.ShapeDtypeStruct((count, rows), f32),
                jax.ShapeDtypeStruct((levels, HD), f32),
            ),
            in_specs=[smem()] + [vmem()] * 5 + [anywhere()] * 3,
            out_specs=(vmem(),) * 4,
            scratch_shapes=[pltpu.VMEM((count, rows), f32)] * 2
            + [pltpu.VMEM((rows, HD), f32)] * 2
            + [pltpu.VMEM((total, HD), bf16), pltpu.SemaphoreType.DMA((3,))],
            compiler_params=pltpu.CompilerParams(vmem_limit_bytes=24 << 20),
            cost_estimate=cost(2 * rows * count * HD * total, 4 << 20),
            name="stats",
        )(info, query_pre, early, key_true, key_codes, book, cos_k, sin_k, keys)

    totals = []

    def second(pair):
        pair, ready = lax.optimization_barrier((pair, query_pre))
        totals.extend(log_totals(0, heads // 2, ready))
        return pair

    values = everyone(value, second, lambda v: after(totals[2])(v))
    q_rot_0, q_t_0, log_total_0, init = totals
    query_late, _ = lax.optimization_barrier((query_pre, values[2:5]))
    q_rot_1, q_t_1, log_total_1, _ = log_totals(heads // 2, heads // 2, query_late)

    most = total // BLOCK
    attention_out, local = pl.pallas_call(
        functools.partial(grad_kernel, heads, rows, levels),
        out_shape=(
            jax.ShapeDtypeStruct((rows, width), bf16),
            jax.ShapeDtypeStruct((levels, HD), f32),
        ),
        in_specs=[smem()] + [vmem()] * 10 + [anywhere()] * 10,
        out_specs=(vmem(),) * 2,
        scratch_shapes=[
            pltpu.VMEM((min(most, 7), heads, BLOCK, rows), f32),
            pltpu.VMEM((heads, rows, HD), f32),
            pltpu.VMEM((heads, rows), f32),
            pltpu.VMEM((levels, 8, HD), f32),
            pltpu.VMEM((total, HD), bf16),
            pltpu.VMEM((total, HD), bf16),
            pltpu.VMEM((total, HD), f32),
            pltpu.VMEM((total, HD), f32),
            pltpu.VMEM((total, HD), bf16),
            pltpu.SemaphoreType.DMA((20,)),
        ],
        compiler_params=pltpu.CompilerParams(vmem_limit_bytes=52 << 20),
        cost_estimate=cost(8 * rows * width * total, 8 << 20),
        name="grad",
    )(
        info, q_rot_0, q_t_0, log_total_0, q_rot_1, q_t_1, log_total_1, early, cotangent, cot_t, init,
        keys, cos_k, sin_k, codes, *values,
    )
    for d in (1, 2, 4, 8):
        local = local + cross(local, d)
    return (attention_out, local.T)


def solution(mesh):
    placed = (
        P("tokens", "tensor"),
        P(None, "tensor"),
        P(None, "tensor"),
        P(None, "tensor"),
        P("tokens", "tensor"),
        P("tensor", None),
        P("tokens"),
        P("tokens", "tensor"),
    )
    return jax.shard_map(
        shards,
        mesh=mesh,
        in_specs=placed,
        out_specs=(P("tokens", "tensor"), P("tensor", None)),
        check_vma=False,
    )
```

```python
import functools
import math

import jax
import jax.numpy as jnp
from jax import lax
from jax.experimental import pallas as pl
from jax.experimental.pallas import tpu as pltpu
from jax.sharding import PartitionSpec as P

HD = 128
ROPE_BASE = 500000.0
NEG_BIG = -1e30
LOG2E = math.log2(math.e)
SCALE = 1.0 / math.sqrt(HD)
BLOCK = 512
NN = (((1,), (0,)), ((), ()))
TN = (((0,), (0,)), ((), ()))
TAIL = 16


def sincos(angle):
    turns = jnp.floor(angle * (2.0 / math.pi) + 0.5)
    r = angle - turns * 1.5703125
    r = r - turns * 4.837512969970703125e-4
    r = r - turns * 7.54978995489188216e-8
    z = r * r
    s = ((-1.9515295891e-4 * z + 8.3321608736e-3) * z - 1.6666654611e-1) * z * r + r
    c = ((2.443315711809948e-5 * z - 1.388731625493765e-3) * z + 4.166664568298827e-2) * z * z
    c = c - 0.5 * z + 1.0
    quadrant = turns.astype(jnp.int32)
    odd = (quadrant & 1) == 1
    sine = jnp.where(odd, c, s)
    cosine = jnp.where(odd, s, c)
    sine = jnp.where((quadrant & 2) == 0, sine, -sine)
    cosine = jnp.where(((quadrant + 1) & 2) == 0, cosine, -cosine)
    return sine, cosine


def slots_y_first(pieces):
    own, y1, y2, y3, x, core = pieces
    found = [(0, own, 0), (4, y1, 0), (8, y2, 0), (12, y3, 0)]
    found += [(2 | 4 * j, x, j) for j in range(4)]
    return found + [(1 | (4 * j if j < 4 else 2 | 4 * (j - 4)), core, j) for j in range(8)]


def slots(pieces):
    own, x, y1, y2, y3, core = pieces
    found = [(0, own, 0), (2, x, 0)]
    for y, ref in ((1, y1), (2, y2), (3, y3)):
        found += [(4 * y, ref, 0), (4 * y + 2, ref, 1)]
    return found + [(2 * j + 1, core, j) for j in range(8)]


def token_rank():
    return lax.axis_index("tokens")


def pack_kernel(rows, key_codes, positions, packed, early, info):
    packed[:rows, :] = key_codes[...].astype(jnp.float32).astype(jnp.bfloat16)
    place = positions[...]
    high, low = place & ~63, place & 63
    wide = [x[:, j * HD : (j + 1) * HD] for x in (high, low) for j in range(rows // HD)]
    blank = jnp.zeros((TAIL - len(wide), HD), jnp.int32)
    tail = jnp.concatenate(wide + [blank], axis=0)
    packed[rows:, :] = tail.astype(jnp.float32).astype(jnp.bfloat16)
    index = token_rank() * rows + lax.broadcasted_iota(jnp.int32, (1, rows), 1)
    first = index - place
    early[...] = first
    first = first.astype(jnp.float32)
    info[0] = jnp.min(first).astype(jnp.int32) // BLOCK
    info[1] = jnp.max(first).astype(jnp.int32)


def prep_kernel(
    rows, ranks, levels, heads,
    inverse, book, cot, p_own, p_y1, p_y2, p_y3, p_x, p_core,
    keys, cos_k, sin_k, codes, cot_t, packed_s, sems,
):
    me = token_rank()
    tall = rows + TAIL
    copies = []
    for j, (bits, ref, at) in enumerate(slots_y_first((p_own, p_y1, p_y2, p_y3, p_x, p_core))):
        start = pl.multiple_of((me ^ bits) * tall, TAIL)
        copies.append(
            pltpu.make_async_copy(
                ref.at[at * tall : (at + 1) * tall, :], packed_s.at[pl.ds(start, tall), :], sems.at[j]
            )
        )
    for copy in copies:
        copy.start()
    for h in range(heads):
        cot_t[h] = cot[:, h * HD : (h + 1) * HD].T
    for copy in copies:
        copy.wait()
    eye = lax.broadcasted_iota(jnp.int32, (HD, HD), 0) == lax.broadcasted_iota(
        jnp.int32, (HD, HD), 1
    )
    lane = lax.broadcasted_iota(jnp.int32, (HD, HD), 1)
    ones = jnp.ones((2 * HD, HD), jnp.bfloat16)

    @pl.loop(0, ranks)
    def _(i):
        source = pl.multiple_of(i * tall, TAIL)
        tail = packed_s[pl.ds(source + rows, TAIL), :].astype(jnp.float32)
        for part in range(rows // HD):
            target = pl.multiple_of(i * rows + part * HD, HD)
            high = jnp.where(eye, tail[part : part + 1, :], 0.0)
            low = jnp.where(eye, tail[rows // HD + part : rows // HD + part + 1, :], 0.0)
            digits = jnp.concatenate([high, low], axis=1).astype(jnp.bfloat16)
            place = lax.dot_general(digits, ones, NN, preferred_element_type=jnp.float32)
            sine, cosine = sincos(place * inverse[...])
            sine = jnp.where(lane < HD // 2, -sine, sine)
            cos_k[pl.ds(target, HD), :] = cosine
            sin_k[pl.ds(target, HD), :] = sine
            raw = packed_s[pl.ds(source + part * HD, HD), :]
            codes[pl.ds(target, HD), :] = raw
            code = raw.astype(jnp.float32).astype(jnp.int32)
            layer = [book[e : e + 1, :] for e in range(levels)]
            bit = 1
            while len(layer) > 1:
                on = (code & bit) != 0
                layer = [jnp.where(on, layer[j + 1], layer[j]) for j in range(0, len(layer), 2)]
                bit *= 2
            deq = layer[0]
            turned = deq * cosine + pltpu.roll(deq, HD // 2, 1) * sine
            keys[pl.ds(target, HD), :] = turned.astype(jnp.bfloat16)


def shard_rows(place, n, part):
    return pl.ds(pl.multiple_of(place[n] * part, part), part)


def fetch(pieces, x_s, sem):
    copies, at = [], 0
    for piece in pieces:
        width = piece.shape[1]
        copies.append(pltpu.make_async_copy(piece, x_s.at[:, at : at + width], sem(len(copies))))
        at += width
    return copies


def project_kernel(
    count, part, place, wq, wk, wv, *refs,
):
    pieces, (q_out, kv_out, x_s, wq_s, wkv_s, sems) = refs[:count], refs[count:]
    copies = []
    for n, piece in enumerate(pieces):
        rows = shard_rows(place, n, part)
        copies.append([
            pltpu.make_async_copy(piece, x_s.at[n], sems.at[4 * n]),
            pltpu.make_async_copy(wq.at[rows, :], wq_s.at[n], sems.at[4 * n + 1]),
            pltpu.make_async_copy(wk.at[rows, :], wkv_s.at[n, :, :HD], sems.at[4 * n + 2]),
            pltpu.make_async_copy(wv.at[rows, :], wkv_s.at[n, :, HD:], sems.at[4 * n + 3]),
        ])
        for copy in copies[-1]:
            copy.start()
    for n in range(count):
        for copy in copies[n]:
            copy.wait()
        x = x_s[n]
        q = jnp.dot(x, wq_s[n], preferred_element_type=jnp.float32)
        kv = jnp.dot(x, wkv_s[n], preferred_element_type=jnp.float32)
        q_out[...] = q if n == 0 else q_out[...] + q
        kv_out[...] = kv if n == 0 else kv_out[...] + kv


def value_kernel(first, count, part, place, w, before, *refs):
    pieces, (value, x_s, w_s, before_s, sems) = refs[:-5], refs[-5:]
    copies = fetch(pieces, x_s, lambda j: sems.at[j])
    copies.append(pltpu.make_async_copy(before.at[:, HD:], before_s, sems.at[len(copies)]))
    for n in range(count):
        copies.append(
            pltpu.make_async_copy(w.at[shard_rows(place, first + n, part), :], w_s.at[n], sems.at[len(copies)])
        )
    for copy in copies:
        copy.start()
    for copy in copies:
        copy.wait()
    total = before_s[...]
    for n in range(count):
        total += jnp.dot(x_s[:, n * part : (n + 1) * part], w_s[n], preferred_element_type=jnp.float32)
    value[...] = total.astype(jnp.bfloat16)


def visible_block(base, block, own, earliest, rows):
    key = base + lax.broadcasted_iota(jnp.int32, (block, rows), 0)
    query = own + lax.broadcasted_iota(jnp.int32, (block, rows), 1)
    return (key <= query) & (key >= earliest)


def over_blocks(own, info, rows, body):
    first, edge = info[0], info[1]
    last = (own + rows + BLOCK - 1) // BLOCK

    @pl.loop(first, last)
    def _(b):
        masked = (b * BLOCK < edge) | (b * BLOCK + BLOCK > own)

        @pl.when(masked)
        def _():
            body(b, True)

        @pl.when(jnp.logical_not(masked))
        def _():
            body(b, False)


def stats_kernel(
    begin, heads, rows, levels, weight, first, count, part,
    place, info, early, codes, book, cos_k, sin_k, keys_k, q_before, kv_before, wq, wk, *refs,
):
    pieces = refs[:-17]
    (
        q_rot, q_t, log_total, bins,
        peak_s, mass_s, cos_q, sin_q, keys, x_s, wq_s, wk_s, q_s, true_s, x_sems, w_sems, sems,
    ) = refs[-17:]
    own = token_rank() * rows
    mine = pl.ds(pl.multiple_of(own, rows), rows)
    columns = pl.ds(begin * HD, heads * HD)
    loads = fetch(pieces, x_s, lambda j: x_sems.at[j])
    weights = []
    for n in range(count):
        at = shard_rows(place, first + n, part)
        row = [pltpu.make_async_copy(wq.at[at, columns], wq_s.at[n], w_sems.at[2 * n])]
        if begin == 0:
            row.append(pltpu.make_async_copy(wk.at[at, :], wk_s.at[n], w_sems.at[2 * n + 1]))
        weights.append(row)
    before = [pltpu.make_async_copy(q_before.at[:, columns], q_s, sems.at[0])]
    if begin == 0:
        before.append(pltpu.make_async_copy(kv_before.at[:, :HD], true_s, sems.at[1]))
    tables = [
        pltpu.make_async_copy(cos_k.at[mine, :], cos_q, sems.at[2]),
        pltpu.make_async_copy(sin_k.at[mine, :], sin_q, sems.at[3]),
        pltpu.make_async_copy(keys_k, keys, sems.at[4]),
    ]
    for copy in before + loads + sum(weights, []) + tables:
        copy.start()
    peak_s[...] = jnp.full_like(peak_s, NEG_BIG)
    mass_s[...] = jnp.zeros_like(mass_s)
    for copy in before + loads:
        copy.wait()
    for n in range(count):
        for copy in weights[n]:
            copy.wait()
        x = x_s[:, n * part : (n + 1) * part]
        q_s[...] += jnp.dot(x, wq_s[n], preferred_element_type=jnp.float32)
        if begin == 0:
            true_s[...] += jnp.dot(x, wk_s[n], preferred_element_type=jnp.float32)
    if begin == 0:
        code = codes[...]
        for level in range(levels):
            entry = weight * (book[level : level + 1, :] - true_s[...])
            bins[level : level + 1, :] = jnp.sum(
                jnp.where(code == level, entry, 0.0), axis=0, keepdims=True
            )
    else:
        bins[...] = jnp.zeros_like(bins)
    for copy in tables:
        copy.wait()
    for h in range(heads):
        x = q_s[:, h * HD : (h + 1) * HD]
        turned = (x * cos_q[...] + pltpu.roll(x, HD // 2, 1) * sin_q[...]).astype(jnp.bfloat16)
        q_rot[h] = turned
        q_t[h] = turned.T

    def body(b, masked):
        base = pl.multiple_of(b * BLOCK, BLOCK)
        k = keys[pl.ds(base, BLOCK), :]
        if masked:
            seen = visible_block(base, BLOCK, own, early[...], rows)
        for h in range(heads):
            t = lax.dot_general(k, q_t[h], NN, preferred_element_type=jnp.float32)
            t = t * (SCALE * LOG2E)
            if masked:
                t = jnp.where(seen, t, NEG_BIG)
            old = peak_s[h : h + 1, :]
            new = jnp.maximum(old, jnp.max(t, axis=0, keepdims=True))
            fresh = jnp.sum(jnp.exp2(t - new), axis=0, keepdims=True)
            mass_s[h : h + 1, :] = mass_s[h : h + 1, :] * jnp.exp2(old - new) + fresh
            peak_s[h : h + 1, :] = new

    over_blocks(own, info, rows, body)
    log_total[...] = peak_s[...] + jnp.log(mass_s[...]) * LOG2E


def grad_kernel(
    heads, rows, levels,
    info, q_rot_0, q_t_0, log_total_0, q_rot_1, q_t_1, log_total_1, early, cot, cot_t, init,
    keys_k, cos_f, sin_f, codes_f, v_own, v_x, v_y1, v_y2, v_y3, v_core,
    out, bins, probs_s, out_s, delta_s, acc_s, values, keys, cos_k, sin_k, codes, sems,
):
    me = token_rank()
    own, first = me * rows, info[0]
    part = heads // 2
    q_rot = [q_rot_0.at[h] for h in range(part)] + [q_rot_1.at[h] for h in range(part)]
    q_t = [q_t_0.at[h] for h in range(part)] + [q_t_1.at[h] for h in range(part)]
    log_total = [ref.at[h : h + 1, :] for ref in (log_total_0, log_total_1) for h in range(part)]
    copies = [pltpu.make_async_copy(keys_k, keys, sems.at[0])]
    for j, (bits, ref, at) in enumerate(slots((v_own, v_x, v_y1, v_y2, v_y3, v_core))):
        start = pl.multiple_of((me ^ bits) * rows, rows)
        copies.append(
            pltpu.make_async_copy(
                ref.at[at * rows : (at + 1) * rows, :], values.at[pl.ds(start, rows), :], sems.at[1 + j]
            )
        )
    late = [
        pltpu.make_async_copy(cos_f, cos_k, sems.at[17]),
        pltpu.make_async_copy(sin_f, sin_k, sems.at[18]),
        pltpu.make_async_copy(codes_f, codes, sems.at[19]),
    ]
    for copy in copies + late:
        copy.start()
    out_s[...] = jnp.zeros_like(out_s)
    for copy in copies:
        copy.wait()

    def forward(b, masked):
        base = pl.multiple_of(b * BLOCK, BLOCK)
        k = keys[pl.ds(base, BLOCK), :]
        v = values[pl.ds(base, BLOCK), :]
        if masked:
            seen = visible_block(base, BLOCK, own, early[...], rows)
        for h in range(heads):
            s = lax.dot_general(k, q_t[h][...], NN, preferred_element_type=jnp.float32)
            p = jnp.exp2(s * (SCALE * LOG2E) - log_total[h][...])
            if masked:
                p = jnp.where(seen, p, 0.0)
            probs_s[b - first, h] = p
            out_s[h] += lax.dot_general(
                p.astype(jnp.bfloat16), v, TN, preferred_element_type=jnp.float32
            )

    over_blocks(own, info, rows, forward)
    for h in range(heads):
        o = out_s[h].astype(jnp.bfloat16)
        out[:, h * HD : (h + 1) * HD] = o
        prod = cot[:, h * HD : (h + 1) * HD].astype(jnp.float32) * o.astype(jnp.float32)
        delta_s[h : h + 1, :] = jnp.sum(prod.T, axis=0, keepdims=True)
    acc_s[...] = jnp.zeros_like(acc_s)
    last = (own + rows + BLOCK - 1) // BLOCK
    for copy in late:
        copy.wait()

    @pl.loop(first, last)
    def _(b):
        base = pl.multiple_of(b * BLOCK, BLOCK)
        v = values[pl.ds(base, BLOCK), :]
        dk = jnp.zeros((BLOCK, HD), jnp.float32)
        for h in range(heads):
            dp = lax.dot_general(v, cot_t[h], NN, preferred_element_type=jnp.float32)
            ds = (probs_s[b - first, h] * (dp - delta_s[h : h + 1, :])).astype(jnp.bfloat16)
            dk = dk + lax.dot_general(ds, q_rot[h][...], NN, preferred_element_type=jnp.float32)
        dk = dk * SCALE
        g = dk * cos_k[pl.ds(base, BLOCK), :] - pltpu.roll(dk, HD // 2, 1) * sin_k[pl.ds(base, BLOCK), :]
        code = codes[pl.ds(base, BLOCK), :].astype(jnp.float32)
        for level in range(levels):
            chosen = jnp.where(code == level, g, 0.0)
            acc_s[level] += jnp.sum(chosen.reshape(BLOCK // 8, 8, HD), axis=0)

    bins[...] = init[...] + jnp.sum(acc_s[...], axis=1)


def anywhere():
    return pl.BlockSpec(memory_space=pl.ANY)


def vmem():
    return pl.BlockSpec(memory_space=pltpu.VMEM)


def smem():
    return pl.BlockSpec(memory_space=pltpu.SMEM)


def cost(flops, size):
    return pl.CostEstimate(flops=flops, bytes_accessed=size, transcendentals=0)


def shards(hidden, w_query, w_key, w_value, key_codes, codebook, positions, cotangent):
    rows, part = hidden.shape
    width = w_query.shape[1]
    heads = width // HD
    levels = codebook.shape[1]
    ranks = lax.axis_size("tokens")
    total = rows * ranks
    group = lax.axis_size("tensor")
    rank = lax.axis_index("tensor")
    me = lax.axis_index("tokens")
    own = me * rows
    bf16, f32 = jnp.bfloat16, jnp.float32

    cross = lambda x, d: lax.ppermute(x, "tokens", [(i, i ^ d) for i in range(ranks)])

    def everyone(x, first, second, third):
        x_side = first(cross(x, 2))
        pair = second(jnp.concatenate([x, x_side], axis=0))
        y_side = [cross(pair, 4 * y) for y in (1, 2, 3)]
        core = cross(third(jnp.concatenate([pair] + y_side, axis=0)), 1)
        return (x, x_side, *y_side, core)

    def after(*others):
        return lambda v: lax.optimization_barrier((v, others))[0]

    flip = [(i, i ^ 1) for i in range(group)]
    up = [(i, (i + 2) % group) for i in range(group)]
    down = [(i, (i - 2) % group) for i in range(group)]
    send = functools.partial(lax.ppermute, axis_name="tensor")
    n = part // 2
    low = send(hidden, perm=up)
    high = send(hidden, perm=down)
    other = send(hidden, perm=flip)
    places = positions[None, :]
    packed, early, info = pl.pallas_call(
        functools.partial(pack_kernel, rows),
        out_shape=(
            jax.ShapeDtypeStruct((rows + TAIL, HD), bf16),
            jax.ShapeDtypeStruct((1, rows), jnp.int32),
            jax.ShapeDtypeStruct((2,), jnp.int32),
        ),
        in_specs=[vmem()] * 2,
        out_specs=(vmem(), vmem(), smem()),
        name="pack",
    )(key_codes, places)
    book = codebook.T
    inverse = jnp.exp((jnp.arange(HD) % (HD // 2)).astype(f32) * (-2.0 * math.log(ROPE_BASE) / HD))

    mate = rank ^ 1
    turn = lambda x, by: (x + by) % group
    shard = [rank, turn(rank, -2), turn(rank, 2), mate]
    shard += [turn(rank, 4), turn(mate, -2), turn(mate, 2), turn(mate, 4)]
    place = jnp.stack(shard).astype(jnp.int32)

    y_side = [cross(packed, 4 * y) for y in (1, 2, 3)]
    column = jnp.concatenate([packed] + y_side, axis=0)
    x_side = cross(column, 2)
    low, high, other = after(column)((low, high, other))
    far_a = send(low[:, :n], perm=up)
    far_b = send(high[:, n:], perm=down)
    other_low = send(other, perm=up)
    other_high = send(other, perm=down)
    other_far_a = send(far_a, perm=flip)
    other_far_b = send(far_b, perm=flip)

    half = group // 2
    low, high, other = after(far_a, far_b)((low, high, other))
    q_sum, kv_sum = pl.pallas_call(
        functools.partial(project_kernel, half, part),
        out_shape=(jax.ShapeDtypeStruct((rows, width), f32), jax.ShapeDtypeStruct((rows, 2 * HD), f32)),
        in_specs=[smem()] + [anywhere()] * (3 + half),
        out_specs=(vmem(),) * 2,
        scratch_shapes=[
            pltpu.VMEM((half, rows, part), bf16),
            pltpu.VMEM((half, part, width), bf16),
            pltpu.VMEM((half, part, 2 * HD), bf16),
            pltpu.SemaphoreType.DMA((4 * half,)),
        ],
        compiler_params=pltpu.CompilerParams(vmem_limit_bytes=50 << 20),
        cost_estimate=cost(1 << 34, 0),
        name="project",
    )(place, w_query, w_key, w_value, hidden, low, high, other)
    core = cross(jnp.concatenate([column, x_side], axis=0), 1)
    packed = (packed, *y_side, x_side, core)

    rest = [far_a, far_b, other_low, other_high, other_far_a, other_far_b]
    value = pl.pallas_call(
        functools.partial(value_kernel, half, half, part),
        out_shape=jax.ShapeDtypeStruct((rows, HD), bf16),
        in_specs=[smem()] + [anywhere()] * (2 + len(rest)),
        out_specs=vmem(),
        scratch_shapes=[
            pltpu.VMEM((rows, half * part), bf16),
            pltpu.VMEM((half, part, HD), bf16),
            pltpu.VMEM((rows, HD), f32),
            pltpu.SemaphoreType.DMA((half + len(rest) + 1,)),
        ],
        compiler_params=pltpu.CompilerParams(vmem_limit_bytes=50 << 20),
        cost_estimate=cost(0, 0),
        name="value",
    )(place, w_value, kv_sum, *rest)

    keys, cos_k, sin_k, codes, cot_t = pl.pallas_call(
        functools.partial(prep_kernel, rows, ranks, levels, heads),
        out_shape=(
            jax.ShapeDtypeStruct((total, HD), bf16),
            jax.ShapeDtypeStruct((total, HD), f32),
            jax.ShapeDtypeStruct((total, HD), f32),
            jax.ShapeDtypeStruct((total, HD), bf16),
            jax.ShapeDtypeStruct((heads, HD, rows), bf16),
        ),
        in_specs=[vmem()] * 3 + [anywhere()] * 6,
        out_specs=(vmem(),) * 5,
        scratch_shapes=[
            pltpu.VMEM((ranks * (rows + TAIL), HD), bf16),
            pltpu.SemaphoreType.DMA((ranks,)),
        ],
        compiler_params=pltpu.CompilerParams(vmem_limit_bytes=16 << 20),
        cost_estimate=cost(1 << 32, 0),
        name="prep",
    )(after(value)(inverse[None, :]), book, cotangent, *packed)

    def log_totals(begin, count, place):
        return pl.pallas_call(
            functools.partial(
                stats_kernel, begin, count, rows, levels, levels / total, half, half, part
            ),
            out_shape=(
                jax.ShapeDtypeStruct((count, rows, HD), bf16),
                jax.ShapeDtypeStruct((count, HD, rows), bf16),
                jax.ShapeDtypeStruct((count, rows), f32),
                jax.ShapeDtypeStruct((levels, HD), f32),
            ),
            in_specs=[smem()] * 2 + [vmem()] * 3 + [anywhere()] * (7 + len(rest)),
            out_specs=(vmem(),) * 4,
            scratch_shapes=[pltpu.VMEM((count, rows), f32)] * 2
            + [pltpu.VMEM((rows, HD), f32)] * 2
            + [
                pltpu.VMEM((total, HD), bf16),
                pltpu.VMEM((rows, half * part), bf16),
                pltpu.VMEM((half, part, count * HD), bf16),
                pltpu.VMEM((half, part, HD), bf16),
                pltpu.VMEM((rows, count * HD), f32),
                pltpu.VMEM((rows, HD), f32),
                pltpu.SemaphoreType.DMA((len(rest),)),
                pltpu.SemaphoreType.DMA((2 * half,)),
                pltpu.SemaphoreType.DMA((5,)),
            ],
            compiler_params=pltpu.CompilerParams(vmem_limit_bytes=50 << 20),
            cost_estimate=cost(1 << 34, 0),
            name="stats",
        )(
            place, info, early, key_codes, book, cos_k, sin_k, keys,
            q_sum, kv_sum, w_query, w_key, *rest,
        )

    totals = []

    def second(pair):
        pair, ready = lax.optimization_barrier((pair, place))
        totals.extend(log_totals(0, heads // 2, ready))
        return pair

    values = everyone(value, after(keys), second, lambda v: after(totals[2])(v))
    q_rot_0, q_t_0, log_total_0, init = totals
    late, _ = lax.optimization_barrier((place, values[2:5]))
    q_rot_1, q_t_1, log_total_1, _ = log_totals(heads // 2, heads // 2, late)

    most = total // BLOCK
    attention_out, local = pl.pallas_call(
        functools.partial(grad_kernel, heads, rows, levels),
        out_shape=(
            jax.ShapeDtypeStruct((rows, width), bf16),
            jax.ShapeDtypeStruct((levels, HD), f32),
        ),
        in_specs=[smem()] + [vmem()] * 10 + [anywhere()] * 10,
        out_specs=(vmem(),) * 2,
        scratch_shapes=[
            pltpu.VMEM((min(most, 7), heads, BLOCK, rows), f32),
            pltpu.VMEM((heads, rows, HD), f32),
            pltpu.VMEM((heads, rows), f32),
            pltpu.VMEM((levels, 8, HD), f32),
            pltpu.VMEM((total, HD), bf16),
            pltpu.VMEM((total, HD), bf16),
            pltpu.VMEM((total, HD), f32),
            pltpu.VMEM((total, HD), f32),
            pltpu.VMEM((total, HD), bf16),
            pltpu.SemaphoreType.DMA((20,)),
        ],
        compiler_params=pltpu.CompilerParams(vmem_limit_bytes=52 << 20),
        cost_estimate=cost(8 * rows * width * total, 8 << 20),
        name="grad",
    )(
        info, q_rot_0, q_t_0, log_total_0, q_rot_1, q_t_1, log_total_1, early, cotangent, cot_t, init,
        keys, cos_k, sin_k, codes, *values,
    )
    for d in (1, 2, 4, 8):
        local = local + cross(local, d)
    return (attention_out, local.T)


def solution(mesh):
    placed = (
        P("tokens", "tensor"),
        P(None, "tensor"),
        P(None, "tensor"),
        P(None, "tensor"),
        P("tokens", "tensor"),
        P("tensor", None),
        P("tokens"),
        P("tokens", "tensor"),
    )
    return jax.shard_map(
        shards,
        mesh=mesh,
        in_specs=placed,
        out_specs=(P("tokens", "tensor"), P("tensor", None)),
        check_vma=False,
    )
```

```python
import functools
import math

import jax
import jax.numpy as jnp
from jax import lax
from jax.experimental import pallas as pl
from jax.experimental.pallas import tpu as pltpu
from jax.sharding import PartitionSpec as P

HD = 128
ROPE_BASE = 500000.0
NEG_BIG = -1e30
LOG2E = math.log2(math.e)
SCALE = 1.0 / math.sqrt(HD)
BLOCK = 512
NN = (((1,), (0,)), ((), ()))
TN = (((0,), (0,)), ((), ()))
TAIL = 16


def sincos(angle):
    turns = jnp.floor(angle * (2.0 / math.pi) + 0.5)
    r = angle - turns * 1.5703125
    r = r - turns * 4.837512969970703125e-4
    r = r - turns * 7.54978995489188216e-8
    z = r * r
    s = ((-1.9515295891e-4 * z + 8.3321608736e-3) * z - 1.6666654611e-1) * z * r + r
    c = ((2.443315711809948e-5 * z - 1.388731625493765e-3) * z + 4.166664568298827e-2) * z * z
    c = c - 0.5 * z + 1.0
    quadrant = turns.astype(jnp.int32)
    odd = (quadrant & 1) == 1
    sine = jnp.where(odd, c, s)
    cosine = jnp.where(odd, s, c)
    sine = jnp.where((quadrant & 2) == 0, sine, -sine)
    cosine = jnp.where(((quadrant + 1) & 2) == 0, cosine, -cosine)
    return sine, cosine


def slots_y_first(pieces):
    own, y1, y2, y3, x, core = pieces
    found = [(0, own, 0), (4, y1, 0), (8, y2, 0), (12, y3, 0)]
    found += [(2 | 4 * j, x, j) for j in range(4)]
    return found + [(1 | (4 * j if j < 4 else 2 | 4 * (j - 4)), core, j) for j in range(8)]


def slots(pieces):
    own, x, y1, y2, y3, core = pieces
    found = [(0, own, 0), (2, x, 0)]
    for y, ref in ((1, y1), (2, y2), (3, y3)):
        found += [(4 * y, ref, 0), (4 * y + 2, ref, 1)]
    return found + [(2 * j + 1, core, j) for j in range(8)]


def token_rank():
    return lax.axis_index("tokens")


def pack_kernel(rows, key_codes, positions, packed, early, info):
    packed[:rows, :] = key_codes[...].astype(jnp.float32).astype(jnp.bfloat16)
    place = positions[...]
    high, low = place & ~63, place & 63
    wide = [x[:, j * HD : (j + 1) * HD] for x in (high, low) for j in range(rows // HD)]
    blank = jnp.zeros((TAIL - len(wide), HD), jnp.int32)
    tail = jnp.concatenate(wide + [blank], axis=0)
    packed[rows:, :] = tail.astype(jnp.float32).astype(jnp.bfloat16)
    index = token_rank() * rows + lax.broadcasted_iota(jnp.int32, (1, rows), 1)
    first = index - place
    early[...] = first
    first = first.astype(jnp.float32)
    info[0] = jnp.min(first).astype(jnp.int32) // BLOCK
    info[1] = jnp.max(first).astype(jnp.int32)


def prep_kernel(
    rows, ranks, levels, heads,
    inverse, book, cot, p_own, p_y1, p_y2, p_y3, p_x, p_core,
    keys_f, cos_f, sin_f, codes_f, cot_t, packed_s, keys, cos_k, sin_k, codes, sems, out_sems,
):
    me = token_rank()
    tall = rows + TAIL
    copies = []
    for j, (bits, ref, at) in enumerate(slots_y_first((p_own, p_y1, p_y2, p_y3, p_x, p_core))):
        start = pl.multiple_of((me ^ bits) * tall, TAIL)
        copies.append(
            pltpu.make_async_copy(
                ref.at[at * tall : (at + 1) * tall, :], packed_s.at[pl.ds(start, tall), :], sems.at[j]
            )
        )
    for copy in copies:
        copy.start()
    for h in range(heads):
        cot_t[h] = cot[:, h * HD : (h + 1) * HD].T
    for copy in copies:
        copy.wait()
    eye = lax.broadcasted_iota(jnp.int32, (HD, HD), 0) == lax.broadcasted_iota(
        jnp.int32, (HD, HD), 1
    )
    left = lax.broadcasted_iota(jnp.int32, (HD, HD), 1) < HD // 2
    ones = jnp.ones((2 * HD, HD), jnp.bfloat16)
    sides = rows // HD
    outs = [(keys, keys_f), (cos_k, cos_f), (sin_k, sin_f), (codes, codes_f)]

    @pl.loop(0, ranks)
    def _(i):
        source = pl.multiple_of(i * tall, TAIL)
        tail = packed_s[pl.ds(source + rows, TAIL), :].astype(jnp.float32)
        places = []
        for part in range(sides):
            high = jnp.where(eye, tail[part : part + 1, :], 0.0)
            low = jnp.where(eye, tail[sides + part : sides + part + 1, :], 0.0)
            digits = jnp.concatenate([high, low], axis=1).astype(jnp.bfloat16)
            places.append(lax.dot_general(digits, ones, NN, preferred_element_type=jnp.float32))
        for part in range(0, sides, 2):
            sine, cosine = sincos(jnp.where(left, places[part], places[part + 1]) * inverse[...])
            sine_r, cosine_r = pltpu.roll(sine, HD // 2, 1), pltpu.roll(cosine, HD // 2, 1)
            tables = (
                (jnp.where(left, cosine, cosine_r), jnp.where(left, -sine, sine_r)),
                (jnp.where(left, cosine_r, cosine), jnp.where(left, -sine_r, sine)),
            )
            for side, (cosine, sine) in enumerate(tables):
                at = part + side
                target = pl.multiple_of(i * rows + at * HD, HD)
                cos_k[pl.ds(target, HD), :] = cosine
                sin_k[pl.ds(target, HD), :] = sine
                raw = packed_s[pl.ds(source + at * HD, HD), :]
                codes[pl.ds(target, HD), :] = raw
                code = raw.astype(jnp.float32).astype(jnp.int32)
                layer = [book[e : e + 1, :] for e in range(levels)]
                bit = 1
                while len(layer) > 1:
                    on = (code & bit) != 0
                    layer = [jnp.where(on, layer[j + 1], layer[j]) for j in range(0, len(layer), 2)]
                    bit *= 2
                deq = layer[0]
                turned = deq * cosine + pltpu.roll(deq, HD // 2, 1) * sine
                keys[pl.ds(target, HD), :] = turned.astype(jnp.bfloat16)
        block = pl.ds(pl.multiple_of(i * rows, rows), rows)
        for j, (ref, full) in enumerate(outs):
            pltpu.make_async_copy(ref.at[block, :], full.at[block, :], out_sems.at[j]).start()

    for j, (ref, full) in enumerate(outs):
        pltpu.make_async_copy(ref, full, out_sems.at[j]).wait()


def shard_rows(place, n, part):
    return pl.ds(pl.multiple_of(place[n] * part, part), part)


def fetch(pieces, x_s, sem):
    copies, at = [], 0
    for piece in pieces:
        width = piece.shape[1]
        copies.append(pltpu.make_async_copy(piece, x_s.at[:, at : at + width], sem(len(copies))))
        at += width
    return copies


def project_kernel(
    count, part, place, wq, wk, wv, *refs,
):
    pieces, (q_out, kv_out, x_s, wq_s, wkv_s, sems) = refs[:count], refs[count:]
    copies = []
    for n, piece in enumerate(pieces):
        rows = shard_rows(place, n, part)
        copies.append([
            pltpu.make_async_copy(piece, x_s.at[n], sems.at[4 * n]),
            pltpu.make_async_copy(wq.at[rows, :], wq_s.at[n], sems.at[4 * n + 1]),
            pltpu.make_async_copy(wk.at[rows, :], wkv_s.at[n, :, :HD], sems.at[4 * n + 2]),
            pltpu.make_async_copy(wv.at[rows, :], wkv_s.at[n, :, HD:], sems.at[4 * n + 3]),
        ])
        for copy in copies[-1]:
            copy.start()
    for n in range(count):
        for copy in copies[n]:
            copy.wait()
        x = x_s[n]
        q = jnp.dot(x, wq_s[n], preferred_element_type=jnp.float32)
        kv = jnp.dot(x, wkv_s[n], preferred_element_type=jnp.float32)
        q_out[...] = q if n == 0 else q_out[...] + q
        kv_out[...] = kv if n == 0 else kv_out[...] + kv


def value_kernel(first, count, part, place, w, before, *refs):
    pieces, (value, x_s, w_s, before_s, sems) = refs[:-5], refs[-5:]
    copies = fetch(pieces, x_s, lambda j: sems.at[j])
    copies.append(pltpu.make_async_copy(before.at[:, HD:], before_s, sems.at[len(copies)]))
    for n in range(count):
        copies.append(
            pltpu.make_async_copy(w.at[shard_rows(place, first + n, part), :], w_s.at[n], sems.at[len(copies)])
        )
    for copy in copies:
        copy.start()
    for copy in copies:
        copy.wait()
    total = before_s[...]
    for n in range(count):
        total += jnp.dot(x_s[:, n * part : (n + 1) * part], w_s[n], preferred_element_type=jnp.float32)
    value[...] = total.astype(jnp.bfloat16)


def visible_block(base, block, own, earliest, rows):
    key = base + lax.broadcasted_iota(jnp.int32, (block, rows), 0)
    query = own + lax.broadcasted_iota(jnp.int32, (block, rows), 1)
    return (key <= query) & (key >= earliest)


def over_blocks(own, info, rows, body):
    first, edge = info[0], info[1]
    last = (own + rows + BLOCK - 1) // BLOCK

    @pl.loop(first, last)
    def _(b):
        masked = (b * BLOCK < edge) | (b * BLOCK + BLOCK > own)

        @pl.when(masked)
        def _():
            body(b, True)

        @pl.when(jnp.logical_not(masked))
        def _():
            body(b, False)


def stats_kernel(
    begin, heads, rows, levels, weight, first, count, part,
    place, info, early, codes, book, cos_k, sin_k, keys_k, q_before, kv_before, wq, wk, *refs,
):
    pieces = refs[:-17]
    (
        q_rot, q_t, log_total, bins,
        peak_s, mass_s, cos_q, sin_q, keys, x_s, wq_s, wk_s, q_s, true_s, x_sems, w_sems, sems,
    ) = refs[-17:]
    own = token_rank() * rows
    mine = pl.ds(pl.multiple_of(own, rows), rows)
    columns = pl.ds(begin * HD, heads * HD)
    loads = fetch(pieces, x_s, lambda j: x_sems.at[j])
    weights = []
    for n in range(count):
        at = shard_rows(place, first + n, part)
        row = [pltpu.make_async_copy(wq.at[at, columns], wq_s.at[n], w_sems.at[2 * n])]
        if begin == 0:
            row.append(pltpu.make_async_copy(wk.at[at, :], wk_s.at[n], w_sems.at[2 * n + 1]))
        weights.append(row)
    before = [pltpu.make_async_copy(q_before.at[:, columns], q_s, sems.at[0])]
    if begin == 0:
        before.append(pltpu.make_async_copy(kv_before.at[:, :HD], true_s, sems.at[1]))
    tables = [
        pltpu.make_async_copy(cos_k.at[mine, :], cos_q, sems.at[2]),
        pltpu.make_async_copy(sin_k.at[mine, :], sin_q, sems.at[3]),
        pltpu.make_async_copy(keys_k, keys, sems.at[4]),
    ]
    for copy in before + loads + sum(weights, []) + tables:
        copy.start()
    peak_s[...] = jnp.full_like(peak_s, NEG_BIG)
    mass_s[...] = jnp.zeros_like(mass_s)
    for copy in before + loads:
        copy.wait()
    for n in range(count):
        for copy in weights[n]:
            copy.wait()
        x = x_s[:, n * part : (n + 1) * part]
        q_s[...] += jnp.dot(x, wq_s[n], preferred_element_type=jnp.float32)
        if begin == 0:
            true_s[...] += jnp.dot(x, wk_s[n], preferred_element_type=jnp.float32)
    if begin == 0:
        code = codes[...]
        for level in range(levels):
            entry = weight * (book[level : level + 1, :] - true_s[...])
            bins[level : level + 1, :] = jnp.sum(
                jnp.where(code == level, entry, 0.0), axis=0, keepdims=True
            )
    else:
        bins[...] = jnp.zeros_like(bins)
    for copy in tables:
        copy.wait()
    for h in range(heads):
        x = q_s[:, h * HD : (h + 1) * HD]
        turned = (x * cos_q[...] + pltpu.roll(x, HD // 2, 1) * sin_q[...]).astype(jnp.bfloat16)
        q_rot[h] = turned
        q_t[h] = turned.T

    def body(b, masked):
        base = pl.multiple_of(b * BLOCK, BLOCK)
        k = keys[pl.ds(base, BLOCK), :]
        if masked:
            seen = visible_block(base, BLOCK, own, early[...], rows)
        for h in range(heads):
            t = lax.dot_general(k, q_t[h], NN, preferred_element_type=jnp.float32)
            t = t * (SCALE * LOG2E)
            if masked:
                t = jnp.where(seen, t, NEG_BIG)
            old = peak_s[h : h + 1, :]
            new = jnp.maximum(old, jnp.max(t, axis=0, keepdims=True))
            fresh = jnp.sum(jnp.exp2(t - new), axis=0, keepdims=True)
            mass_s[h : h + 1, :] = mass_s[h : h + 1, :] * jnp.exp2(old - new) + fresh
            peak_s[h : h + 1, :] = new

    over_blocks(own, info, rows, body)
    log_total[...] = peak_s[...] + jnp.log(mass_s[...]) * LOG2E


def grad_kernel(
    heads, rows, levels,
    info, q_rot_0, q_t_0, log_total_0, q_rot_1, q_t_1, log_total_1, early, cot, cot_t, init,
    keys_k, cos_f, sin_f, codes_f, v_own, v_x, v_y1, v_y2, v_y3, v_core,
    out, bins, probs_s, out_s, delta_s, acc_s, values, keys, cos_k, sin_k, codes, sems,
):
    me = token_rank()
    own, first = me * rows, info[0]
    part = heads // 2
    q_rot = [q_rot_0.at[h] for h in range(part)] + [q_rot_1.at[h] for h in range(part)]
    q_t = [q_t_0.at[h] for h in range(part)] + [q_t_1.at[h] for h in range(part)]
    log_total = [ref.at[h : h + 1, :] for ref in (log_total_0, log_total_1) for h in range(part)]
    copies = [pltpu.make_async_copy(keys_k, keys, sems.at[0])]
    for j, (bits, ref, at) in enumerate(slots((v_own, v_x, v_y1, v_y2, v_y3, v_core))):
        start = pl.multiple_of((me ^ bits) * rows, rows)
        copies.append(
            pltpu.make_async_copy(
                ref.at[at * rows : (at + 1) * rows, :], values.at[pl.ds(start, rows), :], sems.at[1 + j]
            )
        )
    late = [
        pltpu.make_async_copy(cos_f, cos_k, sems.at[17]),
        pltpu.make_async_copy(sin_f, sin_k, sems.at[18]),
        pltpu.make_async_copy(codes_f, codes, sems.at[19]),
    ]
    for copy in copies + late:
        copy.start()
    out_s[...] = jnp.zeros_like(out_s)
    for copy in copies:
        copy.wait()

    def forward(b, masked):
        base = pl.multiple_of(b * BLOCK, BLOCK)
        k = keys[pl.ds(base, BLOCK), :]
        v = values[pl.ds(base, BLOCK), :]
        if masked:
            seen = visible_block(base, BLOCK, own, early[...], rows)
        for h in range(heads):
            s = lax.dot_general(k, q_t[h][...], NN, preferred_element_type=jnp.float32)
            p = jnp.exp2(s * (SCALE * LOG2E) - log_total[h][...])
            if masked:
                p = jnp.where(seen, p, 0.0)
            probs_s[b - first, h] = p
            out_s[h] += lax.dot_general(
                p.astype(jnp.bfloat16), v, TN, preferred_element_type=jnp.float32
            )

    over_blocks(own, info, rows, forward)
    for h in range(heads):
        o = out_s[h].astype(jnp.bfloat16)
        out[:, h * HD : (h + 1) * HD] = o
        prod = cot[:, h * HD : (h + 1) * HD].astype(jnp.float32) * o.astype(jnp.float32)
        delta_s[h : h + 1, :] = jnp.sum(prod.T, axis=0, keepdims=True)
    acc_s[...] = jnp.zeros_like(acc_s)
    last = (own + rows + BLOCK - 1) // BLOCK
    for copy in late:
        copy.wait()

    @pl.loop(first, last)
    def _(b):
        base = pl.multiple_of(b * BLOCK, BLOCK)
        v = values[pl.ds(base, BLOCK), :]
        dk = jnp.zeros((BLOCK, HD), jnp.float32)
        for h in range(heads):
            dp = lax.dot_general(v, cot_t[h], NN, preferred_element_type=jnp.float32)
            ds = (probs_s[b - first, h] * (dp - delta_s[h : h + 1, :])).astype(jnp.bfloat16)
            dk = dk + lax.dot_general(ds, q_rot[h][...], NN, preferred_element_type=jnp.float32)
        dk = dk * SCALE
        g = dk * cos_k[pl.ds(base, BLOCK), :] - pltpu.roll(dk, HD // 2, 1) * sin_k[pl.ds(base, BLOCK), :]
        code = codes[pl.ds(base, BLOCK), :].astype(jnp.float32)
        for level in range(levels):
            chosen = jnp.where(code == level, g, 0.0)
            acc_s[level] += jnp.sum(chosen.reshape(BLOCK // 8, 8, HD), axis=0)

    bins[...] = init[...] + jnp.sum(acc_s[...], axis=1)


def anywhere():
    return pl.BlockSpec(memory_space=pl.ANY)


def vmem():
    return pl.BlockSpec(memory_space=pltpu.VMEM)


def smem():
    return pl.BlockSpec(memory_space=pltpu.SMEM)


def cost(flops, size):
    return pl.CostEstimate(flops=flops, bytes_accessed=size, transcendentals=0)


def shards(hidden, w_query, w_key, w_value, key_codes, codebook, positions, cotangent):
    rows, part = hidden.shape
    width = w_query.shape[1]
    heads = width // HD
    levels = codebook.shape[1]
    ranks = lax.axis_size("tokens")
    total = rows * ranks
    group = lax.axis_size("tensor")
    rank = lax.axis_index("tensor")
    me = lax.axis_index("tokens")
    own = me * rows
    bf16, f32 = jnp.bfloat16, jnp.float32

    cross = lambda x, d: lax.ppermute(x, "tokens", [(i, i ^ d) for i in range(ranks)])

    def everyone(x, first, second, third):
        x_side = first(cross(x, 2))
        pair = second(jnp.concatenate([x, x_side], axis=0))
        y_side = [cross(pair, 4 * y) for y in (1, 2, 3)]
        core = cross(third(jnp.concatenate([pair] + y_side, axis=0)), 1)
        return (x, x_side, *y_side, core)

    def after(*others):
        return lambda v: lax.optimization_barrier((v, others))[0]

    flip = [(i, i ^ 1) for i in range(group)]
    up = [(i, (i + 2) % group) for i in range(group)]
    down = [(i, (i - 2) % group) for i in range(group)]
    send = functools.partial(lax.ppermute, axis_name="tensor")
    n = part // 2
    low = send(hidden, perm=up)
    high = send(hidden, perm=down)
    other = send(hidden, perm=flip)
    places = positions[None, :]
    packed, early, info = pl.pallas_call(
        functools.partial(pack_kernel, rows),
        out_shape=(
            jax.ShapeDtypeStruct((rows + TAIL, HD), bf16),
            jax.ShapeDtypeStruct((1, rows), jnp.int32),
            jax.ShapeDtypeStruct((2,), jnp.int32),
        ),
        in_specs=[vmem()] * 2,
        out_specs=(vmem(), vmem(), smem()),
        name="pack",
    )(key_codes, places)
    book = codebook.T
    inverse = jnp.exp((jnp.arange(HD) % (HD // 2)).astype(f32) * (-2.0 * math.log(ROPE_BASE) / HD))

    mate = rank ^ 1
    turn = lambda x, by: (x + by) % group
    shard = [rank, turn(rank, -2), turn(rank, 2), mate]
    shard += [turn(rank, 4), turn(mate, -2), turn(mate, 2), turn(mate, 4)]
    place = jnp.stack(shard).astype(jnp.int32)

    y_side = [cross(packed, 4 * y) for y in (1, 2, 3)]
    column = jnp.concatenate([packed] + y_side, axis=0)
    x_side = cross(column, 2)
    low, high, other = after(column)((low, high, other))
    far_a = send(low[:, :n], perm=up)
    far_b = send(high[:, n:], perm=down)
    other_low = send(other, perm=up)
    other_high = send(other, perm=down)
    other_far_a = send(far_a, perm=flip)
    other_far_b = send(far_b, perm=flip)

    half = group // 2
    low, high, other = after(far_a, far_b)((low, high, other))
    q_sum, kv_sum = pl.pallas_call(
        functools.partial(project_kernel, half, part),
        out_shape=(jax.ShapeDtypeStruct((rows, width), f32), jax.ShapeDtypeStruct((rows, 2 * HD), f32)),
        in_specs=[smem()] + [anywhere()] * (3 + half),
        out_specs=(vmem(),) * 2,
        scratch_shapes=[
            pltpu.VMEM((half, rows, part), bf16),
            pltpu.VMEM((half, part, width), bf16),
            pltpu.VMEM((half, part, 2 * HD), bf16),
            pltpu.SemaphoreType.DMA((4 * half,)),
        ],
        compiler_params=pltpu.CompilerParams(vmem_limit_bytes=50 << 20),
        cost_estimate=cost(1 << 34, 0),
        name="project",
    )(place, w_query, w_key, w_value, hidden, low, high, other)
    core = cross(jnp.concatenate([column, x_side], axis=0), 1)
    packed = (packed, *y_side, x_side, core)

    rest = [far_a, far_b, other_low, other_high, other_far_a, other_far_b]
    value = pl.pallas_call(
        functools.partial(value_kernel, half, half, part),
        out_shape=jax.ShapeDtypeStruct((rows, HD), bf16),
        in_specs=[smem()] + [anywhere()] * (2 + len(rest)),
        out_specs=vmem(),
        scratch_shapes=[
            pltpu.VMEM((rows, half * part), bf16),
            pltpu.VMEM((half, part, HD), bf16),
            pltpu.VMEM((rows, HD), f32),
            pltpu.SemaphoreType.DMA((half + len(rest) + 1,)),
        ],
        compiler_params=pltpu.CompilerParams(vmem_limit_bytes=50 << 20),
        cost_estimate=cost(0, 0),
        name="value",
    )(place, w_value, kv_sum, *rest)

    keys, cos_k, sin_k, codes, cot_t = pl.pallas_call(
        functools.partial(prep_kernel, rows, ranks, levels, heads),
        out_shape=(
            jax.ShapeDtypeStruct((total, HD), bf16),
            jax.ShapeDtypeStruct((total, HD), f32),
            jax.ShapeDtypeStruct((total, HD), f32),
            jax.ShapeDtypeStruct((total, HD), bf16),
            jax.ShapeDtypeStruct((heads, HD, rows), bf16),
        ),
        in_specs=[vmem()] * 3 + [anywhere()] * 6,
        out_specs=(anywhere(),) * 4 + (vmem(),),
        scratch_shapes=[
            pltpu.VMEM((ranks * (rows + TAIL), HD), bf16),
            pltpu.VMEM((total, HD), bf16),
            pltpu.VMEM((total, HD), f32),
            pltpu.VMEM((total, HD), f32),
            pltpu.VMEM((total, HD), bf16),
            pltpu.SemaphoreType.DMA((ranks,)),
            pltpu.SemaphoreType.DMA((4,)),
        ],
        compiler_params=pltpu.CompilerParams(vmem_limit_bytes=14 << 20),
        cost_estimate=cost(1 << 32, 0),
        name="prep",
    )(after(value)(inverse[None, :]), book, cotangent, *packed)

    def log_totals(begin, count, place):
        return pl.pallas_call(
            functools.partial(
                stats_kernel, begin, count, rows, levels, levels / total, half, half, part
            ),
            out_shape=(
                jax.ShapeDtypeStruct((count, rows, HD), bf16),
                jax.ShapeDtypeStruct((count, HD, rows), bf16),
                jax.ShapeDtypeStruct((count, rows), f32),
                jax.ShapeDtypeStruct((levels, HD), f32),
            ),
            in_specs=[smem()] * 2 + [vmem()] * 3 + [anywhere()] * (7 + len(rest)),
            out_specs=(vmem(),) * 4,
            scratch_shapes=[pltpu.VMEM((count, rows), f32)] * 2
            + [pltpu.VMEM((rows, HD), f32)] * 2
            + [
                pltpu.VMEM((total, HD), bf16),
                pltpu.VMEM((rows, half * part), bf16),
                pltpu.VMEM((half, part, count * HD), bf16),
                pltpu.VMEM((half, part, HD), bf16),
                pltpu.VMEM((rows, count * HD), f32),
                pltpu.VMEM((rows, HD), f32),
                pltpu.SemaphoreType.DMA((len(rest),)),
                pltpu.SemaphoreType.DMA((2 * half,)),
                pltpu.SemaphoreType.DMA((5,)),
            ],
            compiler_params=pltpu.CompilerParams(vmem_limit_bytes=50 << 20),
            cost_estimate=cost(1 << 34, 0),
            name="stats",
        )(
            place, info, early, key_codes, book, cos_k, sin_k, keys,
            q_sum, kv_sum, w_query, w_key, *rest,
        )

    totals = []

    def second(pair):
        pair, ready = lax.optimization_barrier((pair, place))
        totals.extend(log_totals(0, heads // 2, ready))
        return pair

    values = everyone(value, after(keys), second, lambda v: after(totals[2])(v))
    q_rot_0, q_t_0, log_total_0, init = totals
    late, _ = lax.optimization_barrier((place, values[2:5]))
    q_rot_1, q_t_1, log_total_1, _ = log_totals(heads // 2, heads // 2, late)

    most = total // BLOCK
    attention_out, local = pl.pallas_call(
        functools.partial(grad_kernel, heads, rows, levels),
        out_shape=(
            jax.ShapeDtypeStruct((rows, width), bf16),
            jax.ShapeDtypeStruct((levels, HD), f32),
        ),
        in_specs=[smem()] + [vmem()] * 10 + [anywhere()] * 10,
        out_specs=(vmem(),) * 2,
        scratch_shapes=[
            pltpu.VMEM((min(most, 7), heads, BLOCK, rows), f32),
            pltpu.VMEM((heads, rows, HD), f32),
            pltpu.VMEM((heads, rows), f32),
            pltpu.VMEM((levels, 8, HD), f32),
            pltpu.VMEM((total, HD), bf16),
            pltpu.VMEM((total, HD), bf16),
            pltpu.VMEM((total, HD), f32),
            pltpu.VMEM((total, HD), f32),
            pltpu.VMEM((total, HD), bf16),
            pltpu.SemaphoreType.DMA((20,)),
        ],
        compiler_params=pltpu.CompilerParams(vmem_limit_bytes=44 << 20),
        cost_estimate=cost(8 * rows * width * total, 8 << 20),
        name="grad",
    )(
        info, q_rot_0, q_t_0, log_total_0, q_rot_1, q_t_1, log_total_1, early, cotangent, cot_t, init,
        keys, cos_k, sin_k, codes, *values,
    )
    for d in (1, 2, 4, 8):
        local = local + cross(local, d)
    return (attention_out, local.T)


def solution(mesh):
    placed = (
        P("tokens", "tensor"),
        P(None, "tensor"),
        P(None, "tensor"),
        P(None, "tensor"),
        P("tokens", "tensor"),
        P("tensor", None),
        P("tokens"),
        P("tokens", "tensor"),
    )
    return jax.shard_map(
        shards,
        mesh=mesh,
        in_specs=placed,
        out_specs=(P("tokens", "tensor"), P("tensor", None)),
        check_vma=False,
    )
```

```python
import functools
import math

import jax
import jax.numpy as jnp
from jax import lax
from jax.experimental import pallas as pl
from jax.experimental.pallas import tpu as pltpu
from jax.sharding import PartitionSpec as P

HD = 128
ROPE_BASE = 500000.0
NEG_BIG = -1e30
LOG2E = math.log2(math.e)
SCALE = 1.0 / math.sqrt(HD)
BLOCK = 512
NN = (((1,), (0,)), ((), ()))
TN = (((0,), (0,)), ((), ()))
TAIL = 16
PARTNER = 15


def sincos(angle):
    turns = jnp.floor(angle * (2.0 / math.pi) + 0.5)
    r = angle - turns * 1.5703125
    r = r - turns * 4.837512969970703125e-4
    r = r - turns * 7.54978995489188216e-8
    z = r * r
    s = ((-1.9515295891e-4 * z + 8.3321608736e-3) * z - 1.6666654611e-1) * z * r + r
    c = ((2.443315711809948e-5 * z - 1.388731625493765e-3) * z + 4.166664568298827e-2) * z * z
    c = c - 0.5 * z + 1.0
    quadrant = turns.astype(jnp.int32)
    odd = (quadrant & 1) == 1
    sine = jnp.where(odd, c, s)
    cosine = jnp.where(odd, s, c)
    sine = jnp.where((quadrant & 2) == 0, sine, -sine)
    cosine = jnp.where(((quadrant + 1) & 2) == 0, cosine, -cosine)
    return sine, cosine


def slots_y_first(pieces):
    own, y1, y2, y3, x, core = pieces
    found = [(0, own, 0), (4, y1, 0), (8, y2, 0), (12, y3, 0)]
    found += [(2 | 4 * j, x, j) for j in range(4)]
    return found + [(1 | (4 * j if j < 4 else 2 | 4 * (j - 4)), core, j) for j in range(8)]


def slots(pieces):
    own, x, y1, y2, y3, core = pieces
    found = [(0, own, 0), (2, x, 0)]
    for y, ref in ((1, y1), (2, y2), (3, y3)):
        found += [(4 * y, ref, 0), (4 * y + 2, ref, 1)]
    return found + [(2 * j + 1, core, j) for j in range(8)]


def token_rank():
    return lax.axis_index("tokens")


def pack_kernel(rows, key_codes, positions, packed):
    packed[:rows, :] = key_codes[...].astype(jnp.float32).astype(jnp.bfloat16)
    place = positions[...]
    high, low = place & ~63, place & 63
    wide = [x[:, j * HD : (j + 1) * HD] for x in (high, low) for j in range(rows // HD)]
    blank = jnp.zeros((TAIL - len(wide), HD), jnp.int32)
    tail = jnp.concatenate(wide + [blank], axis=0)
    packed[rows:, :] = tail.astype(jnp.float32).astype(jnp.bfloat16)


def prep_kernel(
    rows, ranks, levels, heads,
    inverse, book, cot, cot_b, p_own, p_y1, p_y2, p_y3, p_x, p_core,
    keys_f, cos_f, sin_f, codes_f, cot_t, early, info, packed_s, keys, cos_k, sin_k, codes, sems, out_sems,
):
    me = token_rank()
    tall = rows + TAIL
    copies = []
    for j, (bits, ref, at) in enumerate(slots_y_first((p_own, p_y1, p_y2, p_y3, p_x, p_core))):
        start = pl.multiple_of((me ^ bits) * tall, TAIL)
        copies.append(
            pltpu.make_async_copy(
                ref.at[at * tall : (at + 1) * tall, :], packed_s.at[pl.ds(start, tall), :], sems.at[j]
            )
        )
    for copy in copies:
        copy.start()
    side = rows // 2
    for h in range(heads):
        columns, lanes = slice(h * HD, (h + 1) * HD), slice(h % 2 * side, (h % 2 + 1) * side)
        cot_t[h // 2, :, lanes] = cot[:side, columns].T
        cot_t[heads // 2 + h // 2, :, lanes] = cot_b[:, columns].T
    for copy in copies:
        copy.wait()
    for j, start in enumerate(segments(side)):
        rank = me if j == 0 else me ^ PARTNER
        tail = packed_s[pl.ds(pl.multiple_of(rank * tall + rows, TAIL), TAIL), :].astype(jnp.float32)
        place = tail[j : j + 1, :] + tail[2 + j : 3 + j, :]
        index = start + lax.broadcasted_iota(jnp.int32, (1, side), 1)
        first = index.astype(jnp.float32) - place
        early[j : j + 1, :] = jnp.concatenate([first, first], axis=1).astype(jnp.int32)
        info[2 * j] = jnp.min(first).astype(jnp.int32) // BLOCK
        info[2 * j + 1] = jnp.max(first).astype(jnp.int32)
    eye = lax.broadcasted_iota(jnp.int32, (HD, HD), 0) == lax.broadcasted_iota(
        jnp.int32, (HD, HD), 1
    )
    left = lax.broadcasted_iota(jnp.int32, (HD, HD), 1) < HD // 2
    ones = jnp.ones((2 * HD, HD), jnp.bfloat16)
    sides = rows // HD
    outs = [(keys, keys_f), (cos_k, cos_f), (sin_k, sin_f), (codes, codes_f)]

    @pl.loop(0, ranks)
    def _(i):
        source = pl.multiple_of(i * tall, TAIL)
        tail = packed_s[pl.ds(source + rows, TAIL), :].astype(jnp.float32)
        places = []
        for part in range(sides):
            high = jnp.where(eye, tail[part : part + 1, :], 0.0)
            low = jnp.where(eye, tail[sides + part : sides + part + 1, :], 0.0)
            digits = jnp.concatenate([high, low], axis=1).astype(jnp.bfloat16)
            places.append(lax.dot_general(digits, ones, NN, preferred_element_type=jnp.float32))
        for part in range(0, sides, 2):
            sine, cosine = sincos(jnp.where(left, places[part], places[part + 1]) * inverse[...])
            sine_r, cosine_r = pltpu.roll(sine, HD // 2, 1), pltpu.roll(cosine, HD // 2, 1)
            tables = (
                (jnp.where(left, cosine, cosine_r), jnp.where(left, -sine, sine_r)),
                (jnp.where(left, cosine_r, cosine), jnp.where(left, -sine_r, sine)),
            )
            for side, (cosine, sine) in enumerate(tables):
                at = part + side
                target = pl.multiple_of(i * rows + at * HD, HD)
                cos_k[pl.ds(target, HD), :] = cosine
                sin_k[pl.ds(target, HD), :] = sine
                raw = packed_s[pl.ds(source + at * HD, HD), :]
                codes[pl.ds(target, HD), :] = raw
                code = raw.astype(jnp.float32).astype(jnp.int32)
                layer = [book[e : e + 1, :] for e in range(levels)]
                bit = 1
                while len(layer) > 1:
                    on = (code & bit) != 0
                    layer = [jnp.where(on, layer[j + 1], layer[j]) for j in range(0, len(layer), 2)]
                    bit *= 2
                deq = layer[0]
                turned = deq * cosine + pltpu.roll(deq, HD // 2, 1) * sine
                keys[pl.ds(target, HD), :] = turned.astype(jnp.bfloat16)
        block = pl.ds(pl.multiple_of(i * rows, rows), rows)
        for j, (ref, full) in enumerate(outs):
            pltpu.make_async_copy(ref.at[block, :], full.at[block, :], out_sems.at[j]).start()

    for j, (ref, full) in enumerate(outs):
        pltpu.make_async_copy(ref, full, out_sems.at[j]).wait()


def shard_rows(place, n, part):
    return pl.ds(pl.multiple_of(place[n] * part, part), part)


def fetch(pieces, x_s, part, sem):
    copies = []
    for j, piece in enumerate(pieces):
        side = piece.shape[0]
        target = x_s.at[j % 2 * side : (j % 2 + 1) * side, j // 2 * part : (j // 2 + 1) * part]
        copies.append(pltpu.make_async_copy(piece, target, sem(j)))
    return copies


def project_kernel(
    count, part, place, wq, wk, wv, *refs,
):
    pieces, (q_out, kv_out, x_s, wq_s, wkv_s, sems) = refs[: 2 * count], refs[2 * count :]
    loads = fetch(pieces, x_s, part, lambda j: sems.at[3 * count + j])
    copies = []
    for n in range(count):
        rows = shard_rows(place, n, part)
        copies.append([
            loads[2 * n],
            loads[2 * n + 1],
            pltpu.make_async_copy(wq.at[rows, :], wq_s.at[n], sems.at[3 * n]),
            pltpu.make_async_copy(wk.at[rows, :], wkv_s.at[n, :, :HD], sems.at[3 * n + 1]),
            pltpu.make_async_copy(wv.at[rows, :], wkv_s.at[n, :, HD:], sems.at[3 * n + 2]),
        ])
        for copy in copies[-1]:
            copy.start()
    for n in range(count):
        for copy in copies[n]:
            copy.wait()
        x = x_s[:, n * part : (n + 1) * part]
        q = jnp.dot(x, wq_s[n], preferred_element_type=jnp.float32)
        kv = jnp.dot(x, wkv_s[n], preferred_element_type=jnp.float32)
        q_out[...] = q if n == 0 else q_out[...] + q
        kv_out[...] = kv if n == 0 else kv_out[...] + kv


def value_kernel(first, count, part, place, w, before, *refs):
    pieces, (value, x_s, w_s, before_s, sems) = refs[:-5], refs[-5:]
    copies = fetch(pieces, x_s, part, lambda j: sems.at[j])
    copies.append(pltpu.make_async_copy(before.at[:, HD:], before_s, sems.at[len(copies)]))
    for n in range(count):
        copies.append(
            pltpu.make_async_copy(w.at[shard_rows(place, first + n, part), :], w_s.at[n], sems.at[len(copies)])
        )
    for copy in copies:
        copy.start()
    for copy in copies:
        copy.wait()
    total = before_s[...]
    for n in range(count):
        total += jnp.dot(x_s[:, n * part : (n + 1) * part], w_s[n], preferred_element_type=jnp.float32)
    value[...] = total.astype(jnp.bfloat16)


def visible_block(base, block, own, earliest, side):
    key = base + lax.broadcasted_iota(jnp.int32, (block, 2 * side), 0)
    query = own + lax.broadcasted_iota(jnp.int32, (block, 2 * side), 1) % side
    return (key <= query) & (key >= earliest)


def segments(side):
    me = token_rank()
    return (2 * side * me, 2 * side * (me ^ PARTNER) + side)


def over_blocks(own, first, edge, side, body):
    last = (own + side + BLOCK - 1) // BLOCK

    @pl.loop(first, last)
    def _(b):
        masked = (b * BLOCK < edge) | (b * BLOCK + BLOCK > own)

        @pl.when(masked)
        def _():
            body(b, True)

        @pl.when(jnp.logical_not(masked))
        def _():
            body(b, False)


def stats_kernel(
    begin, heads, rows, levels, weight, first, count, part,
    place, info, early, book, cos_k, sin_k, codes_f, keys_k, q_before, kv_before, wq, wk, *refs,
):
    pieces = refs[:-18]
    (
        q_rot, q_t, log_total, bins,
        peak_s, mass_s, cos_q, sin_q, codes, keys, x_s, wq_s, wk_s, q_s, true_s, x_sems, w_sems, sems,
    ) = refs[-18:]
    side = rows // 2
    columns = pl.ds(begin * HD, heads * HD)
    loads = fetch(pieces, x_s, part, lambda j: x_sems.at[j])
    weights = []
    for n in range(count):
        at = shard_rows(place, first + n, part)
        row = [pltpu.make_async_copy(wq.at[at, columns], wq_s.at[n], w_sems.at[2 * n])]
        if begin == 0:
            row.append(pltpu.make_async_copy(wk.at[at, :], wk_s.at[n], w_sems.at[2 * n + 1]))
        weights.append(row)
    before = [pltpu.make_async_copy(q_before.at[:, columns], q_s, sems.at[0])]
    if begin == 0:
        before.append(pltpu.make_async_copy(kv_before.at[:, :HD], true_s, sems.at[1]))
    tables = [pltpu.make_async_copy(keys_k, keys, sems.at[2])]
    for j, start in enumerate(segments(side)):
        source = pl.ds(pl.multiple_of(start, side), side)
        target = slice(j * side, (j + 1) * side)
        for i, (full, ref) in enumerate(((cos_k, cos_q), (sin_k, sin_q), (codes_f, codes))):
            tables.append(
                pltpu.make_async_copy(full.at[source, :], ref.at[target, :], sems.at[3 + 3 * j + i])
            )
    for copy in before + loads + sum(weights, []) + tables:
        copy.start()
    peak_s[...] = jnp.full_like(peak_s, NEG_BIG)
    mass_s[...] = jnp.zeros_like(mass_s)
    for copy in before + loads:
        copy.wait()
    for n in range(count):
        for copy in weights[n]:
            copy.wait()
        x = x_s[:, n * part : (n + 1) * part]
        q_s[...] += jnp.dot(x, wq_s[n], preferred_element_type=jnp.float32)
        if begin == 0:
            true_s[...] += jnp.dot(x, wk_s[n], preferred_element_type=jnp.float32)
    for copy in tables:
        copy.wait()
    if begin == 0:
        code = codes[...].astype(jnp.float32)
        for level in range(levels):
            entry = weight * (book[level : level + 1, :] - true_s[...])
            bins[level : level + 1, :] = jnp.sum(
                jnp.where(code == level, entry, 0.0), axis=0, keepdims=True
            )
    else:
        bins[...] = jnp.zeros_like(bins)
    pairs = heads // 2
    for h in range(heads):
        x = q_s[:, h * HD : (h + 1) * HD]
        turned = (x * cos_q[...] + pltpu.roll(x, HD // 2, 1) * sin_q[...]).astype(jnp.bfloat16)
        lanes = slice(h % 2 * side, (h % 2 + 1) * side)
        for j in range(2):
            piece = turned[j * side : (j + 1) * side, :]
            q_rot[j * pairs + h // 2, lanes, :] = piece
            q_t[j * pairs + h // 2, :, lanes] = piece.T

    for j, own in enumerate(segments(side)):
        def body(b, masked):
            base = pl.multiple_of(b * BLOCK, BLOCK)
            k = keys[pl.ds(base, BLOCK), :]
            if masked:
                seen = visible_block(base, BLOCK, own, early[j : j + 1, :], side)
            for tile in range(j * pairs, (j + 1) * pairs):
                t = lax.dot_general(k, q_t[tile], NN, preferred_element_type=jnp.float32)
                t = t * (SCALE * LOG2E)
                if masked:
                    t = jnp.where(seen, t, NEG_BIG)
                old = peak_s[tile : tile + 1, :]
                new = jnp.maximum(old, jnp.max(t, axis=0, keepdims=True))
                fresh = jnp.sum(jnp.exp2(t - new), axis=0, keepdims=True)
                mass_s[tile : tile + 1, :] = mass_s[tile : tile + 1, :] * jnp.exp2(old - new) + fresh
                peak_s[tile : tile + 1, :] = new

        over_blocks(own, info[2 * j], info[2 * j + 1], side, body)

    log_total[...] = peak_s[...] + jnp.log(mass_s[...]) * LOG2E


def grad_kernel(
    heads, rows, levels,
    info, q_rot_0, q_t_0, log_total_0, q_rot_1, q_t_1, log_total_1, early, cot, cot_b, cot_t, init,
    keys_k, cos_f, sin_f, codes_f, v_own, v_x, v_y1, v_y2, v_y3, v_core,
    out, out_b, bins, probs_s, out_s, delta_s, acc_s, values, keys, cos_k, sin_k, codes, sems,
):
    me = token_rank()
    side, pairs = rows // 2, heads // 2
    part = pairs // 2

    def tiles(ref_0, ref_1):
        return [
            [(ref_0, ref_1)[p // part].at[j * part + p % part] for p in range(pairs)] for j in range(2)
        ]

    q_rot, q_t = tiles(q_rot_0, q_rot_1), tiles(q_t_0, q_t_1)
    log_total = [
        [(log_total_0, log_total_1)[p // part].at[pl.ds(j * part + p % part, 1), :] for p in range(pairs)]
        for j in range(2)
    ]
    copies = [pltpu.make_async_copy(keys_k, keys, sems.at[0])]
    for i, (bits, ref, at) in enumerate(slots((v_own, v_x, v_y1, v_y2, v_y3, v_core))):
        rank = me ^ bits
        for j, start in enumerate((rank * rows, (rank ^ PARTNER) * rows + side)):
            source = slice(at * rows + j * side, at * rows + (j + 1) * side)
            target = pl.ds(pl.multiple_of(start, side), side)
            copies.append(
                pltpu.make_async_copy(
                    ref.at[source, :], values.at[target, :], sems.at[1 + 2 * i + j]
                )
            )
    late = [
        pltpu.make_async_copy(cos_f, cos_k, sems.at[33]),
        pltpu.make_async_copy(sin_f, sin_k, sems.at[34]),
        pltpu.make_async_copy(codes_f, codes, sems.at[35]),
    ]
    for copy in copies + late:
        copy.start()
    acc_s[...] = jnp.zeros_like(acc_s)
    out_s[...] = jnp.zeros_like(out_s)
    for copy in copies:
        copy.wait()

    for j, own in enumerate(segments(side)):
        first, edge = info[2 * j], info[2 * j + 1]

        def forward(b, masked):
            base = pl.multiple_of(b * BLOCK, BLOCK)
            k = keys[pl.ds(base, BLOCK), :]
            v = values[pl.ds(base, BLOCK), :]
            if masked:
                seen = visible_block(base, BLOCK, own, early[j : j + 1, :], side)
            for p in range(pairs):
                s = lax.dot_general(k, q_t[j][p][...], NN, preferred_element_type=jnp.float32)
                w = jnp.exp2(s * (SCALE * LOG2E) - log_total[j][p][...])
                if masked:
                    w = jnp.where(seen, w, 0.0)
                probs_s[b - first, p] = w
                out_s[j * pairs + p] += lax.dot_general(
                    w.astype(jnp.bfloat16), v, TN, preferred_element_type=jnp.float32
                )

        over_blocks(own, first, edge, side, forward)
        for h in range(heads):
            columns = slice(h * HD, (h + 1) * HD)
            lanes = slice(h % 2 * side, (h % 2 + 1) * side)
            o = out_s[j * pairs + h // 2, lanes, :].astype(jnp.bfloat16)
            if j == 0:
                out[:, columns] = o
                grad = cot[:side, columns]
            else:
                out_b[:, columns] = o
                grad = cot_b[:, columns]
            prod = grad.astype(jnp.float32) * o.astype(jnp.float32)
            delta_s[h // 2 : h // 2 + 1, lanes] = jnp.sum(prod.T, axis=0, keepdims=True)
        if j == 0:
            for copy in late:
                copy.wait()

        @pl.loop(first, (own + side + BLOCK - 1) // BLOCK)
        def _(b):
            base = pl.multiple_of(b * BLOCK, BLOCK)
            v = values[pl.ds(base, BLOCK), :]
            dk = jnp.zeros((BLOCK, HD), jnp.float32)
            for p in range(pairs):
                dp = lax.dot_general(v, cot_t[j * pairs + p], NN, preferred_element_type=jnp.float32)
                ds = (probs_s[b - first, p] * (dp - delta_s[p : p + 1, :])).astype(jnp.bfloat16)
                dk = dk + lax.dot_general(ds, q_rot[j][p][...], NN, preferred_element_type=jnp.float32)
            dk = dk * SCALE
            g = dk * cos_k[pl.ds(base, BLOCK), :] - pltpu.roll(dk, HD // 2, 1) * sin_k[pl.ds(base, BLOCK), :]
            code = codes[pl.ds(base, BLOCK), :].astype(jnp.float32)
            for level in range(levels):
                chosen = jnp.where(code == level, g, 0.0)
                acc_s[level] += jnp.sum(chosen.reshape(BLOCK // 8, 8, HD), axis=0)

    bins[...] = init[...] + jnp.sum(acc_s[...], axis=1)


def anywhere():
    return pl.BlockSpec(memory_space=pl.ANY)


def vmem():
    return pl.BlockSpec(memory_space=pltpu.VMEM)


def smem():
    return pl.BlockSpec(memory_space=pltpu.SMEM)


def cost(flops, size):
    return pl.CostEstimate(flops=flops, bytes_accessed=size, transcendentals=0)


def shards(hidden, w_query, w_key, w_value, key_codes, codebook, positions, cotangent):
    rows, part = hidden.shape
    width = w_query.shape[1]
    heads = width // HD
    levels = codebook.shape[1]
    ranks = lax.axis_size("tokens")
    total = rows * ranks
    group = lax.axis_size("tensor")
    rank = lax.axis_index("tensor")
    me = lax.axis_index("tokens")
    own = me * rows
    bf16, f32 = jnp.bfloat16, jnp.float32

    cross = lambda x, d: lax.ppermute(x, "tokens", [(i, i ^ d) for i in range(ranks)])

    def everyone(x, first, second, third):
        x_side = first(cross(x, 2))
        pair = second(jnp.concatenate([x, x_side], axis=0))
        y_side = [cross(pair, 4 * y) for y in (1, 2, 3)]
        core = cross(third(jnp.concatenate([pair] + y_side, axis=0)), 1)
        return (x, x_side, *y_side, core)

    def after(*others):
        return lambda v: lax.optimization_barrier((v, others))[0]

    flip = [(i, i ^ 1) for i in range(group)]
    up = [(i, (i + 2) % group) for i in range(group)]
    down = [(i, (i - 2) % group) for i in range(group)]
    send = functools.partial(lax.ppermute, axis_name="tensor")
    side = rows // 2
    upper, lower, key_codes = lax.optimization_barrier((hidden[:side], hidden[side:], key_codes))
    hidden_b = cross(lower, PARTNER)
    mine = (upper, hidden_b)
    low_a, high_a, other_a = (send(mine[0], perm=perm) for perm in (up, down, flip))
    low_b, high_b, other_b = (send(mine[1], perm=perm) for perm in (up, down, flip))
    cot_b = cross(cotangent[side:], PARTNER)
    places = positions[None, :]
    packed = pl.pallas_call(
        functools.partial(pack_kernel, rows),
        out_shape=jax.ShapeDtypeStruct((rows + TAIL, HD), bf16),
        in_specs=[vmem()] * 2,
        out_specs=vmem(),
        name="pack",
    )(key_codes, places)
    book = codebook.T
    inverse = jnp.exp((jnp.arange(HD) % (HD // 2)).astype(f32) * (-2.0 * math.log(ROPE_BASE) / HD))

    mate = rank ^ 1
    turn = lambda x, by: (x + by) % group
    shard = [rank, turn(rank, -2), turn(rank, 2), mate]
    shard += [turn(rank, 4), turn(mate, -2), turn(mate, 2), turn(mate, 4)]
    place = jnp.stack(shard).astype(jnp.int32)

    packed = after(low_a, high_a, other_a)(packed)
    y_side = [cross(packed, 4 * y) for y in (1, 2, 3)]
    column = jnp.concatenate([packed] + y_side, axis=0)
    x_side = cross(column, 2)
    low_a, high_a, other_a = lax.optimization_barrier((low_a, high_a, other_a))
    far_a = send(low_a, perm=up)
    other_low_a = send(other_a, perm=up)
    other_high_a = send(other_a, perm=down)
    low_b, high_b, other_b = after(column)((low_b, high_b, other_b))
    far_b = send(high_b, perm=down)
    other_low_b = send(other_b, perm=up)
    other_high_b = send(other_b, perm=down)
    other_far_a = send(far_a, perm=flip)
    other_far_b = send(far_b, perm=flip)
    half = group // 2
    other_b = after(far_b)(other_b)
    q_sum, kv_sum = pl.pallas_call(
        functools.partial(project_kernel, half, part),
        out_shape=(jax.ShapeDtypeStruct((rows, width), f32), jax.ShapeDtypeStruct((rows, 2 * HD), f32)),
        in_specs=[smem()] + [anywhere()] * (3 + 2 * half),
        out_specs=(vmem(),) * 2,
        scratch_shapes=[
            pltpu.VMEM((rows, half * part), bf16),
            pltpu.VMEM((half, part, width), bf16),
            pltpu.VMEM((half, part, 2 * HD), bf16),
            pltpu.SemaphoreType.DMA((5 * half,)),
        ],
        compiler_params=pltpu.CompilerParams(vmem_limit_bytes=50 << 20),
        cost_estimate=cost(1 << 34, 0),
        name="project",
    )(place, w_query, w_key, w_value, *mine, low_a, low_b, high_a, high_b, other_a, other_b)
    core = cross(jnp.concatenate([column, x_side], axis=0), 1)
    packed = (packed, *y_side, x_side, core)

    rest = [far_a, far_b, other_low_a, other_low_b, other_high_a, other_high_b, other_far_a, other_far_b]
    value = pl.pallas_call(
        functools.partial(value_kernel, half, half, part),
        out_shape=jax.ShapeDtypeStruct((rows, HD), bf16),
        in_specs=[smem()] + [anywhere()] * (2 + len(rest)),
        out_specs=vmem(),
        scratch_shapes=[
            pltpu.VMEM((rows, half * part), bf16),
            pltpu.VMEM((half, part, HD), bf16),
            pltpu.VMEM((rows, HD), f32),
            pltpu.SemaphoreType.DMA((half + len(rest) + 1,)),
        ],
        compiler_params=pltpu.CompilerParams(vmem_limit_bytes=50 << 20),
        cost_estimate=cost(0, 0),
        name="value",
    )(place, w_value, kv_sum, *rest)

    keys, cos_k, sin_k, codes, cot_t, early, info = pl.pallas_call(
        functools.partial(prep_kernel, rows, ranks, levels, heads),
        out_shape=(
            jax.ShapeDtypeStruct((total, HD), bf16),
            jax.ShapeDtypeStruct((total, HD), f32),
            jax.ShapeDtypeStruct((total, HD), f32),
            jax.ShapeDtypeStruct((total, HD), bf16),
            jax.ShapeDtypeStruct((heads, HD, rows), bf16),
            jax.ShapeDtypeStruct((2, rows), jnp.int32),
            jax.ShapeDtypeStruct((4,), jnp.int32),
        ),
        in_specs=[vmem()] * 4 + [anywhere()] * 6,
        out_specs=(anywhere(),) * 4 + (vmem(), vmem(), smem()),
        scratch_shapes=[
            pltpu.VMEM((ranks * (rows + TAIL), HD), bf16),
            pltpu.VMEM((total, HD), bf16),
            pltpu.VMEM((total, HD), f32),
            pltpu.VMEM((total, HD), f32),
            pltpu.VMEM((total, HD), bf16),
            pltpu.SemaphoreType.DMA((ranks,)),
            pltpu.SemaphoreType.DMA((4,)),
        ],
        compiler_params=pltpu.CompilerParams(vmem_limit_bytes=58 << 20),
        cost_estimate=cost(1 << 32, 0),
        name="prep",
    )(after(value)(inverse[None, :]), book, cotangent, cot_b, *packed)

    def log_totals(begin, count, place):
        return pl.pallas_call(
            functools.partial(
                stats_kernel, begin, count, rows, levels, levels / total, half, half, part
            ),
            out_shape=(
                jax.ShapeDtypeStruct((count, rows, HD), bf16),
                jax.ShapeDtypeStruct((count, HD, rows), bf16),
                jax.ShapeDtypeStruct((count, rows), f32),
                jax.ShapeDtypeStruct((levels, HD), f32),
            ),
            in_specs=[smem()] * 2 + [vmem()] * 2 + [anywhere()] * (8 + len(rest)),
            out_specs=(vmem(),) * 4,
            scratch_shapes=[pltpu.VMEM((count, rows), f32)] * 2
            + [pltpu.VMEM((rows, HD), f32)] * 2
            + [
                pltpu.VMEM((rows, HD), bf16),
                pltpu.VMEM((total, HD), bf16),
                pltpu.VMEM((rows, half * part), bf16),
                pltpu.VMEM((half, part, count * HD), bf16),
                pltpu.VMEM((half, part, HD), bf16),
                pltpu.VMEM((rows, count * HD), f32),
                pltpu.VMEM((rows, HD), f32),
                pltpu.SemaphoreType.DMA((len(rest),)),
                pltpu.SemaphoreType.DMA((2 * half,)),
                pltpu.SemaphoreType.DMA((9,)),
            ],
            compiler_params=pltpu.CompilerParams(vmem_limit_bytes=50 << 20),
            cost_estimate=cost(1 << 34, 0),
            name="stats",
        )(
            place, info, early, book, cos_k, sin_k, codes, keys,
            q_sum, kv_sum, w_query, w_key, *rest,
        )

    totals = []

    def second(pair):
        pair, ready = lax.optimization_barrier((pair, place))
        totals.extend(log_totals(0, heads // 2, ready))
        return pair

    values = everyone(value, after(keys), second, lambda v: after(totals[2])(v))
    q_rot_0, q_t_0, log_total_0, init = totals
    late, _ = lax.optimization_barrier((place, values[2:5]))
    q_rot_1, q_t_1, log_total_1, _ = log_totals(heads // 2, heads // 2, late)

    most = total // BLOCK
    out, out_b, local = pl.pallas_call(
        functools.partial(grad_kernel, heads, rows, levels),
        out_shape=(
            jax.ShapeDtypeStruct((side, width), bf16),
            jax.ShapeDtypeStruct((side, width), bf16),
            jax.ShapeDtypeStruct((levels, HD), f32),
        ),
        in_specs=[smem()] + [vmem()] * 11 + [anywhere()] * 10,
        out_specs=(vmem(),) * 3,
        scratch_shapes=[
            pltpu.VMEM((min(most, 7), heads // 2, BLOCK, rows), f32),
            pltpu.VMEM((heads, rows, HD), f32),
            pltpu.VMEM((heads // 2, rows), f32),
            pltpu.VMEM((levels, 8, HD), f32),
            pltpu.VMEM((total, HD), bf16),
            pltpu.VMEM((total, HD), bf16),
            pltpu.VMEM((total, HD), f32),
            pltpu.VMEM((total, HD), f32),
            pltpu.VMEM((total, HD), bf16),
            pltpu.SemaphoreType.DMA((36,)),
        ],
        compiler_params=pltpu.CompilerParams(vmem_limit_bytes=44 << 20),
        cost_estimate=cost(8 * rows * width * total, 8 << 20),
        name="grad",
    )(
        info, q_rot_0, q_t_0, log_total_0, q_rot_1, q_t_1, log_total_1, early, cotangent, cot_b, cot_t, init,
        keys, cos_k, sin_k, codes, *values,
    )
    back = cross(out_b, PARTNER)
    for d in (1, 2, 4, 8):
        local = local + cross(local, d)
    return (jnp.concatenate([out, back], axis=0), local.T)


def solution(mesh):
    placed = (
        P("tokens", "tensor"),
        P(None, "tensor"),
        P(None, "tensor"),
        P(None, "tensor"),
        P("tokens", "tensor"),
        P("tensor", None),
        P("tokens"),
        P("tokens", "tensor"),
    )
    return jax.shard_map(
        shards,
        mesh=mesh,
        in_specs=placed,
        out_specs=(P("tokens", "tensor"), P("tensor", None)),
        check_vma=False,
    )
```

```python
import functools
import math

import jax
import jax.numpy as jnp
from jax import lax
from jax.experimental import pallas as pl
from jax.experimental.pallas import tpu as pltpu
from jax.sharding import PartitionSpec as P

HD = 128
ROPE_BASE = 500000.0
NEG_BIG = -1e30
LOG2E = math.log2(math.e)
SCALE = 1.0 / math.sqrt(HD)
BLOCK = 512
NN = (((1,), (0,)), ((), ()))
TN = (((0,), (0,)), ((), ()))
TAIL = 16


def sincos(angle):
    turns = jnp.floor(angle * (2.0 / math.pi) + 0.5)
    r = angle - turns * 1.5703125
    r = r - turns * 4.837512969970703125e-4
    r = r - turns * 7.54978995489188216e-8
    z = r * r
    s = ((-1.9515295891e-4 * z + 8.3321608736e-3) * z - 1.6666654611e-1) * z * r + r
    c = ((2.443315711809948e-5 * z - 1.388731625493765e-3) * z + 4.166664568298827e-2) * z * z
    c = c - 0.5 * z + 1.0
    quadrant = turns.astype(jnp.int32)
    odd = (quadrant & 1) == 1
    sine = jnp.where(odd, c, s)
    cosine = jnp.where(odd, s, c)
    sine = jnp.where((quadrant & 2) == 0, sine, -sine)
    cosine = jnp.where(((quadrant + 1) & 2) == 0, cosine, -cosine)
    return sine, cosine


def slots(pieces):
    own, x, y1, y2, y3, core = pieces
    found = [(0, own, 0), (2, x, 0)]
    for y, ref in ((1, y1), (2, y2), (3, y3)):
        found += [(4 * y, ref, 0), (4 * y + 2, ref, 1)]
    return found + [(2 * j + 1, core, j) for j in range(8)]


def token_rank():
    return lax.axis_index("tokens")


def pack_kernel(rows, key_codes, positions, packed, early, info):
    packed[:rows, :] = key_codes[...].astype(jnp.float32).astype(jnp.bfloat16)
    place = positions[...]
    high, low = place & ~63, place & 63
    wide = [x[:, j * HD : (j + 1) * HD] for x in (high, low) for j in range(rows // HD)]
    blank = jnp.zeros((TAIL - len(wide), HD), jnp.int32)
    tail = jnp.concatenate(wide + [blank], axis=0)
    packed[rows:, :] = tail.astype(jnp.float32).astype(jnp.bfloat16)
    index = token_rank() * rows + lax.broadcasted_iota(jnp.int32, (1, rows), 1)
    first = index - place
    early[...] = first
    first = first.astype(jnp.float32)
    info[0] = jnp.min(first).astype(jnp.int32) // BLOCK
    info[1] = jnp.max(first).astype(jnp.int32)


def prep_kernel(
    near, rows, ranks, levels,
    inverse, book, *refs,
):
    pieces = refs[:5] if near else refs[:1]
    if near:
        cot, cot_t = refs[5], refs[10]
        for h in range(cot_t.shape[0]):
            cot_t[h] = cot[:, h * HD : (h + 1) * HD].T
        refs = refs[:10] + refs[11:]
    keys_f, cos_f, sin_f, codes_f, packed_s, keys, cos_k, sin_k, codes, sems, out_sems = refs[-11:]
    me = token_rank()
    tall = rows + TAIL
    if near:
        found = [(2 * j, ref, 0) for j, ref in enumerate(pieces[:4])]
        found += [(2 * j + 1, pieces[4], j) for j in range(4)]
    else:
        found = [(2 * j if j < 4 else 2 * (j - 4) + 1, pieces[0], j) for j in range(8)]
    copies = []
    for j, (bits, ref, at) in enumerate(found):
        start = pl.multiple_of(((me // 2) ^ bits) * tall, TAIL)
        copies.append(
            pltpu.make_async_copy(
                ref.at[at * tall : (at + 1) * tall, :], packed_s.at[pl.ds(start, tall), :], sems.at[j]
            )
        )
    for copy in copies:
        copy.start()
    for copy in copies:
        copy.wait()
    eye = lax.broadcasted_iota(jnp.int32, (HD, HD), 0) == lax.broadcasted_iota(
        jnp.int32, (HD, HD), 1
    )
    left = lax.broadcasted_iota(jnp.int32, (HD, HD), 1) < HD // 2
    ones = jnp.ones((2 * HD, HD), jnp.bfloat16)
    sides = rows // HD
    outs = [(keys, keys_f), (cos_k, cos_f), (sin_k, sin_f), (codes, codes_f)]

    @pl.loop(0, ranks)
    def _(i):
        source = pl.multiple_of(i * tall, TAIL)
        tail = packed_s[pl.ds(source + rows, TAIL), :].astype(jnp.float32)
        places = []
        for part in range(sides):
            high = jnp.where(eye, tail[part : part + 1, :], 0.0)
            low = jnp.where(eye, tail[sides + part : sides + part + 1, :], 0.0)
            digits = jnp.concatenate([high, low], axis=1).astype(jnp.bfloat16)
            places.append(lax.dot_general(digits, ones, NN, preferred_element_type=jnp.float32))
        for part in range(0, sides, 2):
            sine, cosine = sincos(jnp.where(left, places[part], places[part + 1]) * inverse[...])
            sine_r, cosine_r = pltpu.roll(sine, HD // 2, 1), pltpu.roll(cosine, HD // 2, 1)
            tables = (
                (jnp.where(left, cosine, cosine_r), jnp.where(left, -sine, sine_r)),
                (jnp.where(left, cosine_r, cosine), jnp.where(left, -sine_r, sine)),
            )
            for side, (cosine, sine) in enumerate(tables):
                at = part + side
                target = pl.ds(at * HD, HD)
                cos_k[i, target, :] = cosine
                sin_k[i, target, :] = sine
                raw = packed_s[pl.ds(source + at * HD, HD), :]
                codes[i, target, :] = raw
                code = raw.astype(jnp.float32).astype(jnp.int32)
                layer = [book[e : e + 1, :] for e in range(levels)]
                bit = 1
                while len(layer) > 1:
                    on = (code & bit) != 0
                    layer = [jnp.where(on, layer[j + 1], layer[j]) for j in range(0, len(layer), 2)]
                    bit *= 2
                deq = layer[0]
                turned = deq * cosine + pltpu.roll(deq, HD // 2, 1) * sine
                keys[i, target, :] = turned.astype(jnp.bfloat16)
        for j, (ref, full) in enumerate(outs):
            pltpu.make_async_copy(ref.at[i], full.at[i], out_sems.at[j]).start()

    for j, (ref, full) in enumerate(outs):
        pltpu.make_async_copy(ref, full, out_sems.at[j]).wait()


def shard_rows(place, n, part):
    return pl.ds(pl.multiple_of(place[n] * part, part), part)


def interleave(near, distant, ref, sem):
    core = token_rank() % 2
    return [
        pltpu.make_async_copy(half, ref.at[:, core ^ j], sem(j))
        for j, half in enumerate((near, distant))
    ]


def fetch(pieces, x_s, sem):
    copies, at = [], 0
    for piece in pieces:
        width = piece.shape[1]
        copies.append(pltpu.make_async_copy(piece, x_s.at[:, at : at + width], sem(len(copies))))
        at += width
    return copies


def project_kernel(
    count, part, place, wq, wk, wv, *refs,
):
    pieces, (q_out, kv_out, x_s, wq_s, wkv_s, sems) = refs[:count], refs[count:]
    copies = []
    for n, piece in enumerate(pieces):
        rows = shard_rows(place, n, part)
        copies.append([
            pltpu.make_async_copy(piece, x_s.at[n], sems.at[4 * n]),
            pltpu.make_async_copy(wq.at[rows, :], wq_s.at[n], sems.at[4 * n + 1]),
            pltpu.make_async_copy(wk.at[rows, :], wkv_s.at[n, :, :HD], sems.at[4 * n + 2]),
            pltpu.make_async_copy(wv.at[rows, :], wkv_s.at[n, :, HD:], sems.at[4 * n + 3]),
        ])
        for copy in copies[-1]:
            copy.start()
    for n in range(count):
        for copy in copies[n]:
            copy.wait()
        x = x_s[n]
        q = jnp.dot(x, wq_s[n], preferred_element_type=jnp.float32)
        kv = jnp.dot(x, wkv_s[n], preferred_element_type=jnp.float32)
        q_out[...] = q if n == 0 else q_out[...] + q
        kv_out[...] = kv if n == 0 else kv_out[...] + kv


def value_kernel(first, count, part, place, w, before, *refs):
    pieces, (value, x_s, w_s, before_s, sems) = refs[:-5], refs[-5:]
    copies = fetch(pieces, x_s, lambda j: sems.at[j])
    copies.append(pltpu.make_async_copy(before.at[:, HD:], before_s, sems.at[len(copies)]))
    for n in range(count):
        copies.append(
            pltpu.make_async_copy(w.at[shard_rows(place, first + n, part), :], w_s.at[n], sems.at[len(copies)])
        )
    for copy in copies:
        copy.start()
    for copy in copies:
        copy.wait()
    total = before_s[...]
    for n in range(count):
        total += jnp.dot(x_s[:, n * part : (n + 1) * part], w_s[n], preferred_element_type=jnp.float32)
    value[...] = total.astype(jnp.bfloat16)


def visible_block(base, block, own, earliest, rows):
    key = base + lax.broadcasted_iota(jnp.int32, (block, rows), 0)
    query = own + lax.broadcasted_iota(jnp.int32, (block, rows), 1)
    return (key <= query) & (key >= earliest)


def over_blocks(own, info, rows, body):
    first, edge = info[0], info[1]
    last = (own + rows + BLOCK - 1) // BLOCK

    @pl.loop(first, last)
    def _(b):
        masked = (b * BLOCK < edge) | (b * BLOCK + BLOCK > own)

        @pl.when(masked)
        def _():
            body(b, True)

        @pl.when(jnp.logical_not(masked))
        def _():
            body(b, False)


def stats_kernel(
    begin, heads, rows, levels, weight, first, count, part,
    place, info, early, codes, book, cos_k, sin_k, keys_n, keys_d, q_before, kv_before, wq, wk, *refs,
):
    pieces = refs[:-17]
    (
        q_rot, q_t, log_total, bins,
        peak_s, mass_s, cos_q, sin_q, keys, x_s, wq_s, wk_s, q_s, true_s, x_sems, w_sems, sems,
    ) = refs[-17:]
    own = token_rank() * rows
    mine = token_rank() // 2
    columns = pl.ds(begin * HD, heads * HD)
    loads = fetch(pieces, x_s, lambda j: x_sems.at[j])
    weights = []
    for n in range(count):
        at = shard_rows(place, first + n, part)
        row = [pltpu.make_async_copy(wq.at[at, columns], wq_s.at[n], w_sems.at[2 * n])]
        if begin == 0:
            row.append(pltpu.make_async_copy(wk.at[at, :], wk_s.at[n], w_sems.at[2 * n + 1]))
        weights.append(row)
    before = [pltpu.make_async_copy(q_before.at[:, columns], q_s, sems.at[0])]
    if begin == 0:
        before.append(pltpu.make_async_copy(kv_before.at[:, :HD], true_s, sems.at[1]))
    tables = [
        pltpu.make_async_copy(cos_k.at[mine], cos_q, sems.at[2]),
        pltpu.make_async_copy(sin_k.at[mine], sin_q, sems.at[3]),
    ] + interleave(keys_n, keys_d, keys, lambda j: sems.at[4 + j])
    for copy in before + loads + sum(weights, []) + tables:
        copy.start()
    peak_s[...] = jnp.full_like(peak_s, NEG_BIG)
    mass_s[...] = jnp.zeros_like(mass_s)
    for copy in before + loads:
        copy.wait()
    for n in range(count):
        for copy in weights[n]:
            copy.wait()
        x = x_s[:, n * part : (n + 1) * part]
        q_s[...] += jnp.dot(x, wq_s[n], preferred_element_type=jnp.float32)
        if begin == 0:
            true_s[...] += jnp.dot(x, wk_s[n], preferred_element_type=jnp.float32)
    if begin == 0:
        code = codes[...]
        for level in range(levels):
            entry = weight * (book[level : level + 1, :] - true_s[...])
            bins[level : level + 1, :] = jnp.sum(
                jnp.where(code == level, entry, 0.0), axis=0, keepdims=True
            )
    else:
        bins[...] = jnp.zeros_like(bins)
    for copy in tables:
        copy.wait()
    for h in range(heads):
        x = q_s[:, h * HD : (h + 1) * HD]
        turned = (x * cos_q[...] + pltpu.roll(x, HD // 2, 1) * sin_q[...]).astype(jnp.bfloat16)
        q_rot[h] = turned
        q_t[h] = turned.T

    def body(b, masked):
        base = pl.multiple_of(b * BLOCK, BLOCK)
        k = keys[b].reshape(BLOCK, HD)
        if masked:
            seen = visible_block(base, BLOCK, own, early[...], rows)
        for h in range(heads):
            t = lax.dot_general(k, q_t[h], NN, preferred_element_type=jnp.float32)
            t = t * (SCALE * LOG2E)
            if masked:
                t = jnp.where(seen, t, NEG_BIG)
            old = peak_s[h : h + 1, :]
            new = jnp.maximum(old, jnp.max(t, axis=0, keepdims=True))
            fresh = jnp.sum(jnp.exp2(t - new), axis=0, keepdims=True)
            mass_s[h : h + 1, :] = mass_s[h : h + 1, :] * jnp.exp2(old - new) + fresh
            peak_s[h : h + 1, :] = new

    over_blocks(own, info, rows, body)
    log_total[...] = peak_s[...] + jnp.log(mass_s[...]) * LOG2E


def grad_kernel(
    heads, rows, levels,
    info, q_rot_0, q_t_0, log_total_0, q_rot_1, q_t_1, log_total_1, early, cot, cot_t, init,
    keys_n, keys_d, cos_n, cos_d, sin_n, sin_d, codes_n, codes_d, v_own, v_x, v_y1, v_y2, v_y3, v_core,
    out, bins, probs_s, out_s, delta_s, acc_s, values, keys, cos_k, sin_k, codes, sems,
):
    me = token_rank()
    own, first = me * rows, info[0]
    part = heads // 2
    q_rot = [q_rot_0.at[h] for h in range(part)] + [q_rot_1.at[h] for h in range(part)]
    q_t = [q_t_0.at[h] for h in range(part)] + [q_t_1.at[h] for h in range(part)]
    log_total = [ref.at[h : h + 1, :] for ref in (log_total_0, log_total_1) for h in range(part)]
    copies = interleave(keys_n, keys_d, keys, lambda j: sems.at[16 + j])
    for j, (bits, ref, at) in enumerate(slots((v_own, v_x, v_y1, v_y2, v_y3, v_core))):
        start = pl.multiple_of((me ^ bits) * rows, rows)
        copies.append(
            pltpu.make_async_copy(
                ref.at[at * rows : (at + 1) * rows, :], values.at[pl.ds(start, rows), :], sems.at[j]
            )
        )
    late = interleave(cos_n, cos_d, cos_k, lambda j: sems.at[18 + j])
    late += interleave(sin_n, sin_d, sin_k, lambda j: sems.at[20 + j])
    late += interleave(codes_n, codes_d, codes, lambda j: sems.at[22 + j])
    for copy in copies + late:
        copy.start()
    out_s[...] = jnp.zeros_like(out_s)
    for copy in copies:
        copy.wait()

    def forward(b, masked):
        base = pl.multiple_of(b * BLOCK, BLOCK)
        k = keys[b].reshape(BLOCK, HD)
        v = values[pl.ds(base, BLOCK), :]
        if masked:
            seen = visible_block(base, BLOCK, own, early[...], rows)
        for h in range(heads):
            s = lax.dot_general(k, q_t[h][...], NN, preferred_element_type=jnp.float32)
            p = jnp.exp2(s * (SCALE * LOG2E) - log_total[h][...])
            if masked:
                p = jnp.where(seen, p, 0.0)
            probs_s[b - first, h] = p
            out_s[h] += lax.dot_general(
                p.astype(jnp.bfloat16), v, TN, preferred_element_type=jnp.float32
            )

    over_blocks(own, info, rows, forward)
    for h in range(heads):
        o = out_s[h].astype(jnp.bfloat16)
        out[:, h * HD : (h + 1) * HD] = o
        prod = cot[:, h * HD : (h + 1) * HD].astype(jnp.float32) * o.astype(jnp.float32)
        delta_s[h : h + 1, :] = jnp.sum(prod.T, axis=0, keepdims=True)
    acc_s[...] = jnp.zeros_like(acc_s)
    last = (own + rows + BLOCK - 1) // BLOCK
    for copy in late:
        copy.wait()

    @pl.loop(first, last)
    def _(b):
        base = pl.multiple_of(b * BLOCK, BLOCK)
        v = values[pl.ds(base, BLOCK), :]
        dk = jnp.zeros((BLOCK, HD), jnp.float32)
        for h in range(heads):
            dp = lax.dot_general(v, cot_t[h], NN, preferred_element_type=jnp.float32)
            ds = (probs_s[b - first, h] * (dp - delta_s[h : h + 1, :])).astype(jnp.bfloat16)
            dk = dk + lax.dot_general(ds, q_rot[h][...], NN, preferred_element_type=jnp.float32)
        dk = dk * SCALE
        cosine, sine = cos_k[b].reshape(BLOCK, HD), sin_k[b].reshape(BLOCK, HD)
        g = dk * cosine - pltpu.roll(dk, HD // 2, 1) * sine
        code = codes[b].reshape(BLOCK, HD).astype(jnp.float32)
        for level in range(levels):
            chosen = jnp.where(code == level, g, 0.0)
            acc_s[level] += jnp.sum(chosen.reshape(BLOCK // 8, 8, HD), axis=0)

    bins[...] = init[...] + jnp.sum(acc_s[...], axis=1)


def anywhere():
    return pl.BlockSpec(memory_space=pl.ANY)


def vmem():
    return pl.BlockSpec(memory_space=pltpu.VMEM)


def smem():
    return pl.BlockSpec(memory_space=pltpu.SMEM)


def cost(flops, size):
    return pl.CostEstimate(flops=flops, bytes_accessed=size, transcendentals=0)


def shards(hidden, w_query, w_key, w_value, key_codes, codebook, positions, cotangent):
    rows, part = hidden.shape
    width = w_query.shape[1]
    heads = width // HD
    levels = codebook.shape[1]
    ranks = lax.axis_size("tokens")
    total = rows * ranks
    group = lax.axis_size("tensor")
    rank = lax.axis_index("tensor")
    me = lax.axis_index("tokens")
    own = me * rows
    bf16, f32 = jnp.bfloat16, jnp.float32

    cross = lambda x, d: lax.ppermute(x, "tokens", [(i, i ^ d) for i in range(ranks)])

    def everyone(x, first, second, third):
        x_side = first(cross(x, 2))
        pair = second(jnp.concatenate([x, x_side], axis=0))
        y_side = [cross(pair, 4 * y) for y in (1, 2, 3)]
        core = cross(third(jnp.concatenate([pair] + y_side, axis=0)), 1)
        return (x, x_side, *y_side, core)

    def after(*others):
        return lambda v: lax.optimization_barrier((v, others))[0]

    flip = [(i, i ^ 1) for i in range(group)]
    up = [(i, (i + 2) % group) for i in range(group)]
    down = [(i, (i - 2) % group) for i in range(group)]
    send = functools.partial(lax.ppermute, axis_name="tensor")
    n = part // 2
    low = send(hidden, perm=up)
    high = send(hidden, perm=down)
    other = send(hidden, perm=flip)
    places = positions[None, :]
    packed, early, info = pl.pallas_call(
        functools.partial(pack_kernel, rows),
        out_shape=(
            jax.ShapeDtypeStruct((rows + TAIL, HD), bf16),
            jax.ShapeDtypeStruct((1, rows), jnp.int32),
            jax.ShapeDtypeStruct((2,), jnp.int32),
        ),
        in_specs=[vmem()] * 2,
        out_specs=(vmem(), vmem(), smem()),
        name="pack",
    )(key_codes, places)
    book = codebook.T
    inverse = jnp.exp((jnp.arange(HD) % (HD // 2)).astype(f32) * (-2.0 * math.log(ROPE_BASE) / HD))

    mate = rank ^ 1
    turn = lambda x, by: (x + by) % group
    shard = [rank, turn(rank, -2), turn(rank, 2), mate]
    shard += [turn(rank, 4), turn(mate, -2), turn(mate, 2), turn(mate, 4)]
    place = jnp.stack(shard).astype(jnp.int32)

    y_side = [cross(packed, 4 * y) for y in (1, 2, 3)]
    column = jnp.concatenate([packed] + y_side, axis=0)
    x_side = cross(column, 2)
    low, high, other = after(column)((low, high, other))
    far_a = send(low[:, :n], perm=up)
    far_b = send(high[:, n:], perm=down)
    other_low = send(other, perm=up)
    other_high = send(other, perm=down)
    other_far_a = send(far_a, perm=flip)
    other_far_b = send(far_b, perm=flip)

    half = group // 2
    low, high, other = after(far_a, far_b)((low, high, other))
    q_sum, kv_sum = pl.pallas_call(
        functools.partial(project_kernel, half, part),
        out_shape=(jax.ShapeDtypeStruct((rows, width), f32), jax.ShapeDtypeStruct((rows, 2 * HD), f32)),
        in_specs=[smem()] + [anywhere()] * (3 + half),
        out_specs=(vmem(),) * 2,
        scratch_shapes=[
            pltpu.VMEM((half, rows, part), bf16),
            pltpu.VMEM((half, part, width), bf16),
            pltpu.VMEM((half, part, 2 * HD), bf16),
            pltpu.SemaphoreType.DMA((4 * half,)),
        ],
        compiler_params=pltpu.CompilerParams(vmem_limit_bytes=50 << 20),
        cost_estimate=cost(1 << 34, 0),
        name="project",
    )(place, w_query, w_key, w_value, hidden, low, high, other)
    core = cross(jnp.concatenate([column, x_side], axis=0), 1)
    packed = (packed, *y_side, x_side, core)

    rest = [far_a, far_b, other_low, other_high, other_far_a, other_far_b]
    value = pl.pallas_call(
        functools.partial(value_kernel, half, half, part),
        out_shape=jax.ShapeDtypeStruct((rows, HD), bf16),
        in_specs=[smem()] + [anywhere()] * (2 + len(rest)),
        out_specs=vmem(),
        scratch_shapes=[
            pltpu.VMEM((rows, half * part), bf16),
            pltpu.VMEM((half, part, HD), bf16),
            pltpu.VMEM((rows, HD), f32),
            pltpu.SemaphoreType.DMA((half + len(rest) + 1,)),
        ],
        compiler_params=pltpu.CompilerParams(vmem_limit_bytes=50 << 20),
        cost_estimate=cost(0, 0),
        name="value",
    )(place, w_value, kv_sum, *rest)

    def prep(near, inverse, *pieces):
        few = ranks // 2
        shapes = [(few, rows, HD)] * 4
        kinds = [bf16, f32, f32, bf16]
        return pl.pallas_call(
            functools.partial(prep_kernel, near, rows, few, levels),
            out_shape=[jax.ShapeDtypeStruct(size, kind) for size, kind in zip(shapes, kinds)]
            + [jax.ShapeDtypeStruct((heads, HD, rows), bf16)] * near,
            in_specs=[vmem()] * 2 + [anywhere()] * (5 if near else 1) + [vmem()] * near,
            out_specs=[anywhere()] * 4 + [vmem()] * near,
            scratch_shapes=[pltpu.VMEM((few * (rows + TAIL), HD), bf16)]
            + [pltpu.VMEM(size, kind) for size, kind in zip(shapes, kinds)]
            + [pltpu.SemaphoreType.DMA((few,)), pltpu.SemaphoreType.DMA((4,))],
            compiler_params=pltpu.CompilerParams(vmem_limit_bytes=58 << 20),
            cost_estimate=cost(1 << 32, 0),
            name="prep",
        )(inverse, book, *pieces)

    *near, cot_t = prep(True, after(kv_sum)(inverse[None, :]), *packed[:5], cotangent)
    distant = prep(False, after(value)(inverse[None, :]), packed[5])
    keys = distant[0]

    def log_totals(begin, count, place):
        return pl.pallas_call(
            functools.partial(
                stats_kernel, begin, count, rows, levels, levels / total, half, half, part
            ),
            out_shape=(
                jax.ShapeDtypeStruct((count, rows, HD), bf16),
                jax.ShapeDtypeStruct((count, HD, rows), bf16),
                jax.ShapeDtypeStruct((count, rows), f32),
                jax.ShapeDtypeStruct((levels, HD), f32),
            ),
            in_specs=[smem()] * 2 + [vmem()] * 3 + [anywhere()] * (8 + len(rest)),
            out_specs=(vmem(),) * 4,
            scratch_shapes=[pltpu.VMEM((count, rows), f32)] * 2
            + [pltpu.VMEM((rows, HD), f32)] * 2
            + [
                pltpu.VMEM((ranks // 2, 2, rows, HD), bf16),
                pltpu.VMEM((rows, half * part), bf16),
                pltpu.VMEM((half, part, count * HD), bf16),
                pltpu.VMEM((half, part, HD), bf16),
                pltpu.VMEM((rows, count * HD), f32),
                pltpu.VMEM((rows, HD), f32),
                pltpu.SemaphoreType.DMA((len(rest),)),
                pltpu.SemaphoreType.DMA((2 * half,)),
                pltpu.SemaphoreType.DMA((6,)),
            ],
            compiler_params=pltpu.CompilerParams(vmem_limit_bytes=50 << 20),
            cost_estimate=cost(1 << 34, 0),
            name="stats",
        )(
            place, info, early, key_codes, book, near[1], near[2], near[0], distant[0],
            q_sum, kv_sum, w_query, w_key, *rest,
        )

    totals = []

    def second(pair):
        pair, ready = lax.optimization_barrier((pair, place))
        totals.extend(log_totals(0, heads // 2, ready))
        return pair

    values = everyone(value, after(keys), second, lambda v: after(totals[2])(v))
    q_rot_0, q_t_0, log_total_0, init = totals
    late, _ = lax.optimization_barrier((place, values[2:5]))
    q_rot_1, q_t_1, log_total_1, _ = log_totals(heads // 2, heads // 2, late)

    most = total // BLOCK
    attention_out, local = pl.pallas_call(
        functools.partial(grad_kernel, heads, rows, levels),
        out_shape=(
            jax.ShapeDtypeStruct((rows, width), bf16),
            jax.ShapeDtypeStruct((levels, HD), f32),
        ),
        in_specs=[smem()] + [vmem()] * 10 + [anywhere()] * 14,
        out_specs=(vmem(),) * 2,
        scratch_shapes=[
            pltpu.VMEM((min(most, 7), heads, BLOCK, rows), f32),
            pltpu.VMEM((heads, rows, HD), f32),
            pltpu.VMEM((heads, rows), f32),
            pltpu.VMEM((levels, 8, HD), f32),
            pltpu.VMEM((total, HD), bf16),
            pltpu.VMEM((ranks // 2, 2, rows, HD), bf16),
            pltpu.VMEM((ranks // 2, 2, rows, HD), f32),
            pltpu.VMEM((ranks // 2, 2, rows, HD), f32),
            pltpu.VMEM((ranks // 2, 2, rows, HD), bf16),
            pltpu.SemaphoreType.DMA((24,)),
        ],
        compiler_params=pltpu.CompilerParams(vmem_limit_bytes=44 << 20),
        cost_estimate=cost(8 * rows * width * total, 8 << 20),
        name="grad",
    )(
        info, q_rot_0, q_t_0, log_total_0, q_rot_1, q_t_1, log_total_1, early, cotangent, cot_t, init,
        *[table for both in zip(near, distant) for table in both], *values,
    )
    for d in (1, 2, 4, 12):
        local = local + cross(local, d)
    return (attention_out, local.T)


def solution(mesh):
    placed = (
        P("tokens", "tensor"),
        P(None, "tensor"),
        P(None, "tensor"),
        P(None, "tensor"),
        P("tokens", "tensor"),
        P("tensor", None),
        P("tokens"),
        P("tokens", "tensor"),
    )
    return jax.shard_map(
        shards,
        mesh=mesh,
        in_specs=placed,
        out_specs=(P("tokens", "tensor"), P("tensor", None)),
        check_vma=False,
    )
```

```python
import functools
import math

import jax
import jax.numpy as jnp
from jax import lax
from jax.experimental import pallas as pl
from jax.experimental.pallas import tpu as pltpu
from jax.sharding import PartitionSpec as P

HD = 128
ROPE_BASE = 500000.0
NEG_BIG = -1e30
LOG2E = math.log2(math.e)
SCALE = 1.0 / math.sqrt(HD)
BLOCK = 512
NN = (((1,), (0,)), ((), ()))
TN = (((0,), (0,)), ((), ()))
TAIL = 16


def sincos(angle):
    turns = jnp.floor(angle * (2.0 / math.pi) + 0.5)
    r = angle - turns * 1.5703125
    r = r - turns * 4.837512969970703125e-4
    r = r - turns * 7.54978995489188216e-8
    z = r * r
    s = ((-1.9515295891e-4 * z + 8.3321608736e-3) * z - 1.6666654611e-1) * z * r + r
    c = ((2.443315711809948e-5 * z - 1.388731625493765e-3) * z + 4.166664568298827e-2) * z * z
    c = c - 0.5 * z + 1.0
    quadrant = turns.astype(jnp.int32)
    odd = (quadrant & 1) == 1
    sine = jnp.where(odd, c, s)
    cosine = jnp.where(odd, s, c)
    sine = jnp.where((quadrant & 2) == 0, sine, -sine)
    cosine = jnp.where(((quadrant + 1) & 2) == 0, cosine, -cosine)
    return sine, cosine


def slots(pieces):
    own, x, y1, y2, y3, core = pieces
    found = [(0, own, 0), (2, x, 0)]
    for y, ref in ((1, y1), (2, y2), (3, y3)):
        found += [(4 * y, ref, 0), (4 * y + 2, ref, 1)]
    return found + [(2 * j + 1, core, j) for j in range(8)]


def token_rank():
    return lax.axis_index("tokens")


def pack_kernel(rows, key_codes, positions, packed, early, info):
    packed[:rows, :] = key_codes[...].astype(jnp.float32).astype(jnp.bfloat16)
    place = positions[...]
    high, low = place & ~63, place & 63
    wide = [x[:, j * HD : (j + 1) * HD] for x in (high, low) for j in range(rows // HD)]
    blank = jnp.zeros((TAIL - len(wide), HD), jnp.int32)
    tail = jnp.concatenate(wide + [blank], axis=0)
    packed[rows:, :] = tail.astype(jnp.float32).astype(jnp.bfloat16)
    index = token_rank() * rows + lax.broadcasted_iota(jnp.int32, (1, rows), 1)
    first = index - place
    early[...] = first
    first = first.astype(jnp.float32)
    info[0] = jnp.min(first).astype(jnp.int32) // BLOCK
    info[1] = jnp.max(first).astype(jnp.int32)


def prep_kernel(
    near, rows, ranks, levels,
    inverse, book, *refs,
):
    pieces = refs[:5] if near else refs[:1]
    if near:
        cot, cot_t = refs[5], refs[10]
        for h in range(cot_t.shape[0]):
            cot_t[h] = cot[:, h * HD : (h + 1) * HD].T
        refs = refs[:10] + refs[11:]
    keys_f, cos_f, sin_f, codes_f, packed_s, keys, cos_k, sin_k, codes, sems, out_sems = refs[-11:]
    me = token_rank()
    tall = rows + TAIL
    if near:
        found = [(2 * j, ref, 0) for j, ref in enumerate(pieces[:4])]
        found += [(2 * j + 1, pieces[4], j) for j in range(4)]
    else:
        found = [(2 * j if j < 4 else 2 * (j - 4) + 1, pieces[0], j) for j in range(8)]
    copies = []
    for j, (bits, ref, at) in enumerate(found):
        start = pl.multiple_of(((me // 2) ^ bits) * tall, TAIL)
        copies.append(
            pltpu.make_async_copy(
                ref.at[at * tall : (at + 1) * tall, :], packed_s.at[pl.ds(start, tall), :], sems.at[j]
            )
        )
    for copy in copies:
        copy.start()
    for copy in copies:
        copy.wait()
    eye = lax.broadcasted_iota(jnp.int32, (HD, HD), 0) == lax.broadcasted_iota(
        jnp.int32, (HD, HD), 1
    )
    left = lax.broadcasted_iota(jnp.int32, (HD, HD), 1) < HD // 2
    ones = jnp.ones((2 * HD, HD), jnp.bfloat16)
    sides = rows // HD
    outs = [(keys, keys_f), (cos_k, cos_f), (sin_k, sin_f), (codes, codes_f)]

    @pl.loop(0, ranks)
    def _(i):
        source = pl.multiple_of(i * tall, TAIL)
        tail = packed_s[pl.ds(source + rows, TAIL), :].astype(jnp.float32)
        places = []
        for part in range(sides):
            high = jnp.where(eye, tail[part : part + 1, :], 0.0)
            low = jnp.where(eye, tail[sides + part : sides + part + 1, :], 0.0)
            digits = jnp.concatenate([high, low], axis=1).astype(jnp.bfloat16)
            places.append(lax.dot_general(digits, ones, NN, preferred_element_type=jnp.float32))
        for part in range(0, sides, 2):
            sine, cosine = sincos(jnp.where(left, places[part], places[part + 1]) * inverse[...])
            sine_r, cosine_r = pltpu.roll(sine, HD // 2, 1), pltpu.roll(cosine, HD // 2, 1)
            tables = (
                (jnp.where(left, cosine, cosine_r), jnp.where(left, -sine, sine_r)),
                (jnp.where(left, cosine_r, cosine), jnp.where(left, -sine_r, sine)),
            )
            for side, (cosine, sine) in enumerate(tables):
                at = part + side
                target = pl.ds(at * HD, HD)
                cos_k[i, target, :] = cosine
                sin_k[i, target, :] = sine
                raw = packed_s[pl.ds(source + at * HD, HD), :]
                codes[i, target, :] = raw
                code = raw.astype(jnp.float32).astype(jnp.int32)
                layer = [book[e : e + 1, :] for e in range(levels)]
                bit = 1
                while len(layer) > 1:
                    on = (code & bit) != 0
                    layer = [jnp.where(on, layer[j + 1], layer[j]) for j in range(0, len(layer), 2)]
                    bit *= 2
                deq = layer[0]
                turned = deq * cosine + pltpu.roll(deq, HD // 2, 1) * sine
                keys[i, target, :] = turned.astype(jnp.bfloat16)
        for j, (ref, full) in enumerate(outs):
            pltpu.make_async_copy(ref.at[i], full.at[i], out_sems.at[j]).start()

    for j, (ref, full) in enumerate(outs):
        pltpu.make_async_copy(ref, full, out_sems.at[j]).wait()


def shard_rows(place, n, part):
    return pl.ds(pl.multiple_of(place[n] * part, part), part)


def interleave(near, distant, ref, sem):
    core = token_rank() % 2
    return [
        pltpu.make_async_copy(half, ref.at[:, core ^ j], sem(j))
        for j, half in enumerate((near, distant))
    ]


def fetch(pieces, x_s, sem):
    copies, at = [], 0
    for piece in pieces:
        width = piece.shape[1]
        copies.append(pltpu.make_async_copy(piece, x_s.at[:, at : at + width], sem(len(copies))))
        at += width
    return copies


def project_kernel(
    count, part, place, wq, wk, wv, *refs,
):
    pieces, (q_out, kv_out, x_s, wq_s, wkv_s, sems) = refs[:count], refs[count:]
    copies = []
    for n, piece in enumerate(pieces):
        rows = shard_rows(place, n, part)
        copies.append([
            pltpu.make_async_copy(piece, x_s.at[n], sems.at[4 * n]),
            pltpu.make_async_copy(wq.at[rows, :], wq_s.at[n], sems.at[4 * n + 1]),
            pltpu.make_async_copy(wk.at[rows, :], wkv_s.at[n, :, :HD], sems.at[4 * n + 2]),
            pltpu.make_async_copy(wv.at[rows, :], wkv_s.at[n, :, HD:], sems.at[4 * n + 3]),
        ])
        for copy in copies[-1]:
            copy.start()
    for n in range(count):
        for copy in copies[n]:
            copy.wait()
        x = x_s[n]
        q = jnp.dot(x, wq_s[n], preferred_element_type=jnp.float32)
        kv = jnp.dot(x, wkv_s[n], preferred_element_type=jnp.float32)
        q_out[...] = q if n == 0 else q_out[...] + q
        kv_out[...] = kv if n == 0 else kv_out[...] + kv


def value_kernel(first, count, part, place, w, before, *refs):
    pieces, (value, x_s, w_s, before_s, sems) = refs[:-5], refs[-5:]
    copies = fetch(pieces, x_s, lambda j: sems.at[j])
    copies.append(pltpu.make_async_copy(before.at[:, HD:], before_s, sems.at[len(copies)]))
    for n in range(count):
        copies.append(
            pltpu.make_async_copy(w.at[shard_rows(place, first + n, part), :], w_s.at[n], sems.at[len(copies)])
        )
    for copy in copies:
        copy.start()
    for copy in copies:
        copy.wait()
    total = before_s[...]
    for n in range(count):
        total += jnp.dot(x_s[:, n * part : (n + 1) * part], w_s[n], preferred_element_type=jnp.float32)
    value[...] = total.astype(jnp.bfloat16)


def visible_block(base, block, own, earliest, rows):
    key = base + lax.broadcasted_iota(jnp.int32, (block, rows), 0)
    query = own + lax.broadcasted_iota(jnp.int32, (block, rows), 1)
    return (key <= query) & (key >= earliest)


def over_blocks(own, info, rows, body):
    first, edge = info[0], info[1]
    last = (own + rows + BLOCK - 1) // BLOCK

    @pl.loop(first, last)
    def _(b):
        masked = (b * BLOCK < edge) | (b * BLOCK + BLOCK > own)

        @pl.when(masked)
        def _():
            body(b, True)

        @pl.when(jnp.logical_not(masked))
        def _():
            body(b, False)


def stats_kernel(
    begin, heads, rows, levels, weight, first, count, part,
    place, info, early, codes, book, cos_k, sin_k, keys_n, keys_d, q_before, kv_before, wq, wk, *refs,
):
    pieces = refs[:-17]
    (
        q_rot, q_t, log_total, bins,
        peak_s, mass_s, cos_q, sin_q, keys, x_s, wq_s, wk_s, q_s, true_s, x_sems, w_sems, sems,
    ) = refs[-17:]
    own = token_rank() * rows
    mine = token_rank() // 2
    columns = pl.ds(begin * HD, heads * HD)
    loads = fetch(pieces, x_s, lambda j: x_sems.at[j])
    weights = []
    for n in range(count):
        at = shard_rows(place, first + n, part)
        row = [pltpu.make_async_copy(wq.at[at, columns], wq_s.at[n], w_sems.at[2 * n])]
        if begin == 0:
            row.append(pltpu.make_async_copy(wk.at[at, :], wk_s.at[n], w_sems.at[2 * n + 1]))
        weights.append(row)
    before = [pltpu.make_async_copy(q_before.at[:, columns], q_s, sems.at[0])]
    if begin == 0:
        before.append(pltpu.make_async_copy(kv_before.at[:, :HD], true_s, sems.at[1]))
    tables = [
        pltpu.make_async_copy(cos_k.at[mine], cos_q, sems.at[2]),
        pltpu.make_async_copy(sin_k.at[mine], sin_q, sems.at[3]),
    ] + interleave(keys_n, keys_d, keys, lambda j: sems.at[4 + j])
    for copy in before + loads + sum(weights, []) + tables:
        copy.start()
    peak_s[...] = jnp.full_like(peak_s, NEG_BIG)
    mass_s[...] = jnp.zeros_like(mass_s)
    for copy in before + loads:
        copy.wait()
    for n in range(count):
        for copy in weights[n]:
            copy.wait()
        x = x_s[:, n * part : (n + 1) * part]
        q_s[...] += jnp.dot(x, wq_s[n], preferred_element_type=jnp.float32)
        if begin == 0:
            true_s[...] += jnp.dot(x, wk_s[n], preferred_element_type=jnp.float32)
    if begin == 0:
        code = codes[...]
        for level in range(levels):
            entry = weight * (book[level : level + 1, :] - true_s[...])
            bins[level : level + 1, :] = jnp.sum(
                jnp.where(code == level, entry, 0.0), axis=0, keepdims=True
            )
    else:
        bins[...] = jnp.zeros_like(bins)
    for copy in tables:
        copy.wait()
    for h in range(heads):
        x = q_s[:, h * HD : (h + 1) * HD]
        turned = (x * cos_q[...] + pltpu.roll(x, HD // 2, 1) * sin_q[...]).astype(jnp.bfloat16)
        q_rot[h] = turned
        q_t[h] = turned.T

    def body(b, masked):
        base = pl.multiple_of(b * BLOCK, BLOCK)
        k = keys[b].reshape(BLOCK, HD)
        if masked:
            seen = visible_block(base, BLOCK, own, early[...], rows)
        for h in range(heads):
            t = lax.dot_general(k, q_t[h], NN, preferred_element_type=jnp.float32)
            t = t * (SCALE * LOG2E)
            if masked:
                t = jnp.where(seen, t, NEG_BIG)
            old = peak_s[h : h + 1, :]
            new = jnp.maximum(old, jnp.max(t, axis=0, keepdims=True))
            fresh = jnp.sum(jnp.exp2(t - new), axis=0, keepdims=True)
            mass_s[h : h + 1, :] = mass_s[h : h + 1, :] * jnp.exp2(old - new) + fresh
            peak_s[h : h + 1, :] = new

    over_blocks(own, info, rows, body)
    log_total[...] = peak_s[...] + jnp.log(mass_s[...]) * LOG2E


def grad_kernel(
    heads, rows, levels,
    info, q_rot_0, q_t_0, log_total_0, q_rot_1, q_t_1, log_total_1, early, cot, cot_t, init,
    keys_n, keys_d, cos_n, cos_d, sin_n, sin_d, codes_n, codes_d, v_own, v_x, v_y1, v_y2, v_y3, v_core,
    out, bins, probs_s, out_s, delta_s, acc_s, values, keys, cos_k, sin_k, codes, sems,
):
    me = token_rank()
    own, first = me * rows, info[0]
    part = heads // 2
    q_rot = [q_rot_0.at[h] for h in range(part)] + [q_rot_1.at[h] for h in range(part)]
    q_t = [q_t_0.at[h] for h in range(part)] + [q_t_1.at[h] for h in range(part)]
    log_total = [ref.at[h : h + 1, :] for ref in (log_total_0, log_total_1) for h in range(part)]
    copies = interleave(keys_n, keys_d, keys, lambda j: sems.at[16 + j])
    for j, (bits, ref, at) in enumerate(slots((v_own, v_x, v_y1, v_y2, v_y3, v_core))):
        start = pl.multiple_of((me ^ bits) * rows, rows)
        copies.append(
            pltpu.make_async_copy(
                ref.at[at * rows : (at + 1) * rows, :], values.at[pl.ds(start, rows), :], sems.at[j]
            )
        )
    late = interleave(cos_n, cos_d, cos_k, lambda j: sems.at[18 + j])
    late += interleave(sin_n, sin_d, sin_k, lambda j: sems.at[20 + j])
    late += interleave(codes_n, codes_d, codes, lambda j: sems.at[22 + j])
    for copy in copies + late:
        copy.start()
    out_s[...] = jnp.zeros_like(out_s)
    for copy in copies:
        copy.wait()

    def forward(b, masked):
        base = pl.multiple_of(b * BLOCK, BLOCK)
        k = keys[b].reshape(BLOCK, HD)
        v = values[pl.ds(base, BLOCK), :]
        if masked:
            seen = visible_block(base, BLOCK, own, early[...], rows)
        for h in range(heads):
            s = lax.dot_general(k, q_t[h][...], NN, preferred_element_type=jnp.float32)
            p = jnp.exp2(s * (SCALE * LOG2E) - log_total[h][...])
            if masked:
                p = jnp.where(seen, p, 0.0)
            probs_s[b - first, h] = p
            out_s[h] += lax.dot_general(
                p.astype(jnp.bfloat16), v, TN, preferred_element_type=jnp.float32
            )

    over_blocks(own, info, rows, forward)
    for h in range(heads):
        o = out_s[h].astype(jnp.bfloat16)
        out[:, h * HD : (h + 1) * HD] = o
        prod = cot[:, h * HD : (h + 1) * HD].astype(jnp.float32) * o.astype(jnp.float32)
        delta_s[h : h + 1, :] = jnp.sum(prod.T, axis=0, keepdims=True)
    acc_s[...] = jnp.zeros_like(acc_s)
    last = (own + rows + BLOCK - 1) // BLOCK
    for copy in late:
        copy.wait()

    @pl.loop(first, last)
    def _(b):
        base = pl.multiple_of(b * BLOCK, BLOCK)
        v = values[pl.ds(base, BLOCK), :]
        dk = jnp.zeros((BLOCK, HD), jnp.float32)
        for h in range(heads):
            dp = lax.dot_general(v, cot_t[h], NN, preferred_element_type=jnp.float32)
            ds = (probs_s[b - first, h] * (dp - delta_s[h : h + 1, :])).astype(jnp.bfloat16)
            dk = dk + lax.dot_general(ds, q_rot[h][...], NN, preferred_element_type=jnp.float32)
        dk = dk * SCALE
        cosine, sine = cos_k[b].reshape(BLOCK, HD), sin_k[b].reshape(BLOCK, HD)
        g = dk * cosine - pltpu.roll(dk, HD // 2, 1) * sine
        code = codes[b].reshape(BLOCK, HD).astype(jnp.float32)
        for level in range(levels):
            chosen = jnp.where(code == level, g, 0.0)
            acc_s[level] += jnp.sum(chosen.reshape(BLOCK // 8, 8, HD), axis=0)

    bins[...] = init[...] + jnp.sum(acc_s[...], axis=1)


def anywhere():
    return pl.BlockSpec(memory_space=pl.ANY)


def vmem():
    return pl.BlockSpec(memory_space=pltpu.VMEM)


def smem():
    return pl.BlockSpec(memory_space=pltpu.SMEM)


def cost(flops, size):
    return pl.CostEstimate(flops=flops, bytes_accessed=size, transcendentals=0)


def shards(hidden, w_query, w_key, w_value, key_codes, codebook, positions, cotangent):
    rows, part = hidden.shape
    width = w_query.shape[1]
    heads = width // HD
    levels = codebook.shape[1]
    ranks = lax.axis_size("tokens")
    total = rows * ranks
    group = lax.axis_size("tensor")
    rank = lax.axis_index("tensor")
    me = lax.axis_index("tokens")
    own = me * rows
    bf16, f32 = jnp.bfloat16, jnp.float32

    cross = lambda x, d: lax.ppermute(x, "tokens", [(i, i ^ d) for i in range(ranks)])

    def everyone(x, first, second, third):
        x_side = first(cross(x, 2))
        pair = second(jnp.concatenate([x, x_side], axis=0))
        y_side = [cross(pair, 4 * y) for y in (1, 2, 3)]
        core = cross(third(jnp.concatenate([pair] + y_side, axis=0)), 1)
        return (x, x_side, *y_side, core)

    def after(*others):
        return lambda v: lax.optimization_barrier((v, others))[0]

    flip = [(i, i ^ 1) for i in range(group)]
    up = [(i, (i + 2) % group) for i in range(group)]
    down = [(i, (i - 2) % group) for i in range(group)]
    send = functools.partial(lax.ppermute, axis_name="tensor")
    n = part // 2
    low = send(hidden, perm=up)
    high = send(hidden, perm=down)
    other = send(hidden, perm=flip)
    places = positions[None, :]
    packed, early, info = pl.pallas_call(
        functools.partial(pack_kernel, rows),
        out_shape=(
            jax.ShapeDtypeStruct((rows + TAIL, HD), bf16),
            jax.ShapeDtypeStruct((1, rows), jnp.int32),
            jax.ShapeDtypeStruct((2,), jnp.int32),
        ),
        in_specs=[vmem()] * 2,
        out_specs=(vmem(), vmem(), smem()),
        name="pack",
    )(key_codes, places)
    book = codebook.T
    inverse = jnp.exp((jnp.arange(HD) % (HD // 2)).astype(f32) * (-2.0 * math.log(ROPE_BASE) / HD))

    mate = rank ^ 1
    turn = lambda x, by: (x + by) % group
    shard = [rank, turn(rank, -2), turn(rank, 2), mate]
    shard += [turn(rank, 4), turn(mate, -2), turn(mate, 2), turn(mate, 4)]
    place = jnp.stack(shard).astype(jnp.int32)

    y_side = [cross(packed, 4 * y) for y in (1, 2, 3)]
    column = jnp.concatenate([packed] + y_side, axis=0)
    x_side = cross(column, 2)
    low, high, other = after(column)((low, high, other))
    far_a = send(low[:, :n], perm=up)
    far_b = send(high[:, n:], perm=down)
    other_low = send(other, perm=up)
    other_high = send(other, perm=down)
    other_far_a = send(far_a, perm=flip)
    other_far_b = send(far_b, perm=flip)

    half = group // 2
    low, high, other = after(far_a, far_b)((low, high, other))
    q_sum, kv_sum = pl.pallas_call(
        functools.partial(project_kernel, half, part),
        out_shape=(jax.ShapeDtypeStruct((rows, width), f32), jax.ShapeDtypeStruct((rows, 2 * HD), f32)),
        in_specs=[smem()] + [anywhere()] * (3 + half),
        out_specs=(vmem(),) * 2,
        scratch_shapes=[
            pltpu.VMEM((half, rows, part), bf16),
            pltpu.VMEM((half, part, width), bf16),
            pltpu.VMEM((half, part, 2 * HD), bf16),
            pltpu.SemaphoreType.DMA((4 * half,)),
        ],
        compiler_params=pltpu.CompilerParams(vmem_limit_bytes=50 << 20),
        cost_estimate=cost(1 << 34, 0),
        name="project",
    )(place, w_query, w_key, w_value, hidden, low, high, other)
    core = cross(jnp.concatenate([column, x_side], axis=0), 1)
    packed = (packed, *y_side, x_side, core)

    rest = [far_a, far_b, other_low, other_high, other_far_a, other_far_b]
    value = pl.pallas_call(
        functools.partial(value_kernel, half, half, part),
        out_shape=jax.ShapeDtypeStruct((rows, HD), bf16),
        in_specs=[smem()] + [anywhere()] * (2 + len(rest)),
        out_specs=vmem(),
        scratch_shapes=[
            pltpu.VMEM((rows, half * part), bf16),
            pltpu.VMEM((half, part, HD), bf16),
            pltpu.VMEM((rows, HD), f32),
            pltpu.SemaphoreType.DMA((half + len(rest) + 1,)),
        ],
        compiler_params=pltpu.CompilerParams(vmem_limit_bytes=50 << 20),
        cost_estimate=cost(0, 0),
        name="value",
    )(place, w_value, kv_sum, *rest)

    def prep(near, inverse, *pieces):
        few = ranks // 2
        shapes = [(few, rows, HD)] * 4
        kinds = [bf16, f32, f32, bf16]
        return pl.pallas_call(
            functools.partial(prep_kernel, near, rows, few, levels),
            out_shape=[jax.ShapeDtypeStruct(size, kind) for size, kind in zip(shapes, kinds)]
            + [jax.ShapeDtypeStruct((heads, HD, rows), bf16)] * near,
            in_specs=[vmem()] * 2 + [anywhere()] * (5 if near else 1) + [vmem()] * near,
            out_specs=[anywhere()] * 4 + [vmem()] * near,
            scratch_shapes=[pltpu.VMEM((few * (rows + TAIL), HD), bf16)]
            + [pltpu.VMEM(size, kind) for size, kind in zip(shapes, kinds)]
            + [pltpu.SemaphoreType.DMA((few,)), pltpu.SemaphoreType.DMA((4,))],
            compiler_params=pltpu.CompilerParams(vmem_limit_bytes=58 << 20),
            cost_estimate=cost(0 if near else 1 << 32, 0),
            name="prep",
        )(inverse, book, *pieces)

    *near, cot_t = prep(True, after(kv_sum)(inverse[None, :]), *packed[:5], cotangent)
    distant = prep(False, after(value)(inverse[None, :]), packed[5])
    keys = distant[0]

    def log_totals(begin, count, place):
        return pl.pallas_call(
            functools.partial(
                stats_kernel, begin, count, rows, levels, levels / total, half, half, part
            ),
            out_shape=(
                jax.ShapeDtypeStruct((count, rows, HD), bf16),
                jax.ShapeDtypeStruct((count, HD, rows), bf16),
                jax.ShapeDtypeStruct((count, rows), f32),
                jax.ShapeDtypeStruct((levels, HD), f32),
            ),
            in_specs=[smem()] * 2 + [vmem()] * 3 + [anywhere()] * (8 + len(rest)),
            out_specs=(vmem(),) * 4,
            scratch_shapes=[pltpu.VMEM((count, rows), f32)] * 2
            + [pltpu.VMEM((rows, HD), f32)] * 2
            + [
                pltpu.VMEM((ranks // 2, 2, rows, HD), bf16),
                pltpu.VMEM((rows, half * part), bf16),
                pltpu.VMEM((half, part, count * HD), bf16),
                pltpu.VMEM((half, part, HD), bf16),
                pltpu.VMEM((rows, count * HD), f32),
                pltpu.VMEM((rows, HD), f32),
                pltpu.SemaphoreType.DMA((len(rest),)),
                pltpu.SemaphoreType.DMA((2 * half,)),
                pltpu.SemaphoreType.DMA((6,)),
            ],
            compiler_params=pltpu.CompilerParams(vmem_limit_bytes=50 << 20),
            cost_estimate=cost(1 << 34, 0),
            name="stats",
        )(
            place, info, early, key_codes, book, near[1], near[2], near[0], distant[0],
            q_sum, kv_sum, w_query, w_key, *rest,
        )

    totals = []

    def second(pair):
        pair, ready = lax.optimization_barrier((pair, place))
        totals.extend(log_totals(0, heads // 2, ready))
        return pair

    values = everyone(value, after(keys), second, lambda v: after(totals[2])(v))
    q_rot_0, q_t_0, log_total_0, init = totals
    late, _ = lax.optimization_barrier((place, values[2:5]))
    q_rot_1, q_t_1, log_total_1, _ = log_totals(heads // 2, heads // 2, late)

    most = total // BLOCK
    attention_out, local = pl.pallas_call(
        functools.partial(grad_kernel, heads, rows, levels),
        out_shape=(
            jax.ShapeDtypeStruct((rows, width), bf16),
            jax.ShapeDtypeStruct((levels, HD), f32),
        ),
        in_specs=[smem()] + [vmem()] * 10 + [anywhere()] * 14,
        out_specs=(vmem(),) * 2,
        scratch_shapes=[
            pltpu.VMEM((min(most, 7), heads, BLOCK, rows), f32),
            pltpu.VMEM((heads, rows, HD), f32),
            pltpu.VMEM((heads, rows), f32),
            pltpu.VMEM((levels, 8, HD), f32),
            pltpu.VMEM((total, HD), bf16),
            pltpu.VMEM((ranks // 2, 2, rows, HD), bf16),
            pltpu.VMEM((ranks // 2, 2, rows, HD), f32),
            pltpu.VMEM((ranks // 2, 2, rows, HD), f32),
            pltpu.VMEM((ranks // 2, 2, rows, HD), bf16),
            pltpu.SemaphoreType.DMA((24,)),
        ],
        compiler_params=pltpu.CompilerParams(vmem_limit_bytes=44 << 20),
        cost_estimate=cost(8 * rows * width * total, 8 << 20),
        name="grad",
    )(
        info, q_rot_0, q_t_0, log_total_0, q_rot_1, q_t_1, log_total_1, early, cotangent, cot_t, init,
        *[table for both in zip(near, distant) for table in both], *values,
    )
    for d in (1, 2, 4, 12):
        local = local + cross(local, d)
    return (attention_out, local.T)


def solution(mesh):
    placed = (
        P("tokens", "tensor"),
        P(None, "tensor"),
        P(None, "tensor"),
        P(None, "tensor"),
        P("tokens", "tensor"),
        P("tensor", None),
        P("tokens"),
        P("tokens", "tensor"),
    )
    return jax.shard_map(
        shards,
        mesh=mesh,
        in_specs=placed,
        out_specs=(P("tokens", "tensor"), P("tensor", None)),
        check_vma=False,
    )
```

```python
import functools
import math

import jax
import jax.numpy as jnp
from jax import lax
from jax.experimental import pallas as pl
from jax.experimental.pallas import tpu as pltpu
from jax.sharding import PartitionSpec as P

HD = 128
ROPE_BASE = 500000.0
NEG_BIG = -1e30
LOG2E = math.log2(math.e)
SCALE = 1.0 / math.sqrt(HD)
BLOCK = 512
NN = (((1,), (0,)), ((), ()))
TN = (((0,), (0,)), ((), ()))
TAIL = 16


def sincos(angle):
    turns = jnp.floor(angle * (2.0 / math.pi) + 0.5)
    r = angle - turns * 1.5703125
    r = r - turns * 4.837512969970703125e-4
    r = r - turns * 7.54978995489188216e-8
    z = r * r
    s = ((-1.9515295891e-4 * z + 8.3321608736e-3) * z - 1.6666654611e-1) * z * r + r
    c = ((2.443315711809948e-5 * z - 1.388731625493765e-3) * z + 4.166664568298827e-2) * z * z
    c = c - 0.5 * z + 1.0
    quadrant = turns.astype(jnp.int32)
    odd = (quadrant & 1) == 1
    sine = jnp.where(odd, c, s)
    cosine = jnp.where(odd, s, c)
    sine = jnp.where((quadrant & 2) == 0, sine, -sine)
    cosine = jnp.where(((quadrant + 1) & 2) == 0, cosine, -cosine)
    return sine, cosine


def slots(pieces):
    own, x, y1, y2, y3, core = pieces
    found = [(0, own, 0), (2, x, 0)]
    for y, ref in ((1, y1), (2, y2), (3, y3)):
        found += [(4 * y, ref, 0), (4 * y + 2, ref, 1)]
    return found + [(2 * j + 1, core, j) for j in range(8)]


def token_rank():
    return lax.axis_index("tokens")


def pack_kernel(rows, key_codes, positions, packed, early, info):
    packed[:rows, :] = key_codes[...].astype(jnp.float32).astype(jnp.bfloat16)
    place = positions[...]
    high, low = place & ~63, place & 63
    wide = [x[:, j * HD : (j + 1) * HD] for x in (high, low) for j in range(rows // HD)]
    blank = jnp.zeros((TAIL - len(wide), HD), jnp.int32)
    tail = jnp.concatenate(wide + [blank], axis=0)
    packed[rows:, :] = tail.astype(jnp.float32).astype(jnp.bfloat16)
    index = token_rank() * rows + lax.broadcasted_iota(jnp.int32, (1, rows), 1)
    first = index - place
    early[...] = first
    first = first.astype(jnp.float32)
    info[0] = jnp.min(first).astype(jnp.int32) // BLOCK
    info[1] = jnp.max(first).astype(jnp.int32)


def prep_kernel(
    near, rows, ranks, levels,
    inverse, book, *refs,
):
    pieces = refs[:5] if near else refs[:1]
    if near:
        cot, cot_t = refs[5], refs[10]
        for h in range(cot_t.shape[0]):
            cot_t[h] = cot[:, h * HD : (h + 1) * HD].T
        refs = refs[:10] + refs[11:]
    keys_f, cos_f, sin_f, codes_f, packed_s, keys, cos_k, sin_k, codes, sems, out_sems = refs[-11:]
    me = token_rank()
    tall = rows + TAIL
    if near:
        found = [(2 * j, ref, 0) for j, ref in enumerate(pieces[:4])]
        found += [(2 * j + 1, pieces[4], j) for j in range(4)]
    else:
        found = [(2 * j if j < 4 else 2 * (j - 4) + 1, pieces[0], j) for j in range(8)]
    copies = []
    for j, (bits, ref, at) in enumerate(found):
        start = pl.multiple_of(((me // 2) ^ bits) * tall, TAIL)
        copies.append(
            pltpu.make_async_copy(
                ref.at[at * tall : (at + 1) * tall, :], packed_s.at[pl.ds(start, tall), :], sems.at[j]
            )
        )
    for copy in copies:
        copy.start()
    for copy in copies:
        copy.wait()
    eye = lax.broadcasted_iota(jnp.int32, (HD, HD), 0) == lax.broadcasted_iota(
        jnp.int32, (HD, HD), 1
    )
    left = lax.broadcasted_iota(jnp.int32, (HD, HD), 1) < HD // 2
    ones = jnp.ones((2 * HD, HD), jnp.bfloat16)
    sides = rows // HD
    outs = [(keys, keys_f), (cos_k, cos_f), (sin_k, sin_f), (codes, codes_f)]

    @pl.loop(0, ranks)
    def _(i):
        source = pl.multiple_of(i * tall, TAIL)
        tail = packed_s[pl.ds(source + rows, TAIL), :].astype(jnp.float32)
        places = []
        for part in range(sides):
            high = jnp.where(eye, tail[part : part + 1, :], 0.0)
            low = jnp.where(eye, tail[sides + part : sides + part + 1, :], 0.0)
            digits = jnp.concatenate([high, low], axis=1).astype(jnp.bfloat16)
            places.append(lax.dot_general(digits, ones, NN, preferred_element_type=jnp.float32))
        for part in range(0, sides, 2):
            sine, cosine = sincos(jnp.where(left, places[part], places[part + 1]) * inverse[...])
            sine_r, cosine_r = pltpu.roll(sine, HD // 2, 1), pltpu.roll(cosine, HD // 2, 1)
            tables = (
                (jnp.where(left, cosine, cosine_r), jnp.where(left, -sine, sine_r)),
                (jnp.where(left, cosine_r, cosine), jnp.where(left, -sine_r, sine)),
            )
            for side, (cosine, sine) in enumerate(tables):
                at = part + side
                target = pl.ds(at * HD, HD)
                cos_k[i, target, :] = cosine
                sin_k[i, target, :] = sine
                raw = packed_s[pl.ds(source + at * HD, HD), :]
                codes[i, target, :] = raw
                code = raw.astype(jnp.float32).astype(jnp.int32)
                layer = [book[e : e + 1, :] for e in range(levels)]
                bit = 1
                while len(layer) > 1:
                    on = (code & bit) != 0
                    layer = [jnp.where(on, layer[j + 1], layer[j]) for j in range(0, len(layer), 2)]
                    bit *= 2
                deq = layer[0]
                turned = deq * cosine + pltpu.roll(deq, HD // 2, 1) * sine
                keys[i, target, :] = turned.astype(jnp.bfloat16)
        for j, (ref, full) in enumerate(outs):
            pltpu.make_async_copy(ref.at[i], full.at[i], out_sems.at[j]).start()

    for j, (ref, full) in enumerate(outs):
        pltpu.make_async_copy(ref, full, out_sems.at[j]).wait()


def shard_rows(place, n, part):
    return pl.ds(pl.multiple_of(place[n] * part, part), part)


def interleave(near, distant, ref, sem):
    core = token_rank() % 2
    return [
        pltpu.make_async_copy(half, ref.at[:, core ^ j], sem(j))
        for j, half in enumerate((near, distant))
    ]


def fetch(pieces, x_s, sem):
    copies, at = [], 0
    for piece in pieces:
        width = piece.shape[1]
        copies.append(pltpu.make_async_copy(piece, x_s.at[:, at : at + width], sem(len(copies))))
        at += width
    return copies


def project_kernel(
    count, part, place, wq, wk, wv, *refs,
):
    pieces, (q_out, kv_out, x_s, wq_s, wkv_s, sems) = refs[:count], refs[count:]
    copies = []
    for n, piece in enumerate(pieces):
        rows = shard_rows(place, n, part)
        copies.append([
            pltpu.make_async_copy(piece, x_s.at[n], sems.at[4 * n]),
            pltpu.make_async_copy(wq.at[rows, :], wq_s.at[n], sems.at[4 * n + 1]),
            pltpu.make_async_copy(wk.at[rows, :], wkv_s.at[n, :, :HD], sems.at[4 * n + 2]),
            pltpu.make_async_copy(wv.at[rows, :], wkv_s.at[n, :, HD:], sems.at[4 * n + 3]),
        ])
        for copy in copies[-1]:
            copy.start()
    for n in range(count):
        for copy in copies[n]:
            copy.wait()
        x = x_s[n]
        q = jnp.dot(x, wq_s[n], preferred_element_type=jnp.float32)
        kv = jnp.dot(x, wkv_s[n], preferred_element_type=jnp.float32)
        q_out[...] = q if n == 0 else q_out[...] + q
        kv_out[...] = kv if n == 0 else kv_out[...] + kv


def value_kernel(first, count, part, place, w, before, *refs):
    pieces, (value, x_s, w_s, before_s, sems) = refs[:-5], refs[-5:]
    copies = fetch(pieces, x_s, lambda j: sems.at[j])
    copies.append(pltpu.make_async_copy(before.at[:, HD:], before_s, sems.at[len(copies)]))
    for n in range(count):
        copies.append(
            pltpu.make_async_copy(w.at[shard_rows(place, first + n, part), :], w_s.at[n], sems.at[len(copies)])
        )
    for copy in copies:
        copy.start()
    for copy in copies:
        copy.wait()
    total = before_s[...]
    for n in range(count):
        total += jnp.dot(x_s[:, n * part : (n + 1) * part], w_s[n], preferred_element_type=jnp.float32)
    value[...] = total.astype(jnp.bfloat16)


def visible_block(base, block, own, earliest, rows):
    key = base + lax.broadcasted_iota(jnp.int32, (block, rows), 0)
    query = own + lax.broadcasted_iota(jnp.int32, (block, rows), 1)
    return (key <= query) & (key >= earliest)


def over_blocks(own, info, rows, body):
    first, edge = info[0], info[1]
    last = (own + rows + BLOCK - 1) // BLOCK

    @pl.loop(first, last)
    def _(b):
        masked = (b * BLOCK < edge) | (b * BLOCK + BLOCK > own)

        @pl.when(masked)
        def _():
            body(b, True)

        @pl.when(jnp.logical_not(masked))
        def _():
            body(b, False)


def stats_kernel(
    heads, wide, rows, levels, weight, first, count, part,
    place, info, early, codes, book, cos_k, sin_k, keys_n, keys_d, q_before, kv_before, wq, wk, *refs,
):
    pieces = refs[:-17]
    (
        q_rot, q_t, log_total, bins,
        peak_s, mass_s, cos_q, sin_q, keys, x_s, wq_s, wk_s, q_s, true_s, x_sems, w_sems, sems,
    ) = refs[-17:]
    own = token_rank() * rows
    mine = token_rank() // 2
    loads = fetch(pieces, x_s, lambda j: x_sems.at[j])
    weights = []
    for n in range(count):
        at = shard_rows(place, first + n, part)
        weights.append([
            pltpu.make_async_copy(wq.at[at, :], wq_s.at[n], w_sems.at[2 * n]),
            pltpu.make_async_copy(wk.at[at, :], wk_s.at[n], w_sems.at[2 * n + 1]),
        ])
    before = [
        pltpu.make_async_copy(q_before, q_s, sems.at[0]),
        pltpu.make_async_copy(kv_before.at[:, :HD], true_s, sems.at[1]),
    ]
    tables = [
        pltpu.make_async_copy(cos_k.at[mine], cos_q, sems.at[2]),
        pltpu.make_async_copy(sin_k.at[mine], sin_q, sems.at[3]),
    ] + interleave(keys_n, keys_d, keys, lambda j: sems.at[4 + j])
    for copy in before + loads + sum(weights, []) + tables:
        copy.start()
    for copy in before + loads:
        copy.wait()
    for n in range(count):
        for copy in weights[n]:
            copy.wait()
        x = x_s[:, n * part : (n + 1) * part]
        q_s[...] += jnp.dot(x, wq_s[n], preferred_element_type=jnp.float32)
        true_s[...] += jnp.dot(x, wk_s[n], preferred_element_type=jnp.float32)
    code = codes[...]
    for level in range(levels):
        entry = weight * (book[level : level + 1, :] - true_s[...])
        bins[level : level + 1, :] = jnp.sum(
            jnp.where(code == level, entry, 0.0), axis=0, keepdims=True
        )
    for copy in tables:
        copy.wait()
    for h in range(wide):
        x = q_s[:, h * HD : (h + 1) * HD]
        turned = (x * cos_q[...] + pltpu.roll(x, HD // 2, 1) * sin_q[...]).astype(jnp.bfloat16)
        q_rot[h] = turned
        q_t[h] = turned.T
    scan_totals(own, info, early, rows, 0, heads, q_t, keys, peak_s, mass_s, log_total)


def scan_totals(own, info, early, rows, begin, heads, q_t, keys, peak_s, mass_s, log_total):
    peak_s[...] = jnp.full_like(peak_s, NEG_BIG)
    mass_s[...] = jnp.zeros_like(mass_s)

    def body(b, masked):
        base = pl.multiple_of(b * BLOCK, BLOCK)
        k = keys[b].reshape(BLOCK, HD)
        if masked:
            seen = visible_block(base, BLOCK, own, early[...], rows)
        for h in range(heads):
            t = lax.dot_general(k, q_t[begin + h], NN, preferred_element_type=jnp.float32)
            t = t * (SCALE * LOG2E)
            if masked:
                t = jnp.where(seen, t, NEG_BIG)
            old = peak_s[h : h + 1, :]
            new = jnp.maximum(old, jnp.max(t, axis=0, keepdims=True))
            fresh = jnp.sum(jnp.exp2(t - new), axis=0, keepdims=True)
            mass_s[h : h + 1, :] = mass_s[h : h + 1, :] * jnp.exp2(old - new) + fresh
            peak_s[h : h + 1, :] = new

    over_blocks(own, info, rows, body)
    log_total[...] = peak_s[...] + jnp.log(mass_s[...]) * LOG2E


def late_stats_kernel(
    begin, heads, rows, info, early, q_t, keys_n, keys_d, log_total, peak_s, mass_s, keys, sems,
):
    copies = interleave(keys_n, keys_d, keys, lambda j: sems.at[j])
    for copy in copies:
        copy.start()
    for copy in copies:
        copy.wait()
    own = token_rank() * rows
    scan_totals(own, info, early, rows, begin, heads, q_t, keys, peak_s, mass_s, log_total)


def grad_kernel(
    heads, rows, levels,
    info, q_rot, q_t, log_total_0, log_total_1, early, cot, cot_t, init,
    keys_n, keys_d, cos_n, cos_d, sin_n, sin_d, codes_n, codes_d, v_own, v_x, v_y1, v_y2, v_y3, v_core,
    out, bins, probs_s, out_s, delta_s, acc_s, values, keys, cos_k, sin_k, codes, held, sems,
):
    me = token_rank()
    own, first = me * rows, info[0]
    part = heads // 2
    early_heads = log_total_0.shape[0]
    log_total = [log_total_0.at[h : h + 1, :] for h in range(early_heads)]
    log_total += [log_total_1.at[h : h + 1, :] for h in range(heads - early_heads)]
    copies = interleave(keys_n, keys_d, keys, lambda j: sems.at[16 + j])
    for j, (bits, ref, at) in enumerate(slots((v_own, v_x, v_y1, v_y2, v_y3, v_core))):
        start = pl.multiple_of((me ^ bits) * rows, rows)
        copies.append(
            pltpu.make_async_copy(
                ref.at[at * rows : (at + 1) * rows, :], values.at[pl.ds(start, rows), :], sems.at[j]
            )
        )
    late = interleave(cos_n, cos_d, cos_k, lambda j: sems.at[18 + j])
    late += interleave(sin_n, sin_d, sin_k, lambda j: sems.at[20 + j])
    late += interleave(codes_n, codes_d, codes, lambda j: sems.at[22 + j])
    for copy in copies + late:
        copy.start()
    out_s[...] = jnp.zeros_like(out_s)
    for copy in copies:
        copy.wait()

    def forward(b, masked):
        base = pl.multiple_of(b * BLOCK, BLOCK)
        k = keys[b].reshape(BLOCK, HD)
        v = values[pl.ds(base, BLOCK), :]
        if masked:
            seen = visible_block(base, BLOCK, own, early[...], rows)
        for h in range(heads):
            s = lax.dot_general(k, q_t[h], NN, preferred_element_type=jnp.float32)
            p = jnp.exp2(s * (SCALE * LOG2E) - log_total[h][...])
            if masked:
                p = jnp.where(seen, p, 0.0)
            probs_s[b - first, h] = p
            out_s[h] += lax.dot_general(
                p.astype(jnp.bfloat16), v, TN, preferred_element_type=jnp.float32
            )

    over_blocks(own, info, rows, forward)
    for h in range(heads):
        o = out_s[h].astype(jnp.bfloat16)
        out[:, h * HD : (h + 1) * HD] = o
        prod = cot[:, h * HD : (h + 1) * HD].astype(jnp.float32) * o.astype(jnp.float32)
        delta_s[h : h + 1, :] = jnp.sum(prod.T, axis=0, keepdims=True)
    acc_s[...] = jnp.zeros_like(acc_s)
    last = (own + rows + BLOCK - 1) // BLOCK
    for copy in late:
        copy.wait()

    def add_bins(b, dk):
        dk = dk * SCALE
        cosine, sine = cos_k[b].reshape(BLOCK, HD), sin_k[b].reshape(BLOCK, HD)
        g = dk * cosine - pltpu.roll(dk, HD // 2, 1) * sine
        code = codes[b].reshape(BLOCK, HD).astype(jnp.float32)
        for level in range(levels):
            chosen = jnp.where(code == level, g, 0.0)
            acc_s[level] += jnp.sum(chosen.reshape(BLOCK // 8, 8, HD), axis=0)

    held[...] = jnp.zeros_like(held)

    @pl.loop(first, last)
    def _(b):
        base = pl.multiple_of(b * BLOCK, BLOCK)
        v = values[pl.ds(base, BLOCK), :]
        add_bins(jnp.maximum(b - 1, first), held[...])
        dk = jnp.zeros((BLOCK, HD), jnp.float32)
        for h in range(heads):
            dp = lax.dot_general(v, cot_t[h], NN, preferred_element_type=jnp.float32)
            ds = (probs_s[b - first, h] * (dp - delta_s[h : h + 1, :])).astype(jnp.bfloat16)
            dk = dk + lax.dot_general(ds, q_rot[h], NN, preferred_element_type=jnp.float32)
        held[...] = dk

    add_bins(last - 1, held[...])
    bins[...] = init[...] + jnp.sum(acc_s[...], axis=1)


def anywhere():
    return pl.BlockSpec(memory_space=pl.ANY)


def vmem():
    return pl.BlockSpec(memory_space=pltpu.VMEM)


def smem():
    return pl.BlockSpec(memory_space=pltpu.SMEM)


def cost(flops, size):
    return pl.CostEstimate(flops=flops, bytes_accessed=size, transcendentals=0)


def shards(hidden, w_query, w_key, w_value, key_codes, codebook, positions, cotangent):
    rows, part = hidden.shape
    width = w_query.shape[1]
    heads = width // HD
    levels = codebook.shape[1]
    ranks = lax.axis_size("tokens")
    total = rows * ranks
    group = lax.axis_size("tensor")
    rank = lax.axis_index("tensor")
    me = lax.axis_index("tokens")
    own = me * rows
    bf16, f32 = jnp.bfloat16, jnp.float32

    cross = lambda x, d: lax.ppermute(x, "tokens", [(i, i ^ d) for i in range(ranks)])

    def everyone(x, first, second, third):
        x_side = first(cross(x, 2))
        pair = second(jnp.concatenate([x, x_side], axis=0))
        y_side = [cross(pair, 4 * y) for y in (1, 2, 3)]
        core = cross(third(jnp.concatenate([pair] + y_side, axis=0)), 1)
        return (x, x_side, *y_side, core)

    def after(*others):
        return lambda v: lax.optimization_barrier((v, others))[0]

    flip = [(i, i ^ 1) for i in range(group)]
    up = [(i, (i + 2) % group) for i in range(group)]
    down = [(i, (i - 2) % group) for i in range(group)]
    send = functools.partial(lax.ppermute, axis_name="tensor")
    n = part // 2
    low = send(hidden, perm=up)
    high = send(hidden, perm=down)
    other = send(hidden, perm=flip)
    places = positions[None, :]
    packed, early, info = pl.pallas_call(
        functools.partial(pack_kernel, rows),
        out_shape=(
            jax.ShapeDtypeStruct((rows + TAIL, HD), bf16),
            jax.ShapeDtypeStruct((1, rows), jnp.int32),
            jax.ShapeDtypeStruct((2,), jnp.int32),
        ),
        in_specs=[vmem()] * 2,
        out_specs=(vmem(), vmem(), smem()),
        name="pack",
    )(key_codes, places)
    book = codebook.T
    inverse = jnp.exp((jnp.arange(HD) % (HD // 2)).astype(f32) * (-2.0 * math.log(ROPE_BASE) / HD))

    mate = rank ^ 1
    turn = lambda x, by: (x + by) % group
    shard = [rank, turn(rank, -2), turn(rank, 2), mate]
    shard += [turn(rank, 4), turn(mate, -2), turn(mate, 2), turn(mate, 4)]
    place = jnp.stack(shard).astype(jnp.int32)

    y_side = [cross(packed, 4 * y) for y in (1, 2, 3)]
    column = jnp.concatenate([packed] + y_side, axis=0)
    x_side = cross(column, 2)
    low, high, other = after(column)((low, high, other))
    far_a = send(low[:, :n], perm=up)
    far_b = send(high[:, n:], perm=down)
    other_low = send(other, perm=up)
    other_high = send(other, perm=down)
    other_far_a = send(far_a, perm=flip)
    other_far_b = send(far_b, perm=flip)

    half = group // 2
    low, high, other = after(far_a, far_b)((low, high, other))
    q_sum, kv_sum = pl.pallas_call(
        functools.partial(project_kernel, half, part),
        out_shape=(jax.ShapeDtypeStruct((rows, width), f32), jax.ShapeDtypeStruct((rows, 2 * HD), f32)),
        in_specs=[smem()] + [anywhere()] * (3 + half),
        out_specs=(vmem(),) * 2,
        scratch_shapes=[
            pltpu.VMEM((half, rows, part), bf16),
            pltpu.VMEM((half, part, width), bf16),
            pltpu.VMEM((half, part, 2 * HD), bf16),
            pltpu.SemaphoreType.DMA((4 * half,)),
        ],
        compiler_params=pltpu.CompilerParams(vmem_limit_bytes=50 << 20),
        cost_estimate=cost(1 << 34, 0),
        name="project",
    )(place, w_query, w_key, w_value, hidden, low, high, other)
    core = cross(jnp.concatenate([column, x_side], axis=0), 1)
    packed = (packed, *y_side, x_side, core)

    rest = [far_a, far_b, other_low, other_high, other_far_a, other_far_b]
    value = pl.pallas_call(
        functools.partial(value_kernel, half, half, part),
        out_shape=jax.ShapeDtypeStruct((rows, HD), bf16),
        in_specs=[smem()] + [anywhere()] * (2 + len(rest)),
        out_specs=vmem(),
        scratch_shapes=[
            pltpu.VMEM((rows, half * part), bf16),
            pltpu.VMEM((half, part, HD), bf16),
            pltpu.VMEM((rows, HD), f32),
            pltpu.SemaphoreType.DMA((half + len(rest) + 1,)),
        ],
        compiler_params=pltpu.CompilerParams(vmem_limit_bytes=50 << 20),
        cost_estimate=cost(0, 0),
        name="value",
    )(place, w_value, kv_sum, *rest)

    def prep(near, inverse, *pieces):
        few = ranks // 2
        shapes = [(few, rows, HD)] * 4
        kinds = [bf16, f32, f32, bf16]
        return pl.pallas_call(
            functools.partial(prep_kernel, near, rows, few, levels),
            out_shape=[jax.ShapeDtypeStruct(size, kind) for size, kind in zip(shapes, kinds)]
            + [jax.ShapeDtypeStruct((heads, HD, rows), bf16)] * near,
            in_specs=[vmem()] * 2 + [anywhere()] * (5 if near else 1) + [vmem()] * near,
            out_specs=[anywhere()] * 4 + [vmem()] * near,
            scratch_shapes=[pltpu.VMEM((few * (rows + TAIL), HD), bf16)]
            + [pltpu.VMEM(size, kind) for size, kind in zip(shapes, kinds)]
            + [pltpu.SemaphoreType.DMA((few,)), pltpu.SemaphoreType.DMA((4,))],
            compiler_params=pltpu.CompilerParams(vmem_limit_bytes=58 << 20),
            cost_estimate=cost(0 if near else 1 << 32, 0),
            name="prep",
        )(inverse, book, *pieces)

    *near, cot_t = prep(True, after(kv_sum)(inverse[None, :]), *packed[:5], cotangent)
    distant = prep(False, after(value)(inverse[None, :]), packed[5])
    keys = distant[0]

    count = heads * 3 // 8
    totals = []

    def second(pair):
        pair, ready = lax.optimization_barrier((pair, place))
        found = pl.pallas_call(
            functools.partial(
                stats_kernel, count, heads, rows, levels, levels / total, half, half, part
            ),
            out_shape=(
                jax.ShapeDtypeStruct((heads, rows, HD), bf16),
                jax.ShapeDtypeStruct((heads, HD, rows), bf16),
                jax.ShapeDtypeStruct((count, rows), f32),
                jax.ShapeDtypeStruct((levels, HD), f32),
            ),
            in_specs=[smem()] * 2 + [vmem()] * 3 + [anywhere()] * (8 + len(rest)),
            out_specs=(vmem(),) * 4,
            scratch_shapes=[pltpu.VMEM((count, rows), f32)] * 2
            + [pltpu.VMEM((rows, HD), f32)] * 2
            + [
                pltpu.VMEM((ranks // 2, 2, rows, HD), bf16),
                pltpu.VMEM((rows, half * part), bf16),
                pltpu.VMEM((half, part, width), bf16),
                pltpu.VMEM((half, part, HD), bf16),
                pltpu.VMEM((rows, width), f32),
                pltpu.VMEM((rows, HD), f32),
                pltpu.SemaphoreType.DMA((len(rest),)),
                pltpu.SemaphoreType.DMA((2 * half,)),
                pltpu.SemaphoreType.DMA((6,)),
            ],
            compiler_params=pltpu.CompilerParams(vmem_limit_bytes=50 << 20),
            cost_estimate=cost(1 << 34, 0),
            name="stats",
        )(
            ready, info, early, key_codes, book, near[1], near[2], near[0], distant[0],
            q_sum, kv_sum, w_query, w_key, *rest,
        )
        totals.extend(found)
        return pair

    values = everyone(value, after(keys), second, lambda v: after(totals[2])(v))
    q_rot, q_t, log_total_0, init = totals
    late, _ = lax.optimization_barrier((q_t, values[2:5]))
    log_total_1 = pl.pallas_call(
        functools.partial(late_stats_kernel, count, heads - count, rows),
        out_shape=jax.ShapeDtypeStruct((heads - count, rows), f32),
        in_specs=[smem()] + [vmem()] * 2 + [anywhere()] * 2,
        out_specs=vmem(),
        scratch_shapes=[pltpu.VMEM((heads - count, rows), f32)] * 2
        + [pltpu.VMEM((ranks // 2, 2, rows, HD), bf16), pltpu.SemaphoreType.DMA((2,))],
        compiler_params=pltpu.CompilerParams(vmem_limit_bytes=32 << 20),
        cost_estimate=cost(1 << 34, 0),
        name="stats_late",
    )(info, early, late, near[0], distant[0])

    most = total // BLOCK
    attention_out, local = pl.pallas_call(
        functools.partial(grad_kernel, heads, rows, levels),
        out_shape=(
            jax.ShapeDtypeStruct((rows, width), bf16),
            jax.ShapeDtypeStruct((levels, HD), f32),
        ),
        in_specs=[smem()] + [vmem()] * 8 + [anywhere()] * 14,
        out_specs=(vmem(),) * 2,
        scratch_shapes=[
            pltpu.VMEM((min(most, 7), heads, BLOCK, rows), f32),
            pltpu.VMEM((heads, rows, HD), f32),
            pltpu.VMEM((heads, rows), f32),
            pltpu.VMEM((levels, 8, HD), f32),
            pltpu.VMEM((total, HD), bf16),
            pltpu.VMEM((ranks // 2, 2, rows, HD), bf16),
            pltpu.VMEM((ranks // 2, 2, rows, HD), f32),
            pltpu.VMEM((ranks // 2, 2, rows, HD), f32),
            pltpu.VMEM((ranks // 2, 2, rows, HD), bf16),
            pltpu.VMEM((BLOCK, HD), f32),
            pltpu.SemaphoreType.DMA((24,)),
        ],
        compiler_params=pltpu.CompilerParams(vmem_limit_bytes=44 << 20),
        cost_estimate=cost(8 * rows * width * total, 8 << 20),
        name="grad",
    )(
        info, q_rot, q_t, log_total_0, log_total_1, early, cotangent, cot_t, init,
        *[table for both in zip(near, distant) for table in both], *values,
    )
    for d in (1, 2, 4, 12):
        local = local + cross(local, d)
    return (attention_out, local.T)


def solution(mesh):
    placed = (
        P("tokens", "tensor"),
        P(None, "tensor"),
        P(None, "tensor"),
        P(None, "tensor"),
        P("tokens", "tensor"),
        P("tensor", None),
        P("tokens"),
        P("tokens", "tensor"),
    )
    return jax.shard_map(
        shards,
        mesh=mesh,
        in_specs=placed,
        out_specs=(P("tokens", "tensor"), P("tensor", None)),
        check_vma=False,
    )
```

```python
import functools
import math

import jax
import jax.numpy as jnp
from jax import lax
from jax.experimental import pallas as pl
from jax.experimental.pallas import tpu as pltpu
from jax.sharding import PartitionSpec as P

HD = 128
ROPE_BASE = 500000.0
NEG_BIG = -1e30
LOG2E = math.log2(math.e)
SCALE = 1.0 / math.sqrt(HD)
BLOCK = 512
NN = (((1,), (0,)), ((), ()))
TN = (((0,), (0,)), ((), ()))
TAIL = 16
STRIP = 32


def sincos(angle):
    turns = jnp.floor(angle * (2.0 / math.pi) + 0.5)
    r = angle - turns * 1.5703125
    r = r - turns * 4.837512969970703125e-4
    r = r - turns * 7.54978995489188216e-8
    z = r * r
    s = ((-1.9515295891e-4 * z + 8.3321608736e-3) * z - 1.6666654611e-1) * z * r + r
    c = ((2.443315711809948e-5 * z - 1.388731625493765e-3) * z + 4.166664568298827e-2) * z * z
    c = c - 0.5 * z + 1.0
    quadrant = turns.astype(jnp.int32)
    odd = (quadrant & 1) == 1
    sine = jnp.where(odd, c, s)
    cosine = jnp.where(odd, s, c)
    sine = jnp.where((quadrant & 2) == 0, sine, -sine)
    cosine = jnp.where(((quadrant + 1) & 2) == 0, cosine, -cosine)
    return sine, cosine


def slots(pieces):
    own, x, y1, y2, y3, core = pieces
    found = [(0, own, 0), (2, x, 0)]
    for y, ref in ((1, y1), (2, y2), (3, y3)):
        found += [(4 * y, ref, 0), (4 * y + 2, ref, 1)]
    return found + [(2 * j + 1, core, j) for j in range(8)]


def token_rank():
    return lax.axis_index("tokens")


def pack_kernel(rows, key_codes, positions, packed, early, info):
    packed[:rows, :] = key_codes[...].astype(jnp.float32).astype(jnp.bfloat16)
    place = positions[...]
    high, low = place & ~63, place & 63
    wide = [x[:, j * HD : (j + 1) * HD] for x in (high, low) for j in range(rows // HD)]
    blank = jnp.zeros((TAIL - len(wide), HD), jnp.int32)
    tail = jnp.concatenate(wide + [blank], axis=0)
    packed[rows:, :] = tail.astype(jnp.float32).astype(jnp.bfloat16)
    index = token_rank() * rows + lax.broadcasted_iota(jnp.int32, (1, rows), 1)
    first = index - place
    early[...] = first
    first = first.astype(jnp.float32)
    info[0] = jnp.min(first).astype(jnp.int32) // BLOCK
    info[1] = jnp.max(first).astype(jnp.int32)


def prep_kernel(
    near, rows, ranks, levels,
    book, *refs,
):
    pieces = refs[:5] if near else refs[:1]
    if near:
        cot_f, cot_t, cot = refs[5], refs[10], refs[-1]
        refs = refs[:10] + refs[11:-1]
    keys_f, cos_f, sin_f, codes_f, packed_s, keys, cos_k, sin_k, codes, sems, out_sems = refs[-11:]
    me = token_rank()
    tall = rows + TAIL
    if near:
        loading = pltpu.make_async_copy(cot_f, cot, sems.at[ranks])
        loading.start()
    if near:
        found = [(2 * j, ref, 0) for j, ref in enumerate(pieces[:4])]
        found += [(2 * j + 1, pieces[4], j) for j in range(4)]
    else:
        found = [(2 * j if j < 4 else 2 * (j - 4) + 1, pieces[0], j) for j in range(8)]
    copies = []
    for j, (bits, ref, at) in enumerate(found):
        start = pl.multiple_of(((me // 2) ^ bits) * tall, TAIL)
        copies.append(
            pltpu.make_async_copy(
                ref.at[at * tall : (at + 1) * tall, :], packed_s.at[pl.ds(start, tall), :], sems.at[j]
            )
        )
    for copy in copies:
        copy.start()
    for copy in copies:
        copy.wait()
    eye = lax.broadcasted_iota(jnp.int32, (HD, HD), 0) == lax.broadcasted_iota(
        jnp.int32, (HD, HD), 1
    )
    left = lax.broadcasted_iota(jnp.int32, (STRIP, HD), 1) < HD // 2
    ones = jnp.ones((2 * HD, HD), jnp.bfloat16)
    sides = rows // HD
    outs = [(keys, keys_f), (cos_k, cos_f), (sin_k, sin_f), (codes, codes_f)]

    inverse = jnp.exp(
        (lax.broadcasted_iota(jnp.int32, (1, HD), 1) % (HD // 2)).astype(jnp.float32)
        * (-2.0 * math.log(ROPE_BASE) / HD)
    )

    def prep_strip(i, part, strip, places, source):
        rows_of = slice(strip, strip + STRIP)
        place = jnp.where(left, places[part][rows_of, :], places[part + 1][rows_of, :])
        sine, cosine = sincos(place * inverse)
        sine_r, cosine_r = pltpu.roll(sine, HD // 2, 1), pltpu.roll(cosine, HD // 2, 1)
        tables = (
            (jnp.where(left, cosine, cosine_r), jnp.where(left, -sine, sine_r)),
            (jnp.where(left, cosine_r, cosine), jnp.where(left, -sine_r, sine)),
        )
        for side, (cosine, sine) in enumerate(tables):
            at = (part + side) * HD + strip
            target = pl.ds(at, STRIP)
            cos_k[i, target, :] = cosine
            sin_k[i, target, :] = sine
            raw = packed_s[pl.ds(source + at, STRIP), :]
            codes[i, target, :] = raw
            code = raw.astype(jnp.float32).astype(jnp.int32)
            layer = [book[e : e + 1, :] for e in range(levels)]
            bit = 1
            while len(layer) > 1:
                on = (code & bit) != 0
                layer = [jnp.where(on, layer[j + 1], layer[j]) for j in range(0, len(layer), 2)]
                bit *= 2
            deq = layer[0]
            turned = deq * cosine + pltpu.roll(deq, HD // 2, 1) * sine
            keys[i, target, :] = turned.astype(jnp.bfloat16)

    @pl.loop(0, ranks)
    def _(i):
        source = pl.multiple_of(i * tall, TAIL)
        tail = packed_s[pl.ds(source + rows, TAIL), :].astype(jnp.float32)
        places = []
        for part in range(sides):
            high = jnp.where(eye, tail[part : part + 1, :], 0.0)
            low = jnp.where(eye, tail[sides + part : sides + part + 1, :], 0.0)
            digits = jnp.concatenate([high, low], axis=1).astype(jnp.bfloat16)
            places.append(lax.dot_general(digits, ones, NN, preferred_element_type=jnp.float32))
        for part in range(0, sides, 2):
            for strip in range(0, HD, STRIP):
                prep_strip(i, part, strip, places, source)
        for j, (ref, full) in enumerate(outs):
            pltpu.make_async_copy(ref.at[i], full.at[i], out_sems.at[j]).start()

    if near:
        loading.wait()
        for h in range(cot_t.shape[0]):
            cot_t[h] = cot[:, h * HD : (h + 1) * HD].T
    for j, (ref, full) in enumerate(outs):
        pltpu.make_async_copy(ref, full, out_sems.at[j]).wait()


def shard_rows(place, n, part):
    return pl.ds(pl.multiple_of(place[n] * part, part), part)


def interleave(near, distant, ref, sem):
    core = token_rank() % 2
    return [
        pltpu.make_async_copy(half, ref.at[:, core ^ j], sem(j))
        for j, half in enumerate((near, distant))
    ]


def fetch(pieces, x_s, sem):
    copies, at = [], 0
    for piece in pieces:
        width = piece.shape[1]
        copies.append(pltpu.make_async_copy(piece, x_s.at[:, at : at + width], sem(len(copies))))
        at += width
    return copies


def project_kernel(
    count, part, place, wq, wk, wv, *refs,
):
    pieces, (q_out, kv_out, x_s, wq_s, wkv_s, sems) = refs[:count], refs[count:]
    copies = []
    for n, piece in enumerate(pieces):
        rows = shard_rows(place, n, part)
        copies.append([
            pltpu.make_async_copy(piece, x_s.at[n], sems.at[4 * n]),
            pltpu.make_async_copy(wq.at[rows, :], wq_s.at[n], sems.at[4 * n + 1]),
            pltpu.make_async_copy(wk.at[rows, :], wkv_s.at[n, :, :HD], sems.at[4 * n + 2]),
            pltpu.make_async_copy(wv.at[rows, :], wkv_s.at[n, :, HD:], sems.at[4 * n + 3]),
        ])
        for copy in copies[-1]:
            copy.start()
    for n in range(count):
        for copy in copies[n]:
            copy.wait()
        x = x_s[n]
        q = jnp.dot(x, wq_s[n], preferred_element_type=jnp.float32)
        kv = jnp.dot(x, wkv_s[n], preferred_element_type=jnp.float32)
        q_out[...] = q if n == 0 else q_out[...] + q
        kv_out[...] = kv if n == 0 else kv_out[...] + kv


def value_kernel(first, count, part, place, w, before, *refs):
    pieces, (value, x_s, w_s, before_s, sems) = refs[:-5], refs[-5:]
    copies = fetch(pieces, x_s, lambda j: sems.at[j])
    copies.append(pltpu.make_async_copy(before.at[:, HD:], before_s, sems.at[len(copies)]))
    for n in range(count):
        copies.append(
            pltpu.make_async_copy(w.at[shard_rows(place, first + n, part), :], w_s.at[n], sems.at[len(copies)])
        )
    for copy in copies:
        copy.start()
    for copy in copies:
        copy.wait()
    total = before_s[...]
    for n in range(count):
        total += jnp.dot(x_s[:, n * part : (n + 1) * part], w_s[n], preferred_element_type=jnp.float32)
    value[...] = total.astype(jnp.bfloat16)


def visible_block(base, block, own, earliest, rows):
    key = base + lax.broadcasted_iota(jnp.int32, (block, rows), 0)
    query = own + lax.broadcasted_iota(jnp.int32, (block, rows), 1)
    return (key <= query) & (key >= earliest)


def over_blocks(own, info, rows, body):
    first, edge = info[0], info[1]
    last = (own + rows + BLOCK - 1) // BLOCK

    @pl.loop(first, last)
    def _(b):
        masked = (b * BLOCK < edge) | (b * BLOCK + BLOCK > own)

        @pl.when(masked)
        def _():
            body(b, True)

        @pl.when(jnp.logical_not(masked))
        def _():
            body(b, False)


def stats_kernel(
    heads, wide, rows, levels, weight, first, count, part,
    place, info, early, codes, book, cos_k, sin_k, keys_n, keys_d, q_before, kv_before, wq, wk, *refs,
):
    pieces = refs[:-17]
    (
        q_rot, q_t, log_total, bins,
        peak_s, mass_s, cos_q, sin_q, keys, x_s, wq_s, wk_s, q_s, true_s, x_sems, w_sems, sems,
    ) = refs[-17:]
    own = token_rank() * rows
    mine = token_rank() // 2
    loads = fetch(pieces, x_s, lambda j: x_sems.at[j])
    weights = []
    for n in range(count):
        at = shard_rows(place, first + n, part)
        weights.append([
            pltpu.make_async_copy(wq.at[at, :], wq_s.at[n], w_sems.at[2 * n]),
            pltpu.make_async_copy(wk.at[at, :], wk_s.at[n], w_sems.at[2 * n + 1]),
        ])
    before = [
        pltpu.make_async_copy(q_before, q_s, sems.at[0]),
        pltpu.make_async_copy(kv_before.at[:, :HD], true_s, sems.at[1]),
    ]
    tables = [
        pltpu.make_async_copy(cos_k.at[mine], cos_q, sems.at[2]),
        pltpu.make_async_copy(sin_k.at[mine], sin_q, sems.at[3]),
    ] + interleave(keys_n, keys_d, keys, lambda j: sems.at[4 + j])
    for copy in before + loads + sum(weights, []) + tables:
        copy.start()
    for copy in before + loads:
        copy.wait()
    for n in range(count):
        for copy in weights[n]:
            copy.wait()
        x = x_s[:, n * part : (n + 1) * part]
        q_s[...] += jnp.dot(x, wq_s[n], preferred_element_type=jnp.float32)
        true_s[...] += jnp.dot(x, wk_s[n], preferred_element_type=jnp.float32)
    code = codes[...]
    for level in range(levels):
        entry = weight * (book[level : level + 1, :] - true_s[...])
        bins[level : level + 1, :] = jnp.sum(
            jnp.where(code == level, entry, 0.0), axis=0, keepdims=True
        )
    for copy in tables:
        copy.wait()
    for h in range(wide):
        x = q_s[:, h * HD : (h + 1) * HD]
        turned = (x * cos_q[...] + pltpu.roll(x, HD // 2, 1) * sin_q[...]).astype(jnp.bfloat16)
        q_rot[h] = turned
        q_t[h] = turned.T
    scan_totals(own, info, early, rows, 0, heads, q_t, keys, peak_s, mass_s, log_total)


def scan_totals(own, info, early, rows, begin, heads, q_t, keys, peak_s, mass_s, log_total):
    peak_s[...] = jnp.full_like(peak_s, NEG_BIG)
    mass_s[...] = jnp.zeros_like(mass_s)

    def body(b, masked):
        base = pl.multiple_of(b * BLOCK, BLOCK)
        k = keys[b].reshape(BLOCK, HD)
        if masked:
            seen = visible_block(base, BLOCK, own, early[...], rows)
        for h in range(heads):
            t = lax.dot_general(k, q_t[begin + h], NN, preferred_element_type=jnp.float32)
            t = t * (SCALE * LOG2E)
            if masked:
                t = jnp.where(seen, t, NEG_BIG)
            old = peak_s[h : h + 1, :]
            new = jnp.maximum(old, jnp.max(t, axis=0, keepdims=True))
            fresh = jnp.sum(jnp.exp2(t - new), axis=0, keepdims=True)
            mass_s[h : h + 1, :] = mass_s[h : h + 1, :] * jnp.exp2(old - new) + fresh
            peak_s[h : h + 1, :] = new

    over_blocks(own, info, rows, body)
    log_total[...] = peak_s[...] + jnp.log(mass_s[...]) * LOG2E


def late_stats_kernel(
    begin, heads, rows, info, early, q_t, keys_n, keys_d, log_total, peak_s, mass_s, keys, sems,
):
    copies = interleave(keys_n, keys_d, keys, lambda j: sems.at[j])
    for copy in copies:
        copy.start()
    for copy in copies:
        copy.wait()
    own = token_rank() * rows
    scan_totals(own, info, early, rows, begin, heads, q_t, keys, peak_s, mass_s, log_total)


def grad_kernel(
    heads, rows, levels,
    info, q_rot, q_t, log_total_0, log_total_1, early, cot, cot_t, init,
    keys_n, keys_d, cos_n, cos_d, sin_n, sin_d, codes_n, codes_d, v_own, v_x, v_y1, v_y2, v_y3, v_core,
    out, bins, probs_s, out_s, delta_s, acc_s, values, keys, cos_k, sin_k, codes, held, sems,
):
    me = token_rank()
    own, first = me * rows, info[0]
    part = heads // 2
    early_heads = log_total_0.shape[0]
    log_total = [log_total_0.at[h : h + 1, :] for h in range(early_heads)]
    log_total += [log_total_1.at[h : h + 1, :] for h in range(heads - early_heads)]
    copies = interleave(keys_n, keys_d, keys, lambda j: sems.at[16 + j])
    for j, (bits, ref, at) in enumerate(slots((v_own, v_x, v_y1, v_y2, v_y3, v_core))):
        start = pl.multiple_of((me ^ bits) * rows, rows)
        copies.append(
            pltpu.make_async_copy(
                ref.at[at * rows : (at + 1) * rows, :], values.at[pl.ds(start, rows), :], sems.at[j]
            )
        )
    late = interleave(cos_n, cos_d, cos_k, lambda j: sems.at[18 + j])
    late += interleave(sin_n, sin_d, sin_k, lambda j: sems.at[20 + j])
    late += interleave(codes_n, codes_d, codes, lambda j: sems.at[22 + j])
    for copy in copies + late:
        copy.start()
    out_s[...] = jnp.zeros_like(out_s)
    for copy in copies:
        copy.wait()

    def forward(b, masked):
        base = pl.multiple_of(b * BLOCK, BLOCK)
        k = keys[b].reshape(BLOCK, HD)
        v = values[pl.ds(base, BLOCK), :]
        if masked:
            seen = visible_block(base, BLOCK, own, early[...], rows)
        for h in range(heads):
            s = lax.dot_general(k, q_t[h], NN, preferred_element_type=jnp.float32)
            p = jnp.exp2(s * (SCALE * LOG2E) - log_total[h][...])
            if masked:
                p = jnp.where(seen, p, 0.0)
            probs_s[b - first, h] = p
            out_s[h] += lax.dot_general(
                p.astype(jnp.bfloat16), v, TN, preferred_element_type=jnp.float32
            )

    over_blocks(own, info, rows, forward)
    for h in range(heads):
        o = out_s[h].astype(jnp.bfloat16)
        out[:, h * HD : (h + 1) * HD] = o
        prod = cot[:, h * HD : (h + 1) * HD].astype(jnp.float32) * o.astype(jnp.float32)
        delta_s[h : h + 1, :] = jnp.sum(prod.T, axis=0, keepdims=True)
    acc_s[...] = jnp.zeros_like(acc_s)
    last = (own + rows + BLOCK - 1) // BLOCK
    for copy in late:
        copy.wait()

    def add_bins(b, dk):
        dk = dk * SCALE
        cosine, sine = cos_k[b].reshape(BLOCK, HD), sin_k[b].reshape(BLOCK, HD)
        g = dk * cosine - pltpu.roll(dk, HD // 2, 1) * sine
        code = codes[b].reshape(BLOCK, HD).astype(jnp.float32)
        for level in range(levels):
            chosen = jnp.where(code == level, g, 0.0)
            acc_s[level] += jnp.sum(chosen.reshape(BLOCK // 8, 8, HD), axis=0)

    held[...] = jnp.zeros_like(held)

    @pl.loop(first, last)
    def _(b):
        base = pl.multiple_of(b * BLOCK, BLOCK)
        v = values[pl.ds(base, BLOCK), :]
        add_bins(jnp.maximum(b - 1, first), held[...])
        dk = jnp.zeros((BLOCK, HD), jnp.float32)
        for h in range(heads):
            dp = lax.dot_general(v, cot_t[h], NN, preferred_element_type=jnp.float32)
            ds = (probs_s[b - first, h] * (dp - delta_s[h : h + 1, :])).astype(jnp.bfloat16)
            dk = dk + lax.dot_general(ds, q_rot[h], NN, preferred_element_type=jnp.float32)
        held[...] = dk

    add_bins(last - 1, held[...])
    bins[...] = init[...] + jnp.sum(acc_s[...], axis=1)


def anywhere():
    return pl.BlockSpec(memory_space=pl.ANY)


def vmem():
    return pl.BlockSpec(memory_space=pltpu.VMEM)


def smem():
    return pl.BlockSpec(memory_space=pltpu.SMEM)


def cost(flops, size):
    return pl.CostEstimate(flops=flops, bytes_accessed=size, transcendentals=0)


def shards(hidden, w_query, w_key, w_value, key_codes, codebook, positions, cotangent):
    rows, part = hidden.shape
    width = w_query.shape[1]
    heads = width // HD
    levels = codebook.shape[1]
    ranks = lax.axis_size("tokens")
    total = rows * ranks
    group = lax.axis_size("tensor")
    rank = lax.axis_index("tensor")
    me = lax.axis_index("tokens")
    own = me * rows
    bf16, f32 = jnp.bfloat16, jnp.float32

    cross = lambda x, d: lax.ppermute(x, "tokens", [(i, i ^ d) for i in range(ranks)])

    def everyone(x, first, second, third):
        x_side = first(cross(x, 2))
        pair = second(jnp.concatenate([x, x_side], axis=0))
        y_side = [cross(pair, 4 * y) for y in (1, 2, 3)]
        core = cross(third(jnp.concatenate([pair] + y_side, axis=0)), 1)
        return (x, x_side, *y_side, core)

    def after(*others):
        return lambda v: lax.optimization_barrier((v, others))[0]

    flip = [(i, i ^ 1) for i in range(group)]
    up = [(i, (i + 2) % group) for i in range(group)]
    down = [(i, (i - 2) % group) for i in range(group)]
    send = functools.partial(lax.ppermute, axis_name="tensor")
    n = part // 2
    low = send(hidden, perm=up)
    high = send(hidden, perm=down)
    other = send(hidden, perm=flip)
    places = positions[None, :]
    packed, early, info = pl.pallas_call(
        functools.partial(pack_kernel, rows),
        out_shape=(
            jax.ShapeDtypeStruct((rows + TAIL, HD), bf16),
            jax.ShapeDtypeStruct((1, rows), jnp.int32),
            jax.ShapeDtypeStruct((2,), jnp.int32),
        ),
        in_specs=[vmem()] * 2,
        out_specs=(vmem(), vmem(), smem()),
        name="pack",
    )(key_codes, places)
    book = codebook.T

    mate = rank ^ 1
    turn = lambda x, by: (x + by) % group
    shard = [rank, turn(rank, -2), turn(rank, 2), mate]
    shard += [turn(rank, 4), turn(mate, -2), turn(mate, 2), turn(mate, 4)]
    place = jnp.stack(shard).astype(jnp.int32)

    y_side = [cross(packed, 4 * y) for y in (1, 2, 3)]
    column = jnp.concatenate([packed] + y_side, axis=0)
    x_side = cross(column, 2)
    low, high, other = after(column)((low, high, other))
    far_a = send(low[:, :n], perm=up)
    far_b = send(high[:, n:], perm=down)
    other_low = send(other, perm=up)
    other_high = send(other, perm=down)
    other_far_a = send(far_a, perm=flip)
    other_far_b = send(far_b, perm=flip)

    half = group // 2
    low, high, other = after(far_a, far_b)((low, high, other))
    q_sum, kv_sum = pl.pallas_call(
        functools.partial(project_kernel, half, part),
        out_shape=(jax.ShapeDtypeStruct((rows, width), f32), jax.ShapeDtypeStruct((rows, 2 * HD), f32)),
        in_specs=[smem()] + [anywhere()] * (3 + half),
        out_specs=(vmem(),) * 2,
        scratch_shapes=[
            pltpu.VMEM((half, rows, part), bf16),
            pltpu.VMEM((half, part, width), bf16),
            pltpu.VMEM((half, part, 2 * HD), bf16),
            pltpu.SemaphoreType.DMA((4 * half,)),
        ],
        compiler_params=pltpu.CompilerParams(vmem_limit_bytes=50 << 20),
        cost_estimate=cost(1 << 34, 0),
        name="project",
    )(place, w_query, w_key, w_value, hidden, low, high, other)
    core = cross(jnp.concatenate([column, x_side], axis=0), 1)
    packed = (packed, *y_side, x_side, core)

    rest = [far_a, far_b, other_low, other_high, other_far_a, other_far_b]
    value = pl.pallas_call(
        functools.partial(value_kernel, half, half, part),
        out_shape=jax.ShapeDtypeStruct((rows, HD), bf16),
        in_specs=[smem()] + [anywhere()] * (2 + len(rest)),
        out_specs=vmem(),
        scratch_shapes=[
            pltpu.VMEM((rows, half * part), bf16),
            pltpu.VMEM((half, part, HD), bf16),
            pltpu.VMEM((rows, HD), f32),
            pltpu.SemaphoreType.DMA((half + len(rest) + 1,)),
        ],
        compiler_params=pltpu.CompilerParams(vmem_limit_bytes=50 << 20),
        cost_estimate=cost(0, 0),
        name="value",
    )(place, w_value, kv_sum, *rest)

    def prep(near, book, *pieces):
        few = ranks // 2
        shapes = [(few, rows, HD)] * 4
        kinds = [bf16, f32, f32, bf16]
        return pl.pallas_call(
            functools.partial(prep_kernel, near, rows, few, levels),
            out_shape=[jax.ShapeDtypeStruct(size, kind) for size, kind in zip(shapes, kinds)]
            + [jax.ShapeDtypeStruct((heads, HD, rows), bf16)] * near,
            in_specs=[vmem()] + [anywhere()] * len(pieces),
            out_specs=[anywhere()] * 4 + [vmem()] * near,
            scratch_shapes=[pltpu.VMEM((few * (rows + TAIL), HD), bf16)]
            + [pltpu.VMEM(size, kind) for size, kind in zip(shapes, kinds)]
            + [pltpu.SemaphoreType.DMA((few + 1,)), pltpu.SemaphoreType.DMA((4,))]
            + [pltpu.VMEM((rows, width), bf16)] * near,
            compiler_params=pltpu.CompilerParams(vmem_limit_bytes=58 << 20),
            cost_estimate=cost(0 if near else 1 << 32, 0),
            name="prep",
        )(book, *pieces)

    *near, cot_t = prep(True, after(kv_sum)(book), *packed[:5], cotangent)
    distant = prep(False, after(value)(book), packed[5])
    keys = distant[0]

    count = heads * 3 // 8
    totals = []

    def second(pair):
        pair, ready = lax.optimization_barrier((pair, place))
        found = pl.pallas_call(
            functools.partial(
                stats_kernel, count, heads, rows, levels, levels / total, half, half, part
            ),
            out_shape=(
                jax.ShapeDtypeStruct((heads, rows, HD), bf16),
                jax.ShapeDtypeStruct((heads, HD, rows), bf16),
                jax.ShapeDtypeStruct((count, rows), f32),
                jax.ShapeDtypeStruct((levels, HD), f32),
            ),
            in_specs=[smem()] * 2 + [vmem()] * 3 + [anywhere()] * (8 + len(rest)),
            out_specs=(vmem(),) * 4,
            scratch_shapes=[pltpu.VMEM((count, rows), f32)] * 2
            + [pltpu.VMEM((rows, HD), f32)] * 2
            + [
                pltpu.VMEM((ranks // 2, 2, rows, HD), bf16),
                pltpu.VMEM((rows, half * part), bf16),
                pltpu.VMEM((half, part, width), bf16),
                pltpu.VMEM((half, part, HD), bf16),
                pltpu.VMEM((rows, width), f32),
                pltpu.VMEM((rows, HD), f32),
                pltpu.SemaphoreType.DMA((len(rest),)),
                pltpu.SemaphoreType.DMA((2 * half,)),
                pltpu.SemaphoreType.DMA((6,)),
            ],
            compiler_params=pltpu.CompilerParams(vmem_limit_bytes=50 << 20),
            cost_estimate=cost(1 << 34, 0),
            name="stats",
        )(
            ready, info, early, key_codes, book, near[1], near[2], near[0], distant[0],
            q_sum, kv_sum, w_query, w_key, *rest,
        )
        totals.extend(found)
        return pair

    values = everyone(value, after(keys), second, lambda v: after(totals[2])(v))
    q_rot, q_t, log_total_0, init = totals
    late, _ = lax.optimization_barrier((q_t, values[2:5]))
    log_total_1 = pl.pallas_call(
        functools.partial(late_stats_kernel, count, heads - count, rows),
        out_shape=jax.ShapeDtypeStruct((heads - count, rows), f32),
        in_specs=[smem()] + [vmem()] * 2 + [anywhere()] * 2,
        out_specs=vmem(),
        scratch_shapes=[pltpu.VMEM((heads - count, rows), f32)] * 2
        + [pltpu.VMEM((ranks // 2, 2, rows, HD), bf16), pltpu.SemaphoreType.DMA((2,))],
        compiler_params=pltpu.CompilerParams(vmem_limit_bytes=32 << 20),
        cost_estimate=cost(1 << 34, 0),
        name="stats_late",
    )(info, early, late, near[0], distant[0])

    most = total // BLOCK
    attention_out, local = pl.pallas_call(
        functools.partial(grad_kernel, heads, rows, levels),
        out_shape=(
            jax.ShapeDtypeStruct((rows, width), bf16),
            jax.ShapeDtypeStruct((levels, HD), f32),
        ),
        in_specs=[smem()] + [vmem()] * 8 + [anywhere()] * 14,
        out_specs=(vmem(),) * 2,
        scratch_shapes=[
            pltpu.VMEM((min(most, 7), heads, BLOCK, rows), f32),
            pltpu.VMEM((heads, rows, HD), f32),
            pltpu.VMEM((heads, rows), f32),
            pltpu.VMEM((levels, 8, HD), f32),
            pltpu.VMEM((total, HD), bf16),
            pltpu.VMEM((ranks // 2, 2, rows, HD), bf16),
            pltpu.VMEM((ranks // 2, 2, rows, HD), f32),
            pltpu.VMEM((ranks // 2, 2, rows, HD), f32),
            pltpu.VMEM((ranks // 2, 2, rows, HD), bf16),
            pltpu.VMEM((BLOCK, HD), f32),
            pltpu.SemaphoreType.DMA((24,)),
        ],
        compiler_params=pltpu.CompilerParams(vmem_limit_bytes=44 << 20),
        cost_estimate=cost(8 * rows * width * total, 8 << 20),
        name="grad",
    )(
        info, q_rot, q_t, log_total_0, log_total_1, early, cotangent, cot_t, init,
        *[table for both in zip(near, distant) for table in both], *values,
    )
    for d in (1, 2, 4, 12):
        local = local + cross(local, d)
    return (attention_out, local.T)


def solution(mesh):
    placed = (
        P("tokens", "tensor"),
        P(None, "tensor"),
        P(None, "tensor"),
        P(None, "tensor"),
        P("tokens", "tensor"),
        P("tensor", None),
        P("tokens"),
        P("tokens", "tensor"),
    )
    return jax.shard_map(
        shards,
        mesh=mesh,
        in_specs=placed,
        out_specs=(P("tokens", "tensor"), P("tensor", None)),
        check_vma=False,
    )
```

```python
import functools
import math

import jax
import jax.numpy as jnp
from jax import lax
from jax.experimental import pallas as pl
from jax.experimental.pallas import tpu as pltpu
from jax.sharding import PartitionSpec as P

HD = 128
ROPE_BASE = 500000.0
NEG_BIG = -1e30
LOG2E = math.log2(math.e)
SCALE = 1.0 / math.sqrt(HD)
BLOCK = 512
NN = (((1,), (0,)), ((), ()))
TN = (((0,), (0,)), ((), ()))
TAIL = 16
STRIP = 32


def sincos(angle):
    turns = jnp.floor(angle * (2.0 / math.pi) + 0.5)
    r = angle - turns * 1.5703125
    r = r - turns * 4.837512969970703125e-4
    r = r - turns * 7.54978995489188216e-8
    z = r * r
    s = ((-1.9515295891e-4 * z + 8.3321608736e-3) * z - 1.6666654611e-1) * z * r + r
    c = ((2.443315711809948e-5 * z - 1.388731625493765e-3) * z + 4.166664568298827e-2) * z * z
    c = c - 0.5 * z + 1.0
    quadrant = turns.astype(jnp.int32)
    odd = (quadrant & 1) == 1
    sine = jnp.where(odd, c, s)
    cosine = jnp.where(odd, s, c)
    sine = jnp.where((quadrant & 2) == 0, sine, -sine)
    cosine = jnp.where(((quadrant + 1) & 2) == 0, cosine, -cosine)
    return sine, cosine


def slots(pieces):
    own, x, y1, y2, y3, core = pieces
    found = [(0, own, 0), (2, x, 0)]
    for y, ref in ((1, y1), (2, y2), (3, y3)):
        found += [(4 * y, ref, 0), (4 * y + 2, ref, 1)]
    return found + [(2 * j + 1, core, j) for j in range(8)]


def token_rank():
    return lax.axis_index("tokens")


def pack_kernel(rows, key_codes, positions, packed, early, info):
    packed[:rows, :] = key_codes[...].astype(jnp.float32).astype(jnp.bfloat16)
    place = positions[...]
    high, low = place & ~63, place & 63
    wide = [x[:, j * HD : (j + 1) * HD] for x in (high, low) for j in range(rows // HD)]
    blank = jnp.zeros((TAIL - len(wide), HD), jnp.int32)
    tail = jnp.concatenate(wide + [blank], axis=0)
    packed[rows:, :] = tail.astype(jnp.float32).astype(jnp.bfloat16)
    index = token_rank() * rows + lax.broadcasted_iota(jnp.int32, (1, rows), 1)
    first = index - place
    early[...] = first
    first = first.astype(jnp.float32)
    info[0] = jnp.min(first).astype(jnp.int32) // BLOCK
    info[1] = jnp.max(first).astype(jnp.int32)


def prep_kernel(
    near, rows, ranks, levels,
    book, *refs,
):
    pieces = refs[:5] if near else refs[:1]
    if near:
        cot_f, cot_t, cot = refs[5], refs[10], refs[-1]
        refs = refs[:10] + refs[11:-1]
    keys_f, cos_f, sin_f, codes_f, packed_s, keys, cos_k, sin_k, codes, sems, out_sems = refs[-11:]
    me = token_rank()
    tall = rows + TAIL
    if near:
        loading = pltpu.make_async_copy(cot_f, cot, sems.at[ranks])
        loading.start()
    if near:
        found = [(2 * j, ref, 0) for j, ref in enumerate(pieces[:4])]
        found += [(2 * j + 1, pieces[4], j) for j in range(4)]
    else:
        found = [(2 * j if j < 4 else 2 * (j - 4) + 1, pieces[0], j) for j in range(8)]
    copies = []
    for j, (bits, ref, at) in enumerate(found):
        start = pl.multiple_of(((me // 2) ^ bits) * tall, TAIL)
        copies.append(
            pltpu.make_async_copy(
                ref.at[at * tall : (at + 1) * tall, :], packed_s.at[pl.ds(start, tall), :], sems.at[j]
            )
        )
    for copy in copies:
        copy.start()
    for copy in copies:
        copy.wait()
    eye = lax.broadcasted_iota(jnp.int32, (HD, HD), 0) == lax.broadcasted_iota(
        jnp.int32, (HD, HD), 1
    )
    left = lax.broadcasted_iota(jnp.int32, (STRIP, HD), 1) < HD // 2
    ones = jnp.ones((2 * HD, HD), jnp.bfloat16)
    sides = rows // HD
    outs = [(keys, keys_f), (cos_k, cos_f), (sin_k, sin_f), (codes, codes_f)]

    inverse = jnp.exp(
        (lax.broadcasted_iota(jnp.int32, (1, HD), 1) % (HD // 2)).astype(jnp.float32)
        * (-2.0 * math.log(ROPE_BASE) / HD)
    )

    def prep_strip(i, part, strip, places, source):
        rows_of = slice(strip, strip + STRIP)
        place = jnp.where(left, places[part][rows_of, :], places[part + 1][rows_of, :])
        sine, cosine = sincos(place * inverse)
        sine_r, cosine_r = pltpu.roll(sine, HD // 2, 1), pltpu.roll(cosine, HD // 2, 1)
        tables = (
            (jnp.where(left, cosine, cosine_r), jnp.where(left, -sine, sine_r)),
            (jnp.where(left, cosine_r, cosine), jnp.where(left, -sine_r, sine)),
        )
        for side, (cosine, sine) in enumerate(tables):
            at = (part + side) * HD + strip
            target = pl.ds(at, STRIP)
            cos_k[i, target, :] = cosine
            sin_k[i, target, :] = sine
            raw = packed_s[pl.ds(source + at, STRIP), :]
            codes[i, target, :] = raw
            code = raw.astype(jnp.float32).astype(jnp.int32)
            layer = [book[e : e + 1, :] for e in range(levels)]
            bit = 1
            while len(layer) > 1:
                on = (code & bit) != 0
                layer = [jnp.where(on, layer[j + 1], layer[j]) for j in range(0, len(layer), 2)]
                bit *= 2
            deq = layer[0]
            turned = deq * cosine + pltpu.roll(deq, HD // 2, 1) * sine
            keys[i, target, :] = turned.astype(jnp.bfloat16)

    @pl.loop(0, ranks)
    def _(i):
        source = pl.multiple_of(i * tall, TAIL)
        tail = packed_s[pl.ds(source + rows, TAIL), :].astype(jnp.float32)
        places = []
        for part in range(sides):
            high = jnp.where(eye, tail[part : part + 1, :], 0.0)
            low = jnp.where(eye, tail[sides + part : sides + part + 1, :], 0.0)
            digits = jnp.concatenate([high, low], axis=1).astype(jnp.bfloat16)
            places.append(lax.dot_general(digits, ones, NN, preferred_element_type=jnp.float32))
        for part in range(0, sides, 2):
            for strip in range(0, HD, STRIP):
                prep_strip(i, part, strip, places, source)
        for j, (ref, full) in enumerate(outs):
            pltpu.make_async_copy(ref.at[i], full.at[i], out_sems.at[j]).start()

    if near:
        loading.wait()
        for h in range(cot_t.shape[0]):
            cot_t[h] = cot[:, h * HD : (h + 1) * HD].T
    for j, (ref, full) in enumerate(outs):
        pltpu.make_async_copy(ref, full, out_sems.at[j]).wait()


def shard_rows(place, n, part):
    return pl.ds(pl.multiple_of(place[n] * part, part), part)


def interleave(near, distant, ref, sem):
    core = token_rank() % 2
    return [
        pltpu.make_async_copy(half, ref.at[:, core ^ j], sem(j))
        for j, half in enumerate((near, distant))
    ]


def fetch(pieces, x_s, sem):
    copies, at = [], 0
    for piece in pieces:
        width = piece.shape[1]
        copies.append(pltpu.make_async_copy(piece, x_s.at[:, at : at + width], sem(len(copies))))
        at += width
    return copies


def project_kernel(
    count, part, place, wq, wk, wv, *refs,
):
    pieces, (q_out, kv_out, x_s, wq_s, wkv_s, sems) = refs[:count], refs[count:]
    copies = []
    for n, piece in enumerate(pieces):
        rows = shard_rows(place, n, part)
        copies.append([
            pltpu.make_async_copy(piece, x_s.at[n], sems.at[4 * n]),
            pltpu.make_async_copy(wq.at[rows, :], wq_s.at[n], sems.at[4 * n + 1]),
            pltpu.make_async_copy(wk.at[rows, :], wkv_s.at[n, :, :HD], sems.at[4 * n + 2]),
            pltpu.make_async_copy(wv.at[rows, :], wkv_s.at[n, :, HD:], sems.at[4 * n + 3]),
        ])
        for copy in copies[-1]:
            copy.start()
    for n in range(count):
        for copy in copies[n]:
            copy.wait()
        x = x_s[n]
        q = jnp.dot(x, wq_s[n], preferred_element_type=jnp.float32)
        kv = jnp.dot(x, wkv_s[n], preferred_element_type=jnp.float32)
        q_out[...] = q if n == 0 else q_out[...] + q
        kv_out[...] = kv if n == 0 else kv_out[...] + kv


def value_kernel(first, count, part, place, w, before, *refs):
    pieces, (value, x_s, w_s, before_s, sems) = refs[:-5], refs[-5:]
    copies = fetch(pieces, x_s, lambda j: sems.at[j])
    copies.append(pltpu.make_async_copy(before.at[:, HD:], before_s, sems.at[len(copies)]))
    for n in range(count):
        copies.append(
            pltpu.make_async_copy(w.at[shard_rows(place, first + n, part), :], w_s.at[n], sems.at[len(copies)])
        )
    for copy in copies:
        copy.start()
    for copy in copies:
        copy.wait()
    total = before_s[...]
    for n in range(count):
        total += jnp.dot(x_s[:, n * part : (n + 1) * part], w_s[n], preferred_element_type=jnp.float32)
    value[...] = total.astype(jnp.bfloat16)


def visible_block(base, block, own, earliest, rows):
    key = base + lax.broadcasted_iota(jnp.int32, (block, rows), 0)
    query = own + lax.broadcasted_iota(jnp.int32, (block, rows), 1)
    return (key <= query) & (key >= earliest)


def over_blocks(own, info, rows, body):
    first, edge = info[0], info[1]
    last = (own + rows + BLOCK - 1) // BLOCK

    @pl.loop(first, last)
    def _(b):
        masked = (b * BLOCK < edge) | (b * BLOCK + BLOCK > own)

        @pl.when(masked)
        def _():
            body(b, True)

        @pl.when(jnp.logical_not(masked))
        def _():
            body(b, False)


def stats_kernel(
    heads, wide, rows, levels, weight, first, count, part,
    place, info, early, codes, book, cos_k, sin_k, keys_n, keys_d, q_before, kv_before, wq, wk, *refs,
):
    pieces = refs[:-17]
    (
        q_rot, q_t, log_total, bins,
        peak_s, mass_s, cos_q, sin_q, keys, x_s, wq_s, wk_s, q_s, true_s, x_sems, w_sems, sems,
    ) = refs[-17:]
    own = token_rank() * rows
    mine = token_rank() // 2
    loads = fetch(pieces, x_s, lambda j: x_sems.at[j])
    weights = []
    for n in range(count):
        at = shard_rows(place, first + n, part)
        weights.append([
            pltpu.make_async_copy(wq.at[at, :], wq_s.at[n], w_sems.at[2 * n]),
            pltpu.make_async_copy(wk.at[at, :], wk_s.at[n], w_sems.at[2 * n + 1]),
        ])
    before = [
        pltpu.make_async_copy(q_before, q_s, sems.at[0]),
        pltpu.make_async_copy(kv_before.at[:, :HD], true_s, sems.at[1]),
    ]
    tables = [
        pltpu.make_async_copy(cos_k.at[mine], cos_q, sems.at[2]),
        pltpu.make_async_copy(sin_k.at[mine], sin_q, sems.at[3]),
    ] + interleave(keys_n, keys_d, keys, lambda j: sems.at[4 + j])
    for copy in before + loads + sum(weights, []) + tables:
        copy.start()
    for copy in before + loads:
        copy.wait()
    for n in range(count):
        for copy in weights[n]:
            copy.wait()
        x = x_s[:, n * part : (n + 1) * part]
        q_s[...] += jnp.dot(x, wq_s[n], preferred_element_type=jnp.float32)
        true_s[...] += jnp.dot(x, wk_s[n], preferred_element_type=jnp.float32)
    code = codes[...]
    for level in range(levels):
        entry = weight * (book[level : level + 1, :] - true_s[...])
        bins[level : level + 1, :] = jnp.sum(
            jnp.where(code == level, entry, 0.0), axis=0, keepdims=True
        )
    for copy in tables:
        copy.wait()
    for h in range(wide):
        x = q_s[:, h * HD : (h + 1) * HD]
        turned = (x * cos_q[...] + pltpu.roll(x, HD // 2, 1) * sin_q[...]).astype(jnp.bfloat16)
        q_rot[h] = turned
        q_t[h] = turned.T
    scan_totals(own, info, early, rows, 0, heads, q_t, keys, peak_s, mass_s, log_total)


def scan_totals(own, info, early, rows, begin, heads, q_t, keys, peak_s, mass_s, log_total):
    peak_s[...] = jnp.full_like(peak_s, NEG_BIG)
    mass_s[...] = jnp.zeros_like(mass_s)

    def body(b, masked):
        base = pl.multiple_of(b * BLOCK, BLOCK)
        k = keys[b].reshape(BLOCK, HD)
        if masked:
            seen = visible_block(base, BLOCK, own, early[...], rows)
        for h in range(heads):
            t = lax.dot_general(k, q_t[begin + h], NN, preferred_element_type=jnp.float32)
            t = t * (SCALE * LOG2E)
            if masked:
                t = jnp.where(seen, t, NEG_BIG)
            old = peak_s[h : h + 1, :]
            new = jnp.maximum(old, jnp.max(t, axis=0, keepdims=True))
            fresh = jnp.sum(jnp.exp2(t - new), axis=0, keepdims=True)
            mass_s[h : h + 1, :] = mass_s[h : h + 1, :] * jnp.exp2(old - new) + fresh
            peak_s[h : h + 1, :] = new

    over_blocks(own, info, rows, body)
    log_total[...] = peak_s[...] + jnp.log(mass_s[...]) * LOG2E


def late_stats_kernel(
    begin, heads, rows, info, early, q_t, keys_n, keys_d, log_total, peak_s, mass_s, keys, sems,
):
    copies = interleave(keys_n, keys_d, keys, lambda j: sems.at[j])
    for copy in copies:
        copy.start()
    for copy in copies:
        copy.wait()
    own = token_rank() * rows
    scan_totals(own, info, early, rows, begin, heads, q_t, keys, peak_s, mass_s, log_total)


def grad_kernel(
    heads, rows, levels,
    info, q_rot, q_t, log_total_0, log_total_1, early, cot, cot_t, init,
    keys_n, keys_d, cos_n, cos_d, sin_n, sin_d, codes_n, codes_d, v_own, v_x, v_y1, v_y2, v_y3, v_core,
    out, bins, probs_s, out_s, delta_s, acc_s, values, keys, cos_k, sin_k, codes, held, sems,
):
    me = token_rank()
    own, first = me * rows, info[0]
    part = heads // 2
    early_heads = log_total_0.shape[0]
    log_total = [log_total_0.at[h : h + 1, :] for h in range(early_heads)]
    log_total += [log_total_1.at[h : h + 1, :] for h in range(heads - early_heads)]
    copies = interleave(keys_n, keys_d, keys, lambda j: sems.at[16 + j])
    for j, (bits, ref, at) in enumerate(slots((v_own, v_x, v_y1, v_y2, v_y3, v_core))):
        start = pl.multiple_of((me ^ bits) * rows, rows)
        copies.append(
            pltpu.make_async_copy(
                ref.at[at * rows : (at + 1) * rows, :], values.at[pl.ds(start, rows), :], sems.at[j]
            )
        )
    late = interleave(cos_n, cos_d, cos_k, lambda j: sems.at[18 + j])
    late += interleave(sin_n, sin_d, sin_k, lambda j: sems.at[20 + j])
    late += interleave(codes_n, codes_d, codes, lambda j: sems.at[22 + j])
    for copy in copies + late:
        copy.start()
    out_s[...] = jnp.zeros_like(out_s)
    for copy in copies:
        copy.wait()

    def forward(b, masked):
        base = pl.multiple_of(b * BLOCK, BLOCK)
        k = keys[b].reshape(BLOCK, HD)
        v = values[pl.ds(base, BLOCK), :]
        if masked:
            seen = visible_block(base, BLOCK, own, early[...], rows)
        for h in range(heads):
            s = lax.dot_general(k, q_t[h], NN, preferred_element_type=jnp.float32)
            p = jnp.exp2(s * (SCALE * LOG2E) - log_total[h][...])
            if masked:
                p = jnp.where(seen, p, 0.0)
            probs_s[b - first, h] = p
            out_s[h] += lax.dot_general(
                p.astype(jnp.bfloat16), v, TN, preferred_element_type=jnp.float32
            )

    over_blocks(own, info, rows, forward)
    for h in range(heads):
        o = out_s[h].astype(jnp.bfloat16)
        out[:, h * HD : (h + 1) * HD] = o
        prod = cot[:, h * HD : (h + 1) * HD].astype(jnp.float32) * o.astype(jnp.float32)
        delta_s[h : h + 1, :] = jnp.sum(prod.T, axis=0, keepdims=True)
    acc_s[...] = jnp.zeros_like(acc_s)
    last = (own + rows + BLOCK - 1) // BLOCK
    for copy in late:
        copy.wait()

    def add_bins(b, dk):
        dk = dk * SCALE
        cosine, sine = cos_k[b].reshape(BLOCK, HD), sin_k[b].reshape(BLOCK, HD)
        g = dk * cosine - pltpu.roll(dk, HD // 2, 1) * sine
        code = codes[b].reshape(BLOCK, HD).astype(jnp.float32)
        for level in range(levels):
            chosen = jnp.where(code == level, g, 0.0)
            acc_s[level] += jnp.sum(chosen.reshape(BLOCK // 8, 8, HD), axis=0)

    held[...] = jnp.zeros_like(held)

    @pl.loop(first, last)
    def _(b):
        base = pl.multiple_of(b * BLOCK, BLOCK)
        v = values[pl.ds(base, BLOCK), :]
        add_bins(jnp.maximum(b - 1, first), held[...])
        dk = jnp.zeros((BLOCK, HD), jnp.float32)
        for h in range(heads):
            dp = lax.dot_general(v, cot_t[h], NN, preferred_element_type=jnp.float32)
            ds = (probs_s[b - first, h] * (dp - delta_s[h : h + 1, :])).astype(jnp.bfloat16)
            dk = dk + lax.dot_general(ds, q_rot[h], NN, preferred_element_type=jnp.float32)
        held[...] = dk

    add_bins(last - 1, held[...])
    bins[...] = init[...] + jnp.sum(acc_s[...], axis=1)


def anywhere():
    return pl.BlockSpec(memory_space=pl.ANY)


def vmem():
    return pl.BlockSpec(memory_space=pltpu.VMEM)


def smem():
    return pl.BlockSpec(memory_space=pltpu.SMEM)


def cost(flops, size):
    return pl.CostEstimate(flops=flops, bytes_accessed=size, transcendentals=0)


def shards(hidden, w_query, w_key, w_value, key_codes, codebook, positions, cotangent):
    rows, part = hidden.shape
    width = w_query.shape[1]
    heads = width // HD
    levels = codebook.shape[1]
    ranks = lax.axis_size("tokens")
    total = rows * ranks
    group = lax.axis_size("tensor")
    rank = lax.axis_index("tensor")
    me = lax.axis_index("tokens")
    own = me * rows
    bf16, f32 = jnp.bfloat16, jnp.float32

    cross = lambda x, d: lax.ppermute(x, "tokens", [(i, i ^ d) for i in range(ranks)])

    def everyone(x, first, second, third):
        x_side = first(cross(x, 2))
        pair = second(jnp.concatenate([x, x_side], axis=0))
        y_side = [cross(pair, 4 * y) for y in (1, 2, 3)]
        core = cross(third(jnp.concatenate([pair] + y_side, axis=0)), 1)
        return (x, x_side, *y_side, core)

    def after(*others):
        return lambda v: lax.optimization_barrier((v, others))[0]

    flip = [(i, i ^ 1) for i in range(group)]
    up = [(i, (i + 2) % group) for i in range(group)]
    down = [(i, (i - 2) % group) for i in range(group)]
    send = functools.partial(lax.ppermute, axis_name="tensor")
    n = part // 2
    low = send(hidden, perm=up)
    high = send(hidden, perm=down)
    other = send(hidden, perm=flip)
    places = positions[None, :]
    packed, early, info = pl.pallas_call(
        functools.partial(pack_kernel, rows),
        out_shape=(
            jax.ShapeDtypeStruct((rows + TAIL, HD), bf16),
            jax.ShapeDtypeStruct((1, rows), jnp.int32),
            jax.ShapeDtypeStruct((2,), jnp.int32),
        ),
        in_specs=[vmem()] * 2,
        out_specs=(vmem(), vmem(), smem()),
        name="pack",
    )(key_codes, places)
    book = codebook.T

    mate = rank ^ 1
    turn = lambda x, by: (x + by) % group
    shard = [rank, turn(rank, -2), turn(rank, 2), mate]
    shard += [turn(rank, 4), turn(mate, -2), turn(mate, 2), turn(mate, 4)]
    place = jnp.stack(shard).astype(jnp.int32)

    y_side = [cross(packed, 4 * y) for y in (1, 2, 3)]
    column = jnp.concatenate([packed] + y_side, axis=0)
    x_side = cross(column, 2)
    low, high, other = after(column)((low, high, other))
    far_a = send(low[:, :n], perm=up)
    far_b = send(high[:, n:], perm=down)
    other_low = send(other, perm=up)
    other_high = send(other, perm=down)
    other_far_a = send(far_a, perm=flip)
    other_far_b = send(far_b, perm=flip)

    half = group // 2
    low, high, other = after(far_a, far_b)((low, high, other))
    q_sum, kv_sum = pl.pallas_call(
        functools.partial(project_kernel, half, part),
        out_shape=(jax.ShapeDtypeStruct((rows, width), f32), jax.ShapeDtypeStruct((rows, 2 * HD), f32)),
        in_specs=[smem()] + [anywhere()] * (3 + half),
        out_specs=(vmem(),) * 2,
        scratch_shapes=[
            pltpu.VMEM((half, rows, part), bf16),
            pltpu.VMEM((half, part, width), bf16),
            pltpu.VMEM((half, part, 2 * HD), bf16),
            pltpu.SemaphoreType.DMA((4 * half,)),
        ],
        compiler_params=pltpu.CompilerParams(vmem_limit_bytes=50 << 20),
        cost_estimate=cost(1 << 34, 0),
        name="project",
    )(place, w_query, w_key, w_value, hidden, low, high, other)
    x_side = after(far_a, far_b)(x_side)
    core = cross(jnp.concatenate([column, x_side], axis=0), 1)
    packed = (packed, *y_side, x_side, core)

    rest = [far_a, far_b, other_low, other_high, other_far_a, other_far_b]
    value = pl.pallas_call(
        functools.partial(value_kernel, half, half, part),
        out_shape=jax.ShapeDtypeStruct((rows, HD), bf16),
        in_specs=[smem()] + [anywhere()] * (2 + len(rest)),
        out_specs=vmem(),
        scratch_shapes=[
            pltpu.VMEM((rows, half * part), bf16),
            pltpu.VMEM((half, part, HD), bf16),
            pltpu.VMEM((rows, HD), f32),
            pltpu.SemaphoreType.DMA((half + len(rest) + 1,)),
        ],
        compiler_params=pltpu.CompilerParams(vmem_limit_bytes=50 << 20),
        cost_estimate=cost(0, 0),
        name="value",
    )(place, w_value, kv_sum, *rest)

    def prep(near, book, *pieces):
        few = ranks // 2
        shapes = [(few, rows, HD)] * 4
        kinds = [bf16, f32, f32, bf16]
        return pl.pallas_call(
            functools.partial(prep_kernel, near, rows, few, levels),
            out_shape=[jax.ShapeDtypeStruct(size, kind) for size, kind in zip(shapes, kinds)]
            + [jax.ShapeDtypeStruct((heads, HD, rows), bf16)] * near,
            in_specs=[vmem()] + [anywhere()] * len(pieces),
            out_specs=[anywhere()] * 4 + [vmem()] * near,
            scratch_shapes=[pltpu.VMEM((few * (rows + TAIL), HD), bf16)]
            + [pltpu.VMEM(size, kind) for size, kind in zip(shapes, kinds)]
            + [pltpu.SemaphoreType.DMA((few + 1,)), pltpu.SemaphoreType.DMA((4,))]
            + [pltpu.VMEM((rows, width), bf16)] * near,
            compiler_params=pltpu.CompilerParams(vmem_limit_bytes=58 << 20),
            cost_estimate=cost(0 if near else 1 << 32, 0),
            name="prep",
        )(book, *pieces)

    *near, cot_t = prep(True, after(kv_sum)(book), *packed[:5], cotangent)
    distant = prep(False, after(value)(book), packed[5])
    keys = distant[0]

    count = heads * 3 // 8
    totals = []

    def second(pair):
        pair, ready = lax.optimization_barrier((pair, place))
        found = pl.pallas_call(
            functools.partial(
                stats_kernel, count, heads, rows, levels, levels / total, half, half, part
            ),
            out_shape=(
                jax.ShapeDtypeStruct((heads, rows, HD), bf16),
                jax.ShapeDtypeStruct((heads, HD, rows), bf16),
                jax.ShapeDtypeStruct((count, rows), f32),
                jax.ShapeDtypeStruct((levels, HD), f32),
            ),
            in_specs=[smem()] * 2 + [vmem()] * 3 + [anywhere()] * (8 + len(rest)),
            out_specs=(vmem(),) * 4,
            scratch_shapes=[pltpu.VMEM((count, rows), f32)] * 2
            + [pltpu.VMEM((rows, HD), f32)] * 2
            + [
                pltpu.VMEM((ranks // 2, 2, rows, HD), bf16),
                pltpu.VMEM((rows, half * part), bf16),
                pltpu.VMEM((half, part, width), bf16),
                pltpu.VMEM((half, part, HD), bf16),
                pltpu.VMEM((rows, width), f32),
                pltpu.VMEM((rows, HD), f32),
                pltpu.SemaphoreType.DMA((len(rest),)),
                pltpu.SemaphoreType.DMA((2 * half,)),
                pltpu.SemaphoreType.DMA((6,)),
            ],
            compiler_params=pltpu.CompilerParams(vmem_limit_bytes=50 << 20),
            cost_estimate=cost(1 << 34, 0),
            name="stats",
        )(
            ready, info, early, key_codes, book, near[1], near[2], near[0], distant[0],
            q_sum, kv_sum, w_query, w_key, *rest,
        )
        totals.extend(found)
        return pair

    values = everyone(value, after(keys), second, lambda v: after(totals[2])(v))
    q_rot, q_t, log_total_0, init = totals
    late, _ = lax.optimization_barrier((q_t, values[2:5]))
    log_total_1 = pl.pallas_call(
        functools.partial(late_stats_kernel, count, heads - count, rows),
        out_shape=jax.ShapeDtypeStruct((heads - count, rows), f32),
        in_specs=[smem()] + [vmem()] * 2 + [anywhere()] * 2,
        out_specs=vmem(),
        scratch_shapes=[pltpu.VMEM((heads - count, rows), f32)] * 2
        + [pltpu.VMEM((ranks // 2, 2, rows, HD), bf16), pltpu.SemaphoreType.DMA((2,))],
        compiler_params=pltpu.CompilerParams(vmem_limit_bytes=32 << 20),
        cost_estimate=cost(1 << 34, 0),
        name="stats_late",
    )(info, early, late, near[0], distant[0])

    most = total // BLOCK
    attention_out, local = pl.pallas_call(
        functools.partial(grad_kernel, heads, rows, levels),
        out_shape=(
            jax.ShapeDtypeStruct((rows, width), bf16),
            jax.ShapeDtypeStruct((levels, HD), f32),
        ),
        in_specs=[smem()] + [vmem()] * 8 + [anywhere()] * 14,
        out_specs=(vmem(),) * 2,
        scratch_shapes=[
            pltpu.VMEM((min(most, 7), heads, BLOCK, rows), f32),
            pltpu.VMEM((heads, rows, HD), f32),
            pltpu.VMEM((heads, rows), f32),
            pltpu.VMEM((levels, 8, HD), f32),
            pltpu.VMEM((total, HD), bf16),
            pltpu.VMEM((ranks // 2, 2, rows, HD), bf16),
            pltpu.VMEM((ranks // 2, 2, rows, HD), f32),
            pltpu.VMEM((ranks // 2, 2, rows, HD), f32),
            pltpu.VMEM((ranks // 2, 2, rows, HD), bf16),
            pltpu.VMEM((BLOCK, HD), f32),
            pltpu.SemaphoreType.DMA((24,)),
        ],
        compiler_params=pltpu.CompilerParams(vmem_limit_bytes=44 << 20),
        cost_estimate=cost(8 * rows * width * total, 8 << 20),
        name="grad",
    )(
        info, q_rot, q_t, log_total_0, log_total_1, early, cotangent, cot_t, init,
        *[table for both in zip(near, distant) for table in both], *values,
    )
    for d in (1, 2, 4, 12):
        local = local + cross(local, d)
    return (attention_out, local.T)


def solution(mesh):
    placed = (
        P("tokens", "tensor"),
        P(None, "tensor"),
        P(None, "tensor"),
        P(None, "tensor"),
        P("tokens", "tensor"),
        P("tensor", None),
        P("tokens"),
        P("tokens", "tensor"),
    )
    return jax.shard_map(
        shards,
        mesh=mesh,
        in_specs=placed,
        out_specs=(P("tokens", "tensor"), P("tensor", None)),
        check_vma=False,
    )
```

```python
import functools
import math

import jax
import jax.numpy as jnp
from jax import lax
from jax.experimental import pallas as pl
from jax.experimental.pallas import tpu as pltpu
from jax.sharding import PartitionSpec as P

HD = 128
ROPE_BASE = 500000.0
NEG_BIG = -1e30
LOG2E = math.log2(math.e)
SCALE = 1.0 / math.sqrt(HD)
BLOCK = 512
NN = (((1,), (0,)), ((), ()))
TN = (((0,), (0,)), ((), ()))
TAIL = 16
STRIP = 32


def sincos(angle):
    turns = jnp.floor(angle * (2.0 / math.pi) + 0.5)
    r = angle - turns * 1.5703125
    r = r - turns * 4.837512969970703125e-4
    r = r - turns * 7.54978995489188216e-8
    z = r * r
    s = ((-1.9515295891e-4 * z + 8.3321608736e-3) * z - 1.6666654611e-1) * z * r + r
    c = ((2.443315711809948e-5 * z - 1.388731625493765e-3) * z + 4.166664568298827e-2) * z * z
    c = c - 0.5 * z + 1.0
    quadrant = turns.astype(jnp.int32)
    odd = (quadrant & 1) == 1
    sine = jnp.where(odd, c, s)
    cosine = jnp.where(odd, s, c)
    sine = jnp.where((quadrant & 2) == 0, sine, -sine)
    cosine = jnp.where(((quadrant + 1) & 2) == 0, cosine, -cosine)
    return sine, cosine


def slots(pieces):
    own, x, y1, y2, y3, core = pieces
    found = [(0, own, 0), (2, x, 0)]
    for y, ref in ((1, y1), (2, y2), (3, y3)):
        found += [(4 * y, ref, 0), (4 * y + 2, ref, 1)]
    return found + [(2 * j + 1, core, j) for j in range(8)]


def token_rank():
    return lax.axis_index("tokens")


def pack_kernel(rows, key_codes, positions, packed, early, info):
    packed[:rows, :] = key_codes[...].astype(jnp.float32).astype(jnp.bfloat16)
    place = positions[...]
    high, low = place & ~63, place & 63
    wide = [x[:, j * HD : (j + 1) * HD] for x in (high, low) for j in range(rows // HD)]
    blank = jnp.zeros((TAIL - len(wide), HD), jnp.int32)
    tail = jnp.concatenate(wide + [blank], axis=0)
    packed[rows:, :] = tail.astype(jnp.float32).astype(jnp.bfloat16)
    index = token_rank() * rows + lax.broadcasted_iota(jnp.int32, (1, rows), 1)
    first = index - place
    early[...] = first
    first = first.astype(jnp.float32)
    info[0] = jnp.min(first).astype(jnp.int32) // BLOCK
    info[1] = jnp.max(first).astype(jnp.int32)


def prep_kernel(
    near, rows, ranks, levels,
    book, *refs,
):
    pieces = refs[:5] if near else refs[:1]
    if near:
        cot_f, cot_t, cot = refs[5], refs[10], refs[-1]
        refs = refs[:10] + refs[11:-1]
    keys_f, cos_f, sin_f, codes_f, packed_s, keys, cos_k, sin_k, codes, sems, out_sems = refs[-11:]
    me = token_rank()
    tall = rows + TAIL
    if near:
        loading = pltpu.make_async_copy(cot_f, cot, sems.at[ranks])
        loading.start()
    if near:
        found = [(2 * j, ref, 0) for j, ref in enumerate(pieces[:4])]
        found += [(2 * j + 1, pieces[4], j) for j in range(4)]
    else:
        found = [(2 * j if j < 4 else 2 * (j - 4) + 1, pieces[0], j) for j in range(8)]
    copies = []
    for j, (bits, ref, at) in enumerate(found):
        start = pl.multiple_of(((me // 2) ^ bits) * tall, TAIL)
        copies.append(
            pltpu.make_async_copy(
                ref.at[at * tall : (at + 1) * tall, :], packed_s.at[pl.ds(start, tall), :], sems.at[j]
            )
        )
    for copy in copies:
        copy.start()
    for copy in copies:
        copy.wait()
    eye = lax.broadcasted_iota(jnp.int32, (HD, HD), 0) == lax.broadcasted_iota(
        jnp.int32, (HD, HD), 1
    )
    left = lax.broadcasted_iota(jnp.int32, (STRIP, HD), 1) < HD // 2
    ones = jnp.ones((2 * HD, HD), jnp.bfloat16)
    sides = rows // HD
    outs = [(keys, keys_f), (cos_k, cos_f), (sin_k, sin_f), (codes, codes_f)]

    inverse = jnp.exp(
        (lax.broadcasted_iota(jnp.int32, (1, HD), 1) % (HD // 2)).astype(jnp.float32)
        * (-2.0 * math.log(ROPE_BASE) / HD)
    )

    def prep_strip(i, part, strip, places, source):
        rows_of = slice(strip, strip + STRIP)
        place = jnp.where(left, places[part][rows_of, :], places[part + 1][rows_of, :])
        sine, cosine = sincos(place * inverse)
        sine_r, cosine_r = pltpu.roll(sine, HD // 2, 1), pltpu.roll(cosine, HD // 2, 1)
        tables = (
            (jnp.where(left, cosine, cosine_r), jnp.where(left, -sine, sine_r)),
            (jnp.where(left, cosine_r, cosine), jnp.where(left, -sine_r, sine)),
        )
        for side, (cosine, sine) in enumerate(tables):
            at = (part + side) * HD + strip
            target = pl.ds(at, STRIP)
            cos_k[i, target, :] = cosine
            sin_k[i, target, :] = sine
            raw = packed_s[pl.ds(source + at, STRIP), :]
            codes[i, target, :] = raw
            code = raw.astype(jnp.float32).astype(jnp.int32)
            layer = [book[e : e + 1, :] for e in range(levels)]
            bit = 1
            while len(layer) > 1:
                on = (code & bit) != 0
                layer = [jnp.where(on, layer[j + 1], layer[j]) for j in range(0, len(layer), 2)]
                bit *= 2
            deq = layer[0]
            turned = deq * cosine + pltpu.roll(deq, HD // 2, 1) * sine
            keys[i, target, :] = turned.astype(jnp.bfloat16)

    @pl.loop(0, ranks)
    def _(i):
        source = pl.multiple_of(i * tall, TAIL)
        tail = packed_s[pl.ds(source + rows, TAIL), :].astype(jnp.float32)
        places = []
        for part in range(sides):
            high = jnp.where(eye, tail[part : part + 1, :], 0.0)
            low = jnp.where(eye, tail[sides + part : sides + part + 1, :], 0.0)
            digits = jnp.concatenate([high, low], axis=1).astype(jnp.bfloat16)
            places.append(lax.dot_general(digits, ones, NN, preferred_element_type=jnp.float32))
        for part in range(0, sides, 2):
            for strip in range(0, HD, STRIP):
                prep_strip(i, part, strip, places, source)
        for j, (ref, full) in enumerate(outs):
            pltpu.make_async_copy(ref.at[i], full.at[i], out_sems.at[j]).start()

    if near:
        loading.wait()
        for h in range(cot_t.shape[0]):
            cot_t[h] = cot[:, h * HD : (h + 1) * HD].T
    for j, (ref, full) in enumerate(outs):
        pltpu.make_async_copy(ref, full, out_sems.at[j]).wait()


def shard_rows(place, n, part):
    return pl.ds(pl.multiple_of(place[n] * part, part), part)


def interleave(near, distant, ref, sem):
    core = token_rank() % 2
    return [
        pltpu.make_async_copy(half, ref.at[:, core ^ j], sem(j))
        for j, half in enumerate((near, distant))
    ]


def fetch(pieces, x_s, sem):
    copies, at = [], 0
    for piece in pieces:
        width = piece.shape[1]
        copies.append(pltpu.make_async_copy(piece, x_s.at[:, at : at + width], sem(len(copies))))
        at += width
    return copies


def project_kernel(
    count, part, place, wq, wk, wv, *refs,
):
    pieces, (q_out, kv_out, x_s, wq_s, wkv_s, sems) = refs[:count], refs[count:]
    copies = []
    for n, piece in enumerate(pieces):
        rows = shard_rows(place, n, part)
        copies.append([
            pltpu.make_async_copy(piece, x_s.at[n], sems.at[4 * n]),
            pltpu.make_async_copy(wq.at[rows, :], wq_s.at[n], sems.at[4 * n + 1]),
            pltpu.make_async_copy(wk.at[rows, :], wkv_s.at[n, :, :HD], sems.at[4 * n + 2]),
            pltpu.make_async_copy(wv.at[rows, :], wkv_s.at[n, :, HD:], sems.at[4 * n + 3]),
        ])
        for copy in copies[-1]:
            copy.start()
    for n in range(count):
        for copy in copies[n]:
            copy.wait()
        x = x_s[n]
        q = jnp.dot(x, wq_s[n], preferred_element_type=jnp.float32)
        kv = jnp.dot(x, wkv_s[n], preferred_element_type=jnp.float32)
        q_out[...] = q if n == 0 else q_out[...] + q
        kv_out[...] = kv if n == 0 else kv_out[...] + kv


def value_kernel(first, count, part, place, w, before, *refs):
    pieces, (value, x_s, w_s, before_s, sems) = refs[:-5], refs[-5:]
    copies = fetch(pieces, x_s, lambda j: sems.at[j])
    copies.append(pltpu.make_async_copy(before.at[:, HD:], before_s, sems.at[len(copies)]))
    for n in range(count):
        copies.append(
            pltpu.make_async_copy(w.at[shard_rows(place, first + n, part), :], w_s.at[n], sems.at[len(copies)])
        )
    for copy in copies:
        copy.start()
    for copy in copies:
        copy.wait()
    total = before_s[...]
    for n in range(count):
        total += jnp.dot(x_s[:, n * part : (n + 1) * part], w_s[n], preferred_element_type=jnp.float32)
    value[...] = total.astype(jnp.bfloat16)


def visible_block(base, block, own, earliest, rows):
    key = base + lax.broadcasted_iota(jnp.int32, (block, rows), 0)
    query = own + lax.broadcasted_iota(jnp.int32, (block, rows), 1)
    return (key <= query) & (key >= earliest)


def over_blocks(own, info, rows, body):
    first, edge = info[0], info[1]
    last = (own + rows + BLOCK - 1) // BLOCK

    @pl.loop(first, last)
    def _(b):
        masked = (b * BLOCK < edge) | (b * BLOCK + BLOCK > own)

        @pl.when(masked)
        def _():
            body(b, True)

        @pl.when(jnp.logical_not(masked))
        def _():
            body(b, False)


def stats_kernel(
    heads, wide, rows, levels, weight, first, count, part,
    place, info, early, codes, book, cos_k, sin_k, keys_n, keys_d, q_before, kv_before, wq, wk, *refs,
):
    pieces = refs[:-17]
    (
        q_rot, q_t, log_total, bins,
        peak_s, mass_s, cos_q, sin_q, keys, x_s, wq_s, wk_s, q_s, true_s, x_sems, w_sems, sems,
    ) = refs[-17:]
    own = token_rank() * rows
    mine = token_rank() // 2
    loads = fetch(pieces, x_s, lambda j: x_sems.at[j])
    weights = []
    for n in range(count):
        at = shard_rows(place, first + n, part)
        weights.append([
            pltpu.make_async_copy(wq.at[at, :], wq_s.at[n], w_sems.at[2 * n]),
            pltpu.make_async_copy(wk.at[at, :], wk_s.at[n], w_sems.at[2 * n + 1]),
        ])
    before = [
        pltpu.make_async_copy(q_before, q_s, sems.at[0]),
        pltpu.make_async_copy(kv_before.at[:, :HD], true_s, sems.at[1]),
    ]
    tables = [
        pltpu.make_async_copy(cos_k.at[mine], cos_q, sems.at[2]),
        pltpu.make_async_copy(sin_k.at[mine], sin_q, sems.at[3]),
    ] + interleave(keys_n, keys_d, keys, lambda j: sems.at[4 + j])
    for copy in before + loads + sum(weights, []) + tables:
        copy.start()
    for copy in before + loads:
        copy.wait()
    for n in range(count):
        for copy in weights[n]:
            copy.wait()
        x = x_s[:, n * part : (n + 1) * part]
        q_s[...] += jnp.dot(x, wq_s[n], preferred_element_type=jnp.float32)
        true_s[...] += jnp.dot(x, wk_s[n], preferred_element_type=jnp.float32)
    code = codes[...]
    for level in range(levels):
        entry = weight * (book[level : level + 1, :] - true_s[...])
        bins[level : level + 1, :] = jnp.sum(
            jnp.where(code == level, entry, 0.0), axis=0, keepdims=True
        )
    for copy in tables:
        copy.wait()
    for h in range(wide):
        x = q_s[:, h * HD : (h + 1) * HD]
        turned = (x * cos_q[...] + pltpu.roll(x, HD // 2, 1) * sin_q[...]).astype(jnp.bfloat16)
        q_rot[h] = turned
        q_t[h] = turned.T
    scan_totals(own, info, early, rows, 0, heads, q_t, keys, peak_s, mass_s, log_total)


def scan_totals(own, info, early, rows, begin, heads, q_t, keys, peak_s, mass_s, log_total):
    peak_s[...] = jnp.full_like(peak_s, NEG_BIG)
    mass_s[...] = jnp.zeros_like(mass_s)

    def body(b, masked):
        base = pl.multiple_of(b * BLOCK, BLOCK)
        k = keys[b].reshape(BLOCK, HD)
        if masked:
            seen = visible_block(base, BLOCK, own, early[...], rows)
        for h in range(heads):
            t = lax.dot_general(k, q_t[begin + h], NN, preferred_element_type=jnp.float32)
            t = t * (SCALE * LOG2E)
            if masked:
                t = jnp.where(seen, t, NEG_BIG)
            old = peak_s[h : h + 1, :]
            new = jnp.maximum(old, jnp.max(t, axis=0, keepdims=True))
            fresh = jnp.sum(jnp.exp2(t - new), axis=0, keepdims=True)
            mass_s[h : h + 1, :] = mass_s[h : h + 1, :] * jnp.exp2(old - new) + fresh
            peak_s[h : h + 1, :] = new

    over_blocks(own, info, rows, body)
    log_total[...] = peak_s[...] + jnp.log(mass_s[...]) * LOG2E


def late_stats_kernel(
    begin, heads, rows, info, early, q_t, keys_n, keys_d, log_total, peak_s, mass_s, keys, sems,
):
    copies = interleave(keys_n, keys_d, keys, lambda j: sems.at[j])
    for copy in copies:
        copy.start()
    for copy in copies:
        copy.wait()
    own = token_rank() * rows
    scan_totals(own, info, early, rows, begin, heads, q_t, keys, peak_s, mass_s, log_total)


def grad_kernel(
    heads, rows, levels,
    info, q_rot, q_t, log_total_0, log_total_1, early, cot, cot_t, init,
    keys_n, keys_d, cos_n, cos_d, sin_n, sin_d, codes_n, codes_d, v_own, v_x, v_y1, v_y2, v_y3, v_core,
    out, bins, probs_s, out_s, delta_s, acc_s, values, keys, cos_k, sin_k, codes, held, sems,
):
    me = token_rank()
    own, first = me * rows, info[0]
    part = heads // 2
    early_heads = log_total_0.shape[0]
    log_total = [log_total_0.at[h : h + 1, :] for h in range(early_heads)]
    log_total += [log_total_1.at[h : h + 1, :] for h in range(heads - early_heads)]
    copies = interleave(keys_n, keys_d, keys, lambda j: sems.at[16 + j])
    for j, (bits, ref, at) in enumerate(slots((v_own, v_x, v_y1, v_y2, v_y3, v_core))):
        start = pl.multiple_of((me ^ bits) * rows, rows)
        copies.append(
            pltpu.make_async_copy(
                ref.at[at * rows : (at + 1) * rows, :], values.at[pl.ds(start, rows), :], sems.at[j]
            )
        )
    late = interleave(cos_n, cos_d, cos_k, lambda j: sems.at[18 + j])
    late += interleave(sin_n, sin_d, sin_k, lambda j: sems.at[20 + j])
    late += interleave(codes_n, codes_d, codes, lambda j: sems.at[22 + j])
    for copy in copies + late:
        copy.start()
    out_s[...] = jnp.zeros_like(out_s)
    for copy in copies:
        copy.wait()

    def forward(b, masked):
        base = pl.multiple_of(b * BLOCK, BLOCK)
        k = keys[b].reshape(BLOCK, HD)
        v = values[pl.ds(base, BLOCK), :]
        if masked:
            seen = visible_block(base, BLOCK, own, early[...], rows)
        for h in range(heads):
            s = lax.dot_general(k, q_t[h], NN, preferred_element_type=jnp.float32)
            p = jnp.exp2(s * (SCALE * LOG2E) - log_total[h][...])
            if masked:
                p = jnp.where(seen, p, 0.0)
            probs_s[b - first, h] = p
            out_s[h] += lax.dot_general(
                p.astype(jnp.bfloat16), v, TN, preferred_element_type=jnp.float32
            )

    over_blocks(own, info, rows, forward)
    for h in range(heads):
        o = out_s[h].astype(jnp.bfloat16)
        out[:, h * HD : (h + 1) * HD] = o
        prod = cot[:, h * HD : (h + 1) * HD].astype(jnp.float32) * o.astype(jnp.float32)
        delta_s[h : h + 1, :] = jnp.sum(prod.T, axis=0, keepdims=True)
    acc_s[...] = jnp.zeros_like(acc_s)
    last = (own + rows + BLOCK - 1) // BLOCK
    for copy in late:
        copy.wait()

    def add_bins(b, dk):
        dk = dk * SCALE
        cosine, sine = cos_k[b].reshape(BLOCK, HD), sin_k[b].reshape(BLOCK, HD)
        g = dk * cosine - pltpu.roll(dk, HD // 2, 1) * sine
        code = codes[b].reshape(BLOCK, HD).astype(jnp.float32)
        for level in range(levels):
            chosen = jnp.where(code == level, g, 0.0)
            acc_s[level] += jnp.sum(chosen.reshape(BLOCK // 8, 8, HD), axis=0)

    held[...] = jnp.zeros_like(held)

    @pl.loop(first, last)
    def _(b):
        base = pl.multiple_of(b * BLOCK, BLOCK)
        v = values[pl.ds(base, BLOCK), :]
        add_bins(jnp.maximum(b - 1, first), held[...])
        dk = jnp.zeros((BLOCK, HD), jnp.float32)
        for h in range(heads):
            dp = lax.dot_general(v, cot_t[h], NN, preferred_element_type=jnp.float32)
            ds = (probs_s[b - first, h] * (dp - delta_s[h : h + 1, :])).astype(jnp.bfloat16)
            dk = dk + lax.dot_general(ds, q_rot[h], NN, preferred_element_type=jnp.float32)
        held[...] = dk

    add_bins(last - 1, held[...])
    bins[...] = init[...] + jnp.sum(acc_s[...], axis=1)


def anywhere():
    return pl.BlockSpec(memory_space=pl.ANY)


def vmem():
    return pl.BlockSpec(memory_space=pltpu.VMEM)


def smem():
    return pl.BlockSpec(memory_space=pltpu.SMEM)


def cost(flops, size):
    return pl.CostEstimate(flops=flops, bytes_accessed=size, transcendentals=0)


def shards(hidden, w_query, w_key, w_value, key_codes, codebook, positions, cotangent):
    rows, part = hidden.shape
    width = w_query.shape[1]
    heads = width // HD
    levels = codebook.shape[1]
    ranks = lax.axis_size("tokens")
    total = rows * ranks
    group = lax.axis_size("tensor")
    rank = lax.axis_index("tensor")
    me = lax.axis_index("tokens")
    own = me * rows
    bf16, f32 = jnp.bfloat16, jnp.float32

    cross = lambda x, d: lax.ppermute(x, "tokens", [(i, i ^ d) for i in range(ranks)])

    def everyone(x, first, second, third):
        x_side = first(cross(x, 2))
        pair = second(jnp.concatenate([x, x_side], axis=0))
        y_side = [cross(pair, 4 * y) for y in (1, 2, 3)]
        core = cross(third(jnp.concatenate([pair] + y_side, axis=0)), 1)
        return (x, x_side, *y_side, core)

    def after(*others):
        return lambda v: lax.optimization_barrier((v, others))[0]

    flip = [(i, i ^ 1) for i in range(group)]
    up = [(i, (i + 2) % group) for i in range(group)]
    down = [(i, (i - 2) % group) for i in range(group)]
    send = functools.partial(lax.ppermute, axis_name="tensor")
    n = part // 2
    low = send(hidden, perm=up)
    high = send(hidden, perm=down)
    other = send(hidden, perm=flip)
    places = positions[None, :]
    packed, early, info = pl.pallas_call(
        functools.partial(pack_kernel, rows),
        out_shape=(
            jax.ShapeDtypeStruct((rows + TAIL, HD), bf16),
            jax.ShapeDtypeStruct((1, rows), jnp.int32),
            jax.ShapeDtypeStruct((2,), jnp.int32),
        ),
        in_specs=[vmem()] * 2,
        out_specs=(vmem(), vmem(), smem()),
        name="pack",
    )(key_codes, places)
    book = codebook.T

    mate = rank ^ 1
    turn = lambda x, by: (x + by) % group
    shard = [rank, turn(rank, -2), turn(rank, 2), mate]
    shard += [turn(rank, 4), turn(mate, -2), turn(mate, 2), turn(mate, 4)]
    place = jnp.stack(shard).astype(jnp.int32)

    y_side = [cross(packed, 4 * y) for y in (1, 2, 3)]
    column = jnp.concatenate([packed] + y_side, axis=0)
    x_side = cross(column, 2)
    low, high, other = after(column)((low, high, other))
    far_a = send(low[:, :n], perm=up)
    far_b = send(high[:, n:], perm=down)
    other_low = send(other, perm=up)
    other_high = send(other, perm=down)
    def prep(near, book, *pieces):
        few = ranks // 2
        shapes = [(few, rows, HD)] * 4
        kinds = [bf16, f32, f32, bf16]
        return pl.pallas_call(
            functools.partial(prep_kernel, near, rows, few, levels),
            out_shape=[jax.ShapeDtypeStruct(size, kind) for size, kind in zip(shapes, kinds)]
            + [jax.ShapeDtypeStruct((heads, HD, rows), bf16)] * near,
            in_specs=[vmem()] + [anywhere()] * len(pieces),
            out_specs=[anywhere()] * 4 + [vmem()] * near,
            scratch_shapes=[pltpu.VMEM((few * (rows + TAIL), HD), bf16)]
            + [pltpu.VMEM(size, kind) for size, kind in zip(shapes, kinds)]
            + [pltpu.SemaphoreType.DMA((few + 1,)), pltpu.SemaphoreType.DMA((4,))]
            + [pltpu.VMEM((rows, width), bf16)] * near,
            compiler_params=pltpu.CompilerParams(vmem_limit_bytes=58 << 20),
            cost_estimate=cost(0 if near else 1 << 32, 0),
            name="prep",
        )(book, *pieces)

    *near, cot_t = prep(True, book, packed, *y_side, x_side, cotangent)
    far_a, far_b = after(cot_t)((far_a, far_b))
    other_far_a = send(far_a, perm=flip)
    other_far_b = send(far_b, perm=flip)

    half = group // 2
    low, high, other = after(far_a, far_b)((low, high, other))
    q_sum, kv_sum = pl.pallas_call(
        functools.partial(project_kernel, half, part),
        out_shape=(jax.ShapeDtypeStruct((rows, width), f32), jax.ShapeDtypeStruct((rows, 2 * HD), f32)),
        in_specs=[smem()] + [anywhere()] * (3 + half),
        out_specs=(vmem(),) * 2,
        scratch_shapes=[
            pltpu.VMEM((half, rows, part), bf16),
            pltpu.VMEM((half, part, width), bf16),
            pltpu.VMEM((half, part, 2 * HD), bf16),
            pltpu.SemaphoreType.DMA((4 * half,)),
        ],
        compiler_params=pltpu.CompilerParams(vmem_limit_bytes=50 << 20),
        cost_estimate=cost(1 << 34, 0),
        name="project",
    )(place, w_query, w_key, w_value, hidden, low, high, other)
    x_side = after(far_a, far_b)(x_side)
    core = cross(jnp.concatenate([column, x_side], axis=0), 1)
    packed = (packed, *y_side, x_side, core)

    rest = [far_a, far_b, other_low, other_high, other_far_a, other_far_b]
    value = pl.pallas_call(
        functools.partial(value_kernel, half, half, part),
        out_shape=jax.ShapeDtypeStruct((rows, HD), bf16),
        in_specs=[smem()] + [anywhere()] * (2 + len(rest)),
        out_specs=vmem(),
        scratch_shapes=[
            pltpu.VMEM((rows, half * part), bf16),
            pltpu.VMEM((half, part, HD), bf16),
            pltpu.VMEM((rows, HD), f32),
            pltpu.SemaphoreType.DMA((half + len(rest) + 1,)),
        ],
        compiler_params=pltpu.CompilerParams(vmem_limit_bytes=50 << 20),
        cost_estimate=cost(0, 0),
        name="value",
    )(place, w_value, kv_sum, *rest)

    distant = prep(False, after(value)(book), packed[5])
    keys = distant[0]

    count = heads * 3 // 8
    totals = []

    def second(pair):
        pair, ready = lax.optimization_barrier((pair, place))
        found = pl.pallas_call(
            functools.partial(
                stats_kernel, count, heads, rows, levels, levels / total, half, half, part
            ),
            out_shape=(
                jax.ShapeDtypeStruct((heads, rows, HD), bf16),
                jax.ShapeDtypeStruct((heads, HD, rows), bf16),
                jax.ShapeDtypeStruct((count, rows), f32),
                jax.ShapeDtypeStruct((levels, HD), f32),
            ),
            in_specs=[smem()] * 2 + [vmem()] * 3 + [anywhere()] * (8 + len(rest)),
            out_specs=(vmem(),) * 4,
            scratch_shapes=[pltpu.VMEM((count, rows), f32)] * 2
            + [pltpu.VMEM((rows, HD), f32)] * 2
            + [
                pltpu.VMEM((ranks // 2, 2, rows, HD), bf16),
                pltpu.VMEM((rows, half * part), bf16),
                pltpu.VMEM((half, part, width), bf16),
                pltpu.VMEM((half, part, HD), bf16),
                pltpu.VMEM((rows, width), f32),
                pltpu.VMEM((rows, HD), f32),
                pltpu.SemaphoreType.DMA((len(rest),)),
                pltpu.SemaphoreType.DMA((2 * half,)),
                pltpu.SemaphoreType.DMA((6,)),
            ],
            compiler_params=pltpu.CompilerParams(vmem_limit_bytes=50 << 20),
            cost_estimate=cost(1 << 34, 0),
            name="stats",
        )(
            ready, info, early, key_codes, book, near[1], near[2], near[0], distant[0],
            q_sum, kv_sum, w_query, w_key, *rest,
        )
        totals.extend(found)
        return pair

    values = everyone(value, after(keys), second, lambda v: after(totals[2])(v))
    q_rot, q_t, log_total_0, init = totals
    late, _ = lax.optimization_barrier((q_t, values[2:5]))
    log_total_1 = pl.pallas_call(
        functools.partial(late_stats_kernel, count, heads - count, rows),
        out_shape=jax.ShapeDtypeStruct((heads - count, rows), f32),
        in_specs=[smem()] + [vmem()] * 2 + [anywhere()] * 2,
        out_specs=vmem(),
        scratch_shapes=[pltpu.VMEM((heads - count, rows), f32)] * 2
        + [pltpu.VMEM((ranks // 2, 2, rows, HD), bf16), pltpu.SemaphoreType.DMA((2,))],
        compiler_params=pltpu.CompilerParams(vmem_limit_bytes=32 << 20),
        cost_estimate=cost(1 << 34, 0),
        name="stats_late",
    )(info, early, late, near[0], distant[0])

    most = total // BLOCK
    attention_out, local = pl.pallas_call(
        functools.partial(grad_kernel, heads, rows, levels),
        out_shape=(
            jax.ShapeDtypeStruct((rows, width), bf16),
            jax.ShapeDtypeStruct((levels, HD), f32),
        ),
        in_specs=[smem()] + [vmem()] * 8 + [anywhere()] * 14,
        out_specs=(vmem(),) * 2,
        scratch_shapes=[
            pltpu.VMEM((min(most, 7), heads, BLOCK, rows), f32),
            pltpu.VMEM((heads, rows, HD), f32),
            pltpu.VMEM((heads, rows), f32),
            pltpu.VMEM((levels, 8, HD), f32),
            pltpu.VMEM((total, HD), bf16),
            pltpu.VMEM((ranks // 2, 2, rows, HD), bf16),
            pltpu.VMEM((ranks // 2, 2, rows, HD), f32),
            pltpu.VMEM((ranks // 2, 2, rows, HD), f32),
            pltpu.VMEM((ranks // 2, 2, rows, HD), bf16),
            pltpu.VMEM((BLOCK, HD), f32),
            pltpu.SemaphoreType.DMA((24,)),
        ],
        compiler_params=pltpu.CompilerParams(vmem_limit_bytes=44 << 20),
        cost_estimate=cost(8 * rows * width * total, 8 << 20),
        name="grad",
    )(
        info, q_rot, q_t, log_total_0, log_total_1, early, cotangent, cot_t, init,
        *[table for both in zip(near, distant) for table in both], *values,
    )
    for d in (1, 2, 4, 12):
        local = local + cross(local, d)
    return (attention_out, local.T)


def solution(mesh):
    placed = (
        P("tokens", "tensor"),
        P(None, "tensor"),
        P(None, "tensor"),
        P(None, "tensor"),
        P("tokens", "tensor"),
        P("tensor", None),
        P("tokens"),
        P("tokens", "tensor"),
    )
    return jax.shard_map(
        shards,
        mesh=mesh,
        in_specs=placed,
        out_specs=(P("tokens", "tensor"), P("tensor", None)),
        check_vma=False,
    )
```

```python
import functools
import math

import jax
import jax.numpy as jnp
from jax import lax
from jax.experimental import pallas as pl
from jax.experimental.pallas import tpu as pltpu
from jax.sharding import PartitionSpec as P

HD = 128
ROPE_BASE = 500000.0
NEG_BIG = -1e30
LOG2E = math.log2(math.e)
SCALE = 1.0 / math.sqrt(HD)
BLOCK = 512
NN = (((1,), (0,)), ((), ()))
TN = (((0,), (0,)), ((), ()))
TAIL = 16
STRIP = 32


def sincos(angle):
    turns = jnp.floor(angle * (2.0 / math.pi) + 0.5)
    r = angle - turns * 1.5703125
    r = r - turns * 4.837512969970703125e-4
    r = r - turns * 7.54978995489188216e-8
    z = r * r
    s = ((-1.9515295891e-4 * z + 8.3321608736e-3) * z - 1.6666654611e-1) * z * r + r
    c = ((2.443315711809948e-5 * z - 1.388731625493765e-3) * z + 4.166664568298827e-2) * z * z
    c = c - 0.5 * z + 1.0
    quadrant = turns.astype(jnp.int32)
    odd = (quadrant & 1) == 1
    sine = jnp.where(odd, c, s)
    cosine = jnp.where(odd, s, c)
    sine = jnp.where((quadrant & 2) == 0, sine, -sine)
    cosine = jnp.where(((quadrant + 1) & 2) == 0, cosine, -cosine)
    return sine, cosine


def slots(pieces):
    own, x, y1, y2, y3, core = pieces
    found = [(0, own, 0), (2, x, 0)]
    for y, ref in ((1, y1), (2, y2), (3, y3)):
        found += [(4 * y, ref, 0), (4 * y + 2, ref, 1)]
    return found + [(2 * j + 1, core, j) for j in range(8)]


def token_rank():
    return lax.axis_index("tokens")


def pack_kernel(rows, key_codes, positions, packed, early, info):
    packed[:rows, :] = key_codes[...].astype(jnp.float32).astype(jnp.bfloat16)
    place = positions[...]
    high, low = place & ~63, place & 63
    wide = [x[:, j * HD : (j + 1) * HD] for x in (high, low) for j in range(rows // HD)]
    blank = jnp.zeros((TAIL - len(wide), HD), jnp.int32)
    tail = jnp.concatenate(wide + [blank], axis=0)
    packed[rows:, :] = tail.astype(jnp.float32).astype(jnp.bfloat16)
    index = token_rank() * rows + lax.broadcasted_iota(jnp.int32, (1, rows), 1)
    first = index - place
    early[...] = first
    first = first.astype(jnp.float32)
    info[0] = jnp.min(first).astype(jnp.int32) // BLOCK
    info[1] = jnp.max(first).astype(jnp.int32)


def prep_kernel(
    near, rows, ranks, levels,
    book, *refs,
):
    pieces = refs[:5] if near else refs[:1]
    if near:
        cot_f, cot_t, cot = refs[5], refs[10], refs[-1]
        refs = refs[:10] + refs[11:-1]
    keys_f, cos_f, sin_f, codes_f, packed_s, keys, cos_k, sin_k, codes, sems, out_sems = refs[-11:]
    me = token_rank()
    tall = rows + TAIL
    if near:
        loading = pltpu.make_async_copy(cot_f, cot, sems.at[ranks])
        loading.start()
    if near:
        found = [(2 * j, ref, 0) for j, ref in enumerate(pieces[:4])]
        found += [(2 * j + 1, pieces[4], j) for j in range(4)]
    else:
        found = [(2 * j if j < 4 else 2 * (j - 4) + 1, pieces[0], j) for j in range(8)]
    copies = []
    for j, (bits, ref, at) in enumerate(found):
        start = pl.multiple_of(((me // 2) ^ bits) * tall, TAIL)
        copies.append(
            pltpu.make_async_copy(
                ref.at[at * tall : (at + 1) * tall, :], packed_s.at[pl.ds(start, tall), :], sems.at[j]
            )
        )
    for copy in copies:
        copy.start()
    for copy in copies:
        copy.wait()
    eye = lax.broadcasted_iota(jnp.int32, (HD, HD), 0) == lax.broadcasted_iota(
        jnp.int32, (HD, HD), 1
    )
    left = lax.broadcasted_iota(jnp.int32, (STRIP, HD), 1) < HD // 2
    ones = jnp.ones((2 * HD, HD), jnp.bfloat16)
    sides = rows // HD
    outs = [(keys, keys_f), (cos_k, cos_f), (sin_k, sin_f), (codes, codes_f)]

    inverse = jnp.exp(
        (lax.broadcasted_iota(jnp.int32, (1, HD), 1) % (HD // 2)).astype(jnp.float32)
        * (-2.0 * math.log(ROPE_BASE) / HD)
    )

    def prep_strip(i, part, strip, places, source):
        rows_of = slice(strip, strip + STRIP)
        place = jnp.where(left, places[part][rows_of, :], places[part + 1][rows_of, :])
        sine, cosine = sincos(place * inverse)
        sine_r, cosine_r = pltpu.roll(sine, HD // 2, 1), pltpu.roll(cosine, HD // 2, 1)
        tables = (
            (jnp.where(left, cosine, cosine_r), jnp.where(left, -sine, sine_r)),
            (jnp.where(left, cosine_r, cosine), jnp.where(left, -sine_r, sine)),
        )
        for side, (cosine, sine) in enumerate(tables):
            at = (part + side) * HD + strip
            target = pl.ds(at, STRIP)
            cos_k[i, target, :] = cosine
            sin_k[i, target, :] = sine
            raw = packed_s[pl.ds(source + at, STRIP), :]
            codes[i, target, :] = raw
            code = raw.astype(jnp.float32).astype(jnp.int32)
            layer = [book[e : e + 1, :] for e in range(levels)]
            bit = 1
            while len(layer) > 1:
                on = (code & bit) != 0
                layer = [jnp.where(on, layer[j + 1], layer[j]) for j in range(0, len(layer), 2)]
                bit *= 2
            deq = layer[0]
            turned = deq * cosine + pltpu.roll(deq, HD // 2, 1) * sine
            keys[i, target, :] = turned.astype(jnp.bfloat16)

    @pl.loop(0, ranks)
    def _(i):
        source = pl.multiple_of(i * tall, TAIL)
        tail = packed_s[pl.ds(source + rows, TAIL), :].astype(jnp.float32)
        places = []
        for part in range(sides):
            high = jnp.where(eye, tail[part : part + 1, :], 0.0)
            low = jnp.where(eye, tail[sides + part : sides + part + 1, :], 0.0)
            digits = jnp.concatenate([high, low], axis=1).astype(jnp.bfloat16)
            places.append(lax.dot_general(digits, ones, NN, preferred_element_type=jnp.float32))
        for part in range(0, sides, 2):
            for strip in range(0, HD, STRIP):
                prep_strip(i, part, strip, places, source)
        for j, (ref, full) in enumerate(outs):
            pltpu.make_async_copy(ref.at[i], full.at[i], out_sems.at[j]).start()

    if near:
        loading.wait()
        for h in range(cot_t.shape[0]):
            cot_t[h] = cot[:, h * HD : (h + 1) * HD].T
    for j, (ref, full) in enumerate(outs):
        pltpu.make_async_copy(ref, full, out_sems.at[j]).wait()


def shard_rows(place, n, part):
    return pl.ds(pl.multiple_of(place[n] * part, part), part)


def interleave(near, distant, ref, sem):
    core = token_rank() % 2
    return [
        pltpu.make_async_copy(half, ref.at[:, core ^ j], sem(j))
        for j, half in enumerate((near, distant))
    ]


def fetch(pieces, x_s, sem):
    copies, at = [], 0
    for piece in pieces:
        width = piece.shape[1]
        copies.append(pltpu.make_async_copy(piece, x_s.at[:, at : at + width], sem(len(copies))))
        at += width
    return copies


def project_kernel(
    count, part, place, wq, wk, wv, *refs,
):
    pieces, (q_out, kv_out, x_s, wq_s, wkv_s, sems) = refs[:count], refs[count:]
    copies = []
    for n, piece in enumerate(pieces):
        rows = shard_rows(place, n, part)
        copies.append([
            pltpu.make_async_copy(piece, x_s.at[n], sems.at[4 * n]),
            pltpu.make_async_copy(wq.at[rows, :], wq_s.at[n], sems.at[4 * n + 1]),
            pltpu.make_async_copy(wk.at[rows, :], wkv_s.at[n, :, :HD], sems.at[4 * n + 2]),
            pltpu.make_async_copy(wv.at[rows, :], wkv_s.at[n, :, HD:], sems.at[4 * n + 3]),
        ])
        for copy in copies[-1]:
            copy.start()
    for n in range(count):
        for copy in copies[n]:
            copy.wait()
        x = x_s[n]
        q = jnp.dot(x, wq_s[n], preferred_element_type=jnp.float32)
        kv = jnp.dot(x, wkv_s[n], preferred_element_type=jnp.float32)
        q_out[...] = q if n == 0 else q_out[...] + q
        kv_out[...] = kv if n == 0 else kv_out[...] + kv


def value_kernel(first, count, part, place, w, before, *refs):
    pieces, (value, x_s, w_s, before_s, sems) = refs[:-5], refs[-5:]
    copies = fetch(pieces, x_s, lambda j: sems.at[j])
    copies.append(pltpu.make_async_copy(before.at[:, HD:], before_s, sems.at[len(copies)]))
    for n in range(count):
        copies.append(
            pltpu.make_async_copy(w.at[shard_rows(place, first + n, part), :], w_s.at[n], sems.at[len(copies)])
        )
    for copy in copies:
        copy.start()
    for copy in copies:
        copy.wait()
    total = before_s[...]
    for n in range(count):
        total += jnp.dot(x_s[:, n * part : (n + 1) * part], w_s[n], preferred_element_type=jnp.float32)
    value[...] = total.astype(jnp.bfloat16)


def visible_block(base, block, own, earliest, rows):
    key = base + lax.broadcasted_iota(jnp.int32, (block, rows), 0)
    query = own + lax.broadcasted_iota(jnp.int32, (block, rows), 1)
    return (key <= query) & (key >= earliest)


def over_blocks(own, info, rows, body):
    first, edge = info[0], info[1]
    last = (own + rows + BLOCK - 1) // BLOCK

    @pl.loop(first, last)
    def _(b):
        masked = (b * BLOCK < edge) | (b * BLOCK + BLOCK > own)

        @pl.when(masked)
        def _():
            body(b, True)

        @pl.when(jnp.logical_not(masked))
        def _():
            body(b, False)


def stats_kernel(
    heads, wide, rows, levels, weight, first, count, part,
    place, info, early, codes, book, cos_k, sin_k, keys_n, keys_d, q_before, kv_before, wq, wk, *refs,
):
    pieces = refs[:-17]
    (
        q_rot, q_t, log_total, bins,
        peak_s, mass_s, cos_q, sin_q, keys, x_s, wq_s, wk_s, q_s, true_s, x_sems, w_sems, sems,
    ) = refs[-17:]
    own = token_rank() * rows
    mine = token_rank() // 2
    loads = fetch(pieces, x_s, lambda j: x_sems.at[j])
    weights = []
    for n in range(count):
        at = shard_rows(place, first + n, part)
        weights.append([
            pltpu.make_async_copy(wq.at[at, :], wq_s.at[n], w_sems.at[2 * n]),
            pltpu.make_async_copy(wk.at[at, :], wk_s.at[n], w_sems.at[2 * n + 1]),
        ])
    before = [
        pltpu.make_async_copy(q_before, q_s, sems.at[0]),
        pltpu.make_async_copy(kv_before.at[:, :HD], true_s, sems.at[1]),
    ]
    tables = [
        pltpu.make_async_copy(cos_k.at[mine], cos_q, sems.at[2]),
        pltpu.make_async_copy(sin_k.at[mine], sin_q, sems.at[3]),
    ] + interleave(keys_n, keys_d, keys, lambda j: sems.at[4 + j])
    for copy in before + loads + sum(weights, []) + tables:
        copy.start()
    for copy in before + loads:
        copy.wait()
    for n in range(count):
        for copy in weights[n]:
            copy.wait()
        x = x_s[:, n * part : (n + 1) * part]
        q_s[...] += jnp.dot(x, wq_s[n], preferred_element_type=jnp.float32)
        true_s[...] += jnp.dot(x, wk_s[n], preferred_element_type=jnp.float32)
    code = codes[...]
    for level in range(levels):
        entry = weight * (book[level : level + 1, :] - true_s[...])
        bins[level : level + 1, :] = jnp.sum(
            jnp.where(code == level, entry, 0.0), axis=0, keepdims=True
        )
    for copy in tables:
        copy.wait()
    for h in range(wide):
        x = q_s[:, h * HD : (h + 1) * HD]
        turned = (x * cos_q[...] + pltpu.roll(x, HD // 2, 1) * sin_q[...]).astype(jnp.bfloat16)
        q_rot[h] = turned
        q_t[h] = turned.T
    scan_totals(own, info, early, rows, 0, heads, q_t, keys, peak_s, mass_s, log_total)


def scan_totals(own, info, early, rows, begin, heads, q_t, keys, peak_s, mass_s, log_total):
    peak_s[...] = jnp.full_like(peak_s, NEG_BIG)
    mass_s[...] = jnp.zeros_like(mass_s)

    def body(b, masked):
        base = pl.multiple_of(b * BLOCK, BLOCK)
        k = keys[b].reshape(BLOCK, HD)
        if masked:
            seen = visible_block(base, BLOCK, own, early[...], rows)
        for h in range(heads):
            t = lax.dot_general(k, q_t[begin + h], NN, preferred_element_type=jnp.float32)
            t = t * (SCALE * LOG2E)
            if masked:
                t = jnp.where(seen, t, NEG_BIG)
            old = peak_s[h : h + 1, :]
            new = jnp.maximum(old, jnp.max(t, axis=0, keepdims=True))
            fresh = jnp.sum(jnp.exp2(t - new), axis=0, keepdims=True)
            mass_s[h : h + 1, :] = mass_s[h : h + 1, :] * jnp.exp2(old - new) + fresh
            peak_s[h : h + 1, :] = new

    over_blocks(own, info, rows, body)
    log_total[...] = peak_s[...] + jnp.log(mass_s[...]) * LOG2E


def late_stats_kernel(
    begin, heads, rows, info, early, q_t, keys_n, keys_d, log_total, peak_s, mass_s, keys, sems,
):
    copies = interleave(keys_n, keys_d, keys, lambda j: sems.at[j])
    for copy in copies:
        copy.start()
    for copy in copies:
        copy.wait()
    own = token_rank() * rows
    scan_totals(own, info, early, rows, begin, heads, q_t, keys, peak_s, mass_s, log_total)


def grad_kernel(
    heads, rows, levels,
    info, q_rot, q_t, log_total_0, log_total_1, early, cot, cot_t, init,
    keys_n, keys_d, cos_n, cos_d, sin_n, sin_d, codes_n, codes_d, v_own, v_x, v_y1, v_y2, v_y3, v_core,
    out, bins, probs_s, out_s, delta_s, acc_s, values, keys, cos_k, sin_k, codes, held, sems,
):
    me = token_rank()
    own, first = me * rows, info[0]
    part = heads // 2
    early_heads = log_total_0.shape[0]
    log_total = [log_total_0.at[h : h + 1, :] for h in range(early_heads)]
    log_total += [log_total_1.at[h : h + 1, :] for h in range(heads - early_heads)]
    copies = interleave(keys_n, keys_d, keys, lambda j: sems.at[16 + j])
    for j, (bits, ref, at) in enumerate(slots((v_own, v_x, v_y1, v_y2, v_y3, v_core))):
        start = pl.multiple_of((me ^ bits) * rows, rows)
        copies.append(
            pltpu.make_async_copy(
                ref.at[at * rows : (at + 1) * rows, :], values.at[pl.ds(start, rows), :], sems.at[j]
            )
        )
    late = interleave(cos_n, cos_d, cos_k, lambda j: sems.at[18 + j])
    late += interleave(sin_n, sin_d, sin_k, lambda j: sems.at[20 + j])
    late += interleave(codes_n, codes_d, codes, lambda j: sems.at[22 + j])
    for copy in copies + late:
        copy.start()
    out_s[...] = jnp.zeros_like(out_s)
    for copy in copies:
        copy.wait()

    def forward(b, masked):
        base = pl.multiple_of(b * BLOCK, BLOCK)
        k = keys[b].reshape(BLOCK, HD)
        v = values[pl.ds(base, BLOCK), :]
        if masked:
            seen = visible_block(base, BLOCK, own, early[...], rows)
        for h in range(heads):
            s = lax.dot_general(k, q_t[h], NN, preferred_element_type=jnp.float32)
            p = jnp.exp2(s * (SCALE * LOG2E) - log_total[h][...])
            if masked:
                p = jnp.where(seen, p, 0.0)
            probs_s[b - first, h] = p
            out_s[h] += lax.dot_general(
                p.astype(jnp.bfloat16), v, TN, preferred_element_type=jnp.float32
            )

    over_blocks(own, info, rows, forward)
    for h in range(heads):
        o = out_s[h].astype(jnp.bfloat16)
        out[:, h * HD : (h + 1) * HD] = o
        prod = cot[:, h * HD : (h + 1) * HD].astype(jnp.float32) * o.astype(jnp.float32)
        delta_s[h : h + 1, :] = jnp.sum(prod.T, axis=0, keepdims=True)
    acc_s[...] = jnp.zeros_like(acc_s)
    last = (own + rows + BLOCK - 1) // BLOCK
    for copy in late:
        copy.wait()

    def add_bins(b, dk):
        dk = dk * SCALE
        cosine, sine = cos_k[b].reshape(BLOCK, HD), sin_k[b].reshape(BLOCK, HD)
        g = dk * cosine - pltpu.roll(dk, HD // 2, 1) * sine
        code = codes[b].reshape(BLOCK, HD).astype(jnp.float32)
        for level in range(levels):
            chosen = jnp.where(code == level, g, 0.0)
            acc_s[level] += jnp.sum(chosen.reshape(BLOCK // 8, 8, HD), axis=0)

    held[...] = jnp.zeros_like(held)

    @pl.loop(first, last)
    def _(b):
        base = pl.multiple_of(b * BLOCK, BLOCK)
        v = values[pl.ds(base, BLOCK), :]
        add_bins(jnp.maximum(b - 1, first), held[...])
        dk = jnp.zeros((BLOCK, HD), jnp.float32)
        for h in range(heads):
            dp = lax.dot_general(v, cot_t[h], NN, preferred_element_type=jnp.float32)
            ds = (probs_s[b - first, h] * (dp - delta_s[h : h + 1, :])).astype(jnp.bfloat16)
            dk = dk + lax.dot_general(ds, q_rot[h], NN, preferred_element_type=jnp.float32)
        held[...] = dk

    add_bins(last - 1, held[...])
    bins[...] = init[...] + jnp.sum(acc_s[...], axis=1)


def anywhere():
    return pl.BlockSpec(memory_space=pl.ANY)


def vmem():
    return pl.BlockSpec(memory_space=pltpu.VMEM)


def smem():
    return pl.BlockSpec(memory_space=pltpu.SMEM)


def cost(flops, size):
    return pl.CostEstimate(flops=flops, bytes_accessed=size, transcendentals=0)


def shards(hidden, w_query, w_key, w_value, key_codes, codebook, positions, cotangent):
    rows, part = hidden.shape
    width = w_query.shape[1]
    heads = width // HD
    levels = codebook.shape[1]
    ranks = lax.axis_size("tokens")
    total = rows * ranks
    group = lax.axis_size("tensor")
    rank = lax.axis_index("tensor")
    me = lax.axis_index("tokens")
    own = me * rows
    bf16, f32 = jnp.bfloat16, jnp.float32

    cross = lambda x, d: lax.ppermute(x, "tokens", [(i, i ^ d) for i in range(ranks)])

    def everyone(x, first, second, third):
        x_side = first(cross(x, 2))
        pair = second(jnp.concatenate([x, x_side], axis=0))
        y_side = [cross(pair, 4 * y) for y in (1, 2, 3)]
        core = cross(third(jnp.concatenate([pair] + y_side, axis=0)), 1)
        return (x, x_side, *y_side, core)

    def after(*others):
        return lambda v: lax.optimization_barrier((v, others))[0]

    flip = [(i, i ^ 1) for i in range(group)]
    up = [(i, (i + 2) % group) for i in range(group)]
    down = [(i, (i - 2) % group) for i in range(group)]
    send = functools.partial(lax.ppermute, axis_name="tensor")
    n = part // 2
    low = send(hidden, perm=up)
    high = send(hidden, perm=down)
    other = send(hidden, perm=flip)
    places = positions[None, :]
    packed, early, info = pl.pallas_call(
        functools.partial(pack_kernel, rows),
        out_shape=(
            jax.ShapeDtypeStruct((rows + TAIL, HD), bf16),
            jax.ShapeDtypeStruct((1, rows), jnp.int32),
            jax.ShapeDtypeStruct((2,), jnp.int32),
        ),
        in_specs=[vmem()] * 2,
        out_specs=(vmem(), vmem(), smem()),
        name="pack",
    )(key_codes, places)
    book = codebook.T

    mate = rank ^ 1
    turn = lambda x, by: (x + by) % group
    shard = [rank, turn(rank, -2), turn(rank, 2), mate]
    shard += [turn(rank, 4), turn(mate, -2), turn(mate, 2), turn(mate, 4)]
    place = jnp.stack(shard).astype(jnp.int32)

    y_side = [cross(packed, 4 * y) for y in (1, 2, 3)]
    column = jnp.concatenate([packed] + y_side, axis=0)
    x_side = cross(column, 2)
    low, high, other = after(column)((low, high, other))
    far_a = send(low[:, :n], perm=up)
    far_b = send(high[:, n:], perm=down)
    half = group // 2
    q_sum, kv_sum = pl.pallas_call(
        functools.partial(project_kernel, half, part),
        out_shape=(jax.ShapeDtypeStruct((rows, width), f32), jax.ShapeDtypeStruct((rows, 2 * HD), f32)),
        in_specs=[smem()] + [anywhere()] * (3 + half),
        out_specs=(vmem(),) * 2,
        scratch_shapes=[
            pltpu.VMEM((half, rows, part), bf16),
            pltpu.VMEM((half, part, width), bf16),
            pltpu.VMEM((half, part, 2 * HD), bf16),
            pltpu.SemaphoreType.DMA((4 * half,)),
        ],
        compiler_params=pltpu.CompilerParams(vmem_limit_bytes=50 << 20),
        cost_estimate=cost(1 << 34, 0),
        name="project",
    )(place, w_query, w_key, w_value, hidden, low, high, other)
    far_a, far_b, other, x_side = after(kv_sum)((far_a, far_b, other, x_side))
    other_low = send(other, perm=up)
    other_high = send(other, perm=down)
    other_far_a = send(far_a, perm=flip)
    other_far_b = send(far_b, perm=flip)
    core = cross(jnp.concatenate([column, x_side], axis=0), 1)
    packed = (packed, *y_side, x_side, core)

    rest = [far_a, far_b, other_low, other_high, other_far_a, other_far_b]
    value = pl.pallas_call(
        functools.partial(value_kernel, half, half, part),
        out_shape=jax.ShapeDtypeStruct((rows, HD), bf16),
        in_specs=[smem()] + [anywhere()] * (2 + len(rest)),
        out_specs=vmem(),
        scratch_shapes=[
            pltpu.VMEM((rows, half * part), bf16),
            pltpu.VMEM((half, part, HD), bf16),
            pltpu.VMEM((rows, HD), f32),
            pltpu.SemaphoreType.DMA((half + len(rest) + 1,)),
        ],
        compiler_params=pltpu.CompilerParams(vmem_limit_bytes=50 << 20),
        cost_estimate=cost(0, 0),
        name="value",
    )(place, w_value, kv_sum, *rest)

    def prep(near, book, *pieces):
        few = ranks // 2
        shapes = [(few, rows, HD)] * 4
        kinds = [bf16, f32, f32, bf16]
        return pl.pallas_call(
            functools.partial(prep_kernel, near, rows, few, levels),
            out_shape=[jax.ShapeDtypeStruct(size, kind) for size, kind in zip(shapes, kinds)]
            + [jax.ShapeDtypeStruct((heads, HD, rows), bf16)] * near,
            in_specs=[vmem()] + [anywhere()] * len(pieces),
            out_specs=[anywhere()] * 4 + [vmem()] * near,
            scratch_shapes=[pltpu.VMEM((few * (rows + TAIL), HD), bf16)]
            + [pltpu.VMEM(size, kind) for size, kind in zip(shapes, kinds)]
            + [pltpu.SemaphoreType.DMA((few + 1,)), pltpu.SemaphoreType.DMA((4,))]
            + [pltpu.VMEM((rows, width), bf16)] * near,
            compiler_params=pltpu.CompilerParams(vmem_limit_bytes=58 << 20),
            cost_estimate=cost(1 << 34 if near else 1 << 32, 0),
            name="prep",
        )(book, *pieces)

    *near, cot_t = prep(True, after(kv_sum)(book), *packed[:5], cotangent)
    distant = prep(False, after(value)(book), packed[5])
    keys = distant[0]

    count = heads * 3 // 8
    totals = []

    def second(pair):
        pair, ready = lax.optimization_barrier((pair, place))
        found = pl.pallas_call(
            functools.partial(
                stats_kernel, count, heads, rows, levels, levels / total, half, half, part
            ),
            out_shape=(
                jax.ShapeDtypeStruct((heads, rows, HD), bf16),
                jax.ShapeDtypeStruct((heads, HD, rows), bf16),
                jax.ShapeDtypeStruct((count, rows), f32),
                jax.ShapeDtypeStruct((levels, HD), f32),
            ),
            in_specs=[smem()] * 2 + [vmem()] * 3 + [anywhere()] * (8 + len(rest)),
            out_specs=(vmem(),) * 4,
            scratch_shapes=[pltpu.VMEM((count, rows), f32)] * 2
            + [pltpu.VMEM((rows, HD), f32)] * 2
            + [
                pltpu.VMEM((ranks // 2, 2, rows, HD), bf16),
                pltpu.VMEM((rows, half * part), bf16),
                pltpu.VMEM((half, part, width), bf16),
                pltpu.VMEM((half, part, HD), bf16),
                pltpu.VMEM((rows, width), f32),
                pltpu.VMEM((rows, HD), f32),
                pltpu.SemaphoreType.DMA((len(rest),)),
                pltpu.SemaphoreType.DMA((2 * half,)),
                pltpu.SemaphoreType.DMA((6,)),
            ],
            compiler_params=pltpu.CompilerParams(vmem_limit_bytes=50 << 20),
            cost_estimate=cost(1 << 34, 0),
            name="stats",
        )(
            ready, info, early, key_codes, book, near[1], near[2], near[0], distant[0],
            q_sum, kv_sum, w_query, w_key, *rest,
        )
        totals.extend(found)
        return pair

    values = everyone(value, after(keys), second, lambda v: after(totals[2])(v))
    q_rot, q_t, log_total_0, init = totals
    late, _ = lax.optimization_barrier((q_t, values[2:5]))
    log_total_1 = pl.pallas_call(
        functools.partial(late_stats_kernel, count, heads - count, rows),
        out_shape=jax.ShapeDtypeStruct((heads - count, rows), f32),
        in_specs=[smem()] + [vmem()] * 2 + [anywhere()] * 2,
        out_specs=vmem(),
        scratch_shapes=[pltpu.VMEM((heads - count, rows), f32)] * 2
        + [pltpu.VMEM((ranks // 2, 2, rows, HD), bf16), pltpu.SemaphoreType.DMA((2,))],
        compiler_params=pltpu.CompilerParams(vmem_limit_bytes=32 << 20),
        cost_estimate=cost(1 << 34, 0),
        name="stats_late",
    )(info, early, late, near[0], distant[0])

    most = total // BLOCK
    attention_out, local = pl.pallas_call(
        functools.partial(grad_kernel, heads, rows, levels),
        out_shape=(
            jax.ShapeDtypeStruct((rows, width), bf16),
            jax.ShapeDtypeStruct((levels, HD), f32),
        ),
        in_specs=[smem()] + [vmem()] * 8 + [anywhere()] * 14,
        out_specs=(vmem(),) * 2,
        scratch_shapes=[
            pltpu.VMEM((min(most, 7), heads, BLOCK, rows), f32),
            pltpu.VMEM((heads, rows, HD), f32),
            pltpu.VMEM((heads, rows), f32),
            pltpu.VMEM((levels, 8, HD), f32),
            pltpu.VMEM((total, HD), bf16),
            pltpu.VMEM((ranks // 2, 2, rows, HD), bf16),
            pltpu.VMEM((ranks // 2, 2, rows, HD), f32),
            pltpu.VMEM((ranks // 2, 2, rows, HD), f32),
            pltpu.VMEM((ranks // 2, 2, rows, HD), bf16),
            pltpu.VMEM((BLOCK, HD), f32),
            pltpu.SemaphoreType.DMA((24,)),
        ],
        compiler_params=pltpu.CompilerParams(vmem_limit_bytes=44 << 20),
        cost_estimate=cost(8 * rows * width * total, 8 << 20),
        name="grad",
    )(
        info, q_rot, q_t, log_total_0, log_total_1, early, cotangent, cot_t, init,
        *[table for both in zip(near, distant) for table in both], *values,
    )
    for d in (1, 2, 4, 12):
        local = local + cross(local, d)
    return (attention_out, local.T)


def solution(mesh):
    placed = (
        P("tokens", "tensor"),
        P(None, "tensor"),
        P(None, "tensor"),
        P(None, "tensor"),
        P("tokens", "tensor"),
        P("tensor", None),
        P("tokens"),
        P("tokens", "tensor"),
    )
    return jax.shard_map(
        shards,
        mesh=mesh,
        in_specs=placed,
        out_specs=(P("tokens", "tensor"), P("tensor", None)),
        check_vma=False,
    )
```

```python
import functools
import math

import jax
import jax.numpy as jnp
from jax import lax
from jax.experimental import pallas as pl
from jax.experimental.pallas import tpu as pltpu
from jax.sharding import PartitionSpec as P

HD = 128
ROPE_BASE = 500000.0
NEG_BIG = -1e30
LOG2E = math.log2(math.e)
SCALE = 1.0 / math.sqrt(HD)
BLOCK = 512
NN = (((1,), (0,)), ((), ()))
TN = (((0,), (0,)), ((), ()))
TAIL = 16
STRIP = 32


def sincos(angle):
    turns = jnp.floor(angle * (2.0 / math.pi) + 0.5)
    r = angle - turns * 1.5703125
    r = r - turns * 4.837512969970703125e-4
    r = r - turns * 7.54978995489188216e-8
    z = r * r
    s = ((-1.9515295891e-4 * z + 8.3321608736e-3) * z - 1.6666654611e-1) * z * r + r
    c = ((2.443315711809948e-5 * z - 1.388731625493765e-3) * z + 4.166664568298827e-2) * z * z
    c = c - 0.5 * z + 1.0
    quadrant = turns.astype(jnp.int32)
    odd = (quadrant & 1) == 1
    sine = jnp.where(odd, c, s)
    cosine = jnp.where(odd, s, c)
    sine = jnp.where((quadrant & 2) == 0, sine, -sine)
    cosine = jnp.where(((quadrant + 1) & 2) == 0, cosine, -cosine)
    return sine, cosine


def slots(pieces):
    own, x, y1, y2, y3, core = pieces
    found = [(0, own, 0), (2, x, 0)]
    for y, ref in ((1, y1), (2, y2), (3, y3)):
        found += [(4 * y, ref, 0), (4 * y + 2, ref, 1)]
    return found + [(2 * j + 1, core, j) for j in range(8)]


def token_rank():
    return lax.axis_index("tokens")


def pack_kernel(rows, key_codes, positions, packed, early, info):
    packed[:rows, :] = key_codes[...].astype(jnp.float32).astype(jnp.bfloat16)
    place = positions[...]
    high, low = place & ~63, place & 63
    wide = [x[:, j * HD : (j + 1) * HD] for x in (high, low) for j in range(rows // HD)]
    blank = jnp.zeros((TAIL - len(wide), HD), jnp.int32)
    tail = jnp.concatenate(wide + [blank], axis=0)
    packed[rows:, :] = tail.astype(jnp.float32).astype(jnp.bfloat16)
    index = token_rank() * rows + lax.broadcasted_iota(jnp.int32, (1, rows), 1)
    first = index - place
    early[...] = first
    first = first.astype(jnp.float32)
    info[0] = jnp.min(first).astype(jnp.int32) // BLOCK
    info[1] = jnp.max(first).astype(jnp.int32)


def prep_kernel(
    near, rows, ranks, levels,
    book, *refs,
):
    pieces = refs[:5] if near else refs[:1]
    if near:
        cot_f, cot_t, cot = refs[5], refs[10], refs[-1]
        refs = refs[:10] + refs[11:-1]
    keys_f, cos_f, sin_f, codes_f, packed_s, keys, cos_k, sin_k, codes, sems, out_sems = refs[-11:]
    me = token_rank()
    tall = rows + TAIL
    if near:
        loading = pltpu.make_async_copy(cot_f, cot, sems.at[ranks])
        loading.start()
    if near:
        found = [(2 * j, ref, 0) for j, ref in enumerate(pieces[:4])]
        found += [(2 * j + 1, pieces[4], j) for j in range(4)]
    else:
        found = [(2 * j if j < 4 else 2 * (j - 4) + 1, pieces[0], j) for j in range(8)]
    copies = []
    for j, (bits, ref, at) in enumerate(found):
        start = pl.multiple_of(((me // 2) ^ bits) * tall, TAIL)
        copies.append(
            pltpu.make_async_copy(
                ref.at[at * tall : (at + 1) * tall, :], packed_s.at[pl.ds(start, tall), :], sems.at[j]
            )
        )
    for copy in copies:
        copy.start()
    for copy in copies:
        copy.wait()
    eye = lax.broadcasted_iota(jnp.int32, (HD, HD), 0) == lax.broadcasted_iota(
        jnp.int32, (HD, HD), 1
    )
    left = lax.broadcasted_iota(jnp.int32, (STRIP, HD), 1) < HD // 2
    ones = jnp.ones((2 * HD, HD), jnp.bfloat16)
    sides = rows // HD
    outs = [(keys, keys_f), (cos_k, cos_f), (sin_k, sin_f), (codes, codes_f)]

    inverse = jnp.exp(
        (lax.broadcasted_iota(jnp.int32, (1, HD), 1) % (HD // 2)).astype(jnp.float32)
        * (-2.0 * math.log(ROPE_BASE) / HD)
    )

    def prep_strip(i, part, strip, places, source):
        rows_of = slice(strip, strip + STRIP)
        place = jnp.where(left, places[part][rows_of, :], places[part + 1][rows_of, :])
        sine, cosine = sincos(place * inverse)
        sine_r, cosine_r = pltpu.roll(sine, HD // 2, 1), pltpu.roll(cosine, HD // 2, 1)
        tables = (
            (jnp.where(left, cosine, cosine_r), jnp.where(left, -sine, sine_r)),
            (jnp.where(left, cosine_r, cosine), jnp.where(left, -sine_r, sine)),
        )
        for side, (cosine, sine) in enumerate(tables):
            at = (part + side) * HD + strip
            target = pl.ds(at, STRIP)
            cos_k[i, target, :] = cosine
            sin_k[i, target, :] = sine
            raw = packed_s[pl.ds(source + at, STRIP), :]
            codes[i, target, :] = raw
            code = raw.astype(jnp.float32).astype(jnp.int32)
            layer = [book[e : e + 1, :] for e in range(levels)]
            bit = 1
            while len(layer) > 1:
                on = (code & bit) != 0
                layer = [jnp.where(on, layer[j + 1], layer[j]) for j in range(0, len(layer), 2)]
                bit *= 2
            deq = layer[0]
            turned = deq * cosine + pltpu.roll(deq, HD // 2, 1) * sine
            keys[i, target, :] = turned.astype(jnp.bfloat16)

    @pl.loop(0, ranks)
    def _(i):
        source = pl.multiple_of(i * tall, TAIL)
        tail = packed_s[pl.ds(source + rows, TAIL), :].astype(jnp.float32)
        places = []
        for part in range(sides):
            high = jnp.where(eye, tail[part : part + 1, :], 0.0)
            low = jnp.where(eye, tail[sides + part : sides + part + 1, :], 0.0)
            digits = jnp.concatenate([high, low], axis=1).astype(jnp.bfloat16)
            places.append(lax.dot_general(digits, ones, NN, preferred_element_type=jnp.float32))
        for part in range(0, sides, 2):
            for strip in range(0, HD, STRIP):
                prep_strip(i, part, strip, places, source)
        for j, (ref, full) in enumerate(outs):
            pltpu.make_async_copy(ref.at[i], full.at[i], out_sems.at[j]).start()

    if near:
        loading.wait()
        for h in range(cot_t.shape[0]):
            cot_t[h] = cot[:, h * HD : (h + 1) * HD].T
    for j, (ref, full) in enumerate(outs):
        pltpu.make_async_copy(ref, full, out_sems.at[j]).wait()


def shard_rows(place, n, part):
    return pl.ds(pl.multiple_of(place[n] * part, part), part)


def interleave(near, distant, ref, sem):
    core = token_rank() % 2
    return [
        pltpu.make_async_copy(half, ref.at[:, core ^ j], sem(j))
        for j, half in enumerate((near, distant))
    ]


def fetch(pieces, x_s, sem):
    copies, at = [], 0
    for piece in pieces:
        width = piece.shape[1]
        copies.append(pltpu.make_async_copy(piece, x_s.at[:, at : at + width], sem(len(copies))))
        at += width
    return copies


def project_kernel(
    count, part, place, wq, wk, wv, *refs,
):
    pieces, (q_out, kv_out, x_s, wq_s, wkv_s, sems) = refs[:count], refs[count:]
    copies = []
    for n, piece in enumerate(pieces):
        rows = shard_rows(place, n, part)
        copies.append([
            pltpu.make_async_copy(piece, x_s.at[n], sems.at[4 * n]),
            pltpu.make_async_copy(wq.at[rows, :], wq_s.at[n], sems.at[4 * n + 1]),
            pltpu.make_async_copy(wk.at[rows, :], wkv_s.at[n, :, :HD], sems.at[4 * n + 2]),
            pltpu.make_async_copy(wv.at[rows, :], wkv_s.at[n, :, HD:], sems.at[4 * n + 3]),
        ])
        for copy in copies[-1]:
            copy.start()
    for n in range(count):
        for copy in copies[n]:
            copy.wait()
        x = x_s[n]
        q = jnp.dot(x, wq_s[n], preferred_element_type=jnp.float32)
        kv = jnp.dot(x, wkv_s[n], preferred_element_type=jnp.float32)
        q_out[...] = q if n == 0 else q_out[...] + q
        kv_out[...] = kv if n == 0 else kv_out[...] + kv


def value_kernel(first, count, part, place, w, before, *refs):
    pieces, (value, x_s, w_s, before_s, sems) = refs[:-5], refs[-5:]
    copies = fetch(pieces, x_s, lambda j: sems.at[j])
    copies.append(pltpu.make_async_copy(before.at[:, HD:], before_s, sems.at[len(copies)]))
    for n in range(count):
        copies.append(
            pltpu.make_async_copy(w.at[shard_rows(place, first + n, part), :], w_s.at[n], sems.at[len(copies)])
        )
    loads, (first_sums, *weights) = copies[: len(pieces)], copies[len(pieces) :]
    order, at = [[] for _ in range(count)], 0
    for piece, copy in zip(pieces, loads):
        order[at // part].append(copy)
        at += piece.shape[1]
    for n in range(count):
        order[n].append(weights[n])
    order[0].append(first_sums)
    for copy in sum(order, []):
        copy.start()
    total = None
    for n in range(count):
        for copy in order[n]:
            copy.wait()
        term = jnp.dot(x_s[:, n * part : (n + 1) * part], w_s[n], preferred_element_type=jnp.float32)
        total = before_s[...] + term if n == 0 else total + term
    value[...] = total.astype(jnp.bfloat16)


def visible_block(base, block, own, earliest, rows):
    key = base + lax.broadcasted_iota(jnp.int32, (block, rows), 0)
    query = own + lax.broadcasted_iota(jnp.int32, (block, rows), 1)
    return (key <= query) & (key >= earliest)


def over_blocks(own, info, rows, body):
    first, edge = info[0], info[1]
    last = (own + rows + BLOCK - 1) // BLOCK

    @pl.loop(first, last)
    def _(b):
        masked = (b * BLOCK < edge) | (b * BLOCK + BLOCK > own)

        @pl.when(masked)
        def _():
            body(b, True)

        @pl.when(jnp.logical_not(masked))
        def _():
            body(b, False)


def stats_kernel(
    heads, wide, rows, levels, weight, first, count, part,
    place, info, early, codes, book, cos_k, sin_k, keys_n, keys_d, q_before, kv_before, wq, wk, *refs,
):
    pieces = refs[:-17]
    (
        q_rot, q_t, log_total, bins,
        peak_s, mass_s, cos_q, sin_q, keys, x_s, wq_s, wk_s, q_s, true_s, x_sems, w_sems, sems,
    ) = refs[-17:]
    own = token_rank() * rows
    mine = token_rank() // 2
    loads = fetch(pieces, x_s, lambda j: x_sems.at[j])
    weights = []
    for n in range(count):
        at = shard_rows(place, first + n, part)
        weights.append([
            pltpu.make_async_copy(wq.at[at, :], wq_s.at[n], w_sems.at[2 * n]),
            pltpu.make_async_copy(wk.at[at, :], wk_s.at[n], w_sems.at[2 * n + 1]),
        ])
    before = [
        pltpu.make_async_copy(q_before, q_s, sems.at[0]),
        pltpu.make_async_copy(kv_before.at[:, :HD], true_s, sems.at[1]),
    ]
    tables = [
        pltpu.make_async_copy(cos_k.at[mine], cos_q, sems.at[2]),
        pltpu.make_async_copy(sin_k.at[mine], sin_q, sems.at[3]),
    ] + interleave(keys_n, keys_d, keys, lambda j: sems.at[4 + j])
    for copy in before + loads + sum(weights, []) + tables:
        copy.start()
    for copy in before + loads:
        copy.wait()
    for n in range(count):
        for copy in weights[n]:
            copy.wait()
        x = x_s[:, n * part : (n + 1) * part]
        q_s[...] += jnp.dot(x, wq_s[n], preferred_element_type=jnp.float32)
        true_s[...] += jnp.dot(x, wk_s[n], preferred_element_type=jnp.float32)
    code = codes[...]
    for level in range(levels):
        entry = weight * (book[level : level + 1, :] - true_s[...])
        bins[level : level + 1, :] = jnp.sum(
            jnp.where(code == level, entry, 0.0), axis=0, keepdims=True
        )
    for copy in tables:
        copy.wait()
    for h in range(wide):
        x = q_s[:, h * HD : (h + 1) * HD]
        turned = (x * cos_q[...] + pltpu.roll(x, HD // 2, 1) * sin_q[...]).astype(jnp.bfloat16)
        q_rot[h] = turned
        q_t[h] = turned.T
    scan_totals(own, info, early, rows, 0, heads, q_t, keys, peak_s, mass_s, log_total)


def scan_totals(own, info, early, rows, begin, heads, q_t, keys, peak_s, mass_s, log_total):
    peak_s[...] = jnp.full_like(peak_s, NEG_BIG)
    mass_s[...] = jnp.zeros_like(mass_s)

    def body(b, masked):
        base = pl.multiple_of(b * BLOCK, BLOCK)
        k = keys[b].reshape(BLOCK, HD)
        if masked:
            seen = visible_block(base, BLOCK, own, early[...], rows)
        for h in range(heads):
            t = lax.dot_general(k, q_t[begin + h], NN, preferred_element_type=jnp.float32)
            t = t * (SCALE * LOG2E)
            if masked:
                t = jnp.where(seen, t, NEG_BIG)
            old = peak_s[h : h + 1, :]
            new = jnp.maximum(old, jnp.max(t, axis=0, keepdims=True))
            fresh = jnp.sum(jnp.exp2(t - new), axis=0, keepdims=True)
            mass_s[h : h + 1, :] = mass_s[h : h + 1, :] * jnp.exp2(old - new) + fresh
            peak_s[h : h + 1, :] = new

    over_blocks(own, info, rows, body)
    log_total[...] = peak_s[...] + jnp.log(mass_s[...]) * LOG2E


def late_stats_kernel(
    begin, heads, rows, info, early, q_t, keys_n, keys_d, log_total, peak_s, mass_s, keys, sems,
):
    copies = interleave(keys_n, keys_d, keys, lambda j: sems.at[j])
    for copy in copies:
        copy.start()
    for copy in copies:
        copy.wait()
    own = token_rank() * rows
    scan_totals(own, info, early, rows, begin, heads, q_t, keys, peak_s, mass_s, log_total)


def grad_kernel(
    heads, rows, levels,
    info, q_rot, q_t, log_total_0, log_total_1, early, cot, cot_t, init,
    keys_n, keys_d, cos_n, cos_d, sin_n, sin_d, codes_n, codes_d, v_own, v_x, v_y1, v_y2, v_y3, v_core,
    out, bins, probs_s, out_s, delta_s, acc_s, values, keys, cos_k, sin_k, codes, held, sems,
):
    me = token_rank()
    own, first = me * rows, info[0]
    part = heads // 2
    early_heads = log_total_0.shape[0]
    log_total = [log_total_0.at[h : h + 1, :] for h in range(early_heads)]
    log_total += [log_total_1.at[h : h + 1, :] for h in range(heads - early_heads)]
    copies = interleave(keys_n, keys_d, keys, lambda j: sems.at[16 + j])
    for j, (bits, ref, at) in enumerate(slots((v_own, v_x, v_y1, v_y2, v_y3, v_core))):
        start = pl.multiple_of((me ^ bits) * rows, rows)
        copies.append(
            pltpu.make_async_copy(
                ref.at[at * rows : (at + 1) * rows, :], values.at[pl.ds(start, rows), :], sems.at[j]
            )
        )
    late = interleave(cos_n, cos_d, cos_k, lambda j: sems.at[18 + j])
    late += interleave(sin_n, sin_d, sin_k, lambda j: sems.at[20 + j])
    late += interleave(codes_n, codes_d, codes, lambda j: sems.at[22 + j])
    for copy in copies + late:
        copy.start()
    out_s[...] = jnp.zeros_like(out_s)
    for copy in copies:
        copy.wait()

    def forward(b, masked):
        base = pl.multiple_of(b * BLOCK, BLOCK)
        k = keys[b].reshape(BLOCK, HD)
        v = values[pl.ds(base, BLOCK), :]
        if masked:
            seen = visible_block(base, BLOCK, own, early[...], rows)
        for h in range(heads):
            s = lax.dot_general(k, q_t[h], NN, preferred_element_type=jnp.float32)
            p = jnp.exp2(s * (SCALE * LOG2E) - log_total[h][...])
            if masked:
                p = jnp.where(seen, p, 0.0)
            probs_s[b - first, h] = p
            out_s[h] += lax.dot_general(
                p.astype(jnp.bfloat16), v, TN, preferred_element_type=jnp.float32
            )

    over_blocks(own, info, rows, forward)
    for h in range(heads):
        o = out_s[h].astype(jnp.bfloat16)
        out[:, h * HD : (h + 1) * HD] = o
        prod = cot[:, h * HD : (h + 1) * HD].astype(jnp.float32) * o.astype(jnp.float32)
        delta_s[h : h + 1, :] = jnp.sum(prod.T, axis=0, keepdims=True)
    acc_s[...] = jnp.zeros_like(acc_s)
    last = (own + rows + BLOCK - 1) // BLOCK
    for copy in late:
        copy.wait()

    def add_bins(b, dk):
        dk = dk * SCALE
        cosine, sine = cos_k[b].reshape(BLOCK, HD), sin_k[b].reshape(BLOCK, HD)
        g = dk * cosine - pltpu.roll(dk, HD // 2, 1) * sine
        code = codes[b].reshape(BLOCK, HD).astype(jnp.float32)
        for level in range(levels):
            chosen = jnp.where(code == level, g, 0.0)
            acc_s[level] += jnp.sum(chosen.reshape(BLOCK // 8, 8, HD), axis=0)

    held[...] = jnp.zeros_like(held)

    @pl.loop(first, last)
    def _(b):
        base = pl.multiple_of(b * BLOCK, BLOCK)
        v = values[pl.ds(base, BLOCK), :]
        add_bins(jnp.maximum(b - 1, first), held[...])
        dk = jnp.zeros((BLOCK, HD), jnp.float32)
        for h in range(heads):
            dp = lax.dot_general(v, cot_t[h], NN, preferred_element_type=jnp.float32)
            ds = (probs_s[b - first, h] * (dp - delta_s[h : h + 1, :])).astype(jnp.bfloat16)
            dk = dk + lax.dot_general(ds, q_rot[h], NN, preferred_element_type=jnp.float32)
        held[...] = dk

    add_bins(last - 1, held[...])
    bins[...] = init[...] + jnp.sum(acc_s[...], axis=1)


def anywhere():
    return pl.BlockSpec(memory_space=pl.ANY)


def vmem():
    return pl.BlockSpec(memory_space=pltpu.VMEM)


def smem():
    return pl.BlockSpec(memory_space=pltpu.SMEM)


def cost(flops, size):
    return pl.CostEstimate(flops=flops, bytes_accessed=size, transcendentals=0)


def shards(hidden, w_query, w_key, w_value, key_codes, codebook, positions, cotangent):
    rows, part = hidden.shape
    width = w_query.shape[1]
    heads = width // HD
    levels = codebook.shape[1]
    ranks = lax.axis_size("tokens")
    total = rows * ranks
    group = lax.axis_size("tensor")
    rank = lax.axis_index("tensor")
    me = lax.axis_index("tokens")
    own = me * rows
    bf16, f32 = jnp.bfloat16, jnp.float32

    cross = lambda x, d: lax.ppermute(x, "tokens", [(i, i ^ d) for i in range(ranks)])

    def everyone(x, first, second, third):
        x_side = first(cross(x, 2))
        pair = second(jnp.concatenate([x, x_side], axis=0))
        y_side = [cross(pair, 4 * y) for y in (1, 2, 3)]
        core = cross(third(jnp.concatenate([pair] + y_side, axis=0)), 1)
        return (x, x_side, *y_side, core)

    def after(*others):
        return lambda v: lax.optimization_barrier((v, others))[0]

    flip = [(i, i ^ 1) for i in range(group)]
    up = [(i, (i + 2) % group) for i in range(group)]
    down = [(i, (i - 2) % group) for i in range(group)]
    send = functools.partial(lax.ppermute, axis_name="tensor")
    n = part // 2
    low = send(hidden, perm=up)
    high = send(hidden, perm=down)
    other = send(hidden, perm=flip)
    places = positions[None, :]
    packed, early, info = pl.pallas_call(
        functools.partial(pack_kernel, rows),
        out_shape=(
            jax.ShapeDtypeStruct((rows + TAIL, HD), bf16),
            jax.ShapeDtypeStruct((1, rows), jnp.int32),
            jax.ShapeDtypeStruct((2,), jnp.int32),
        ),
        in_specs=[vmem()] * 2,
        out_specs=(vmem(), vmem(), smem()),
        name="pack",
    )(key_codes, places)
    book = codebook.T

    mate = rank ^ 1
    turn = lambda x, by: (x + by) % group
    shard = [rank, turn(rank, -2), turn(rank, 2), mate]
    shard += [turn(rank, 4), turn(mate, -2), turn(mate, 2), turn(mate, 4)]
    place = jnp.stack(shard).astype(jnp.int32)

    y_side = [cross(packed, 4 * y) for y in (1, 2, 3)]
    column = jnp.concatenate([packed] + y_side, axis=0)
    x_side = cross(column, 2)
    low, high, other = after(column)((low, high, other))
    far_a = send(low[:, :n], perm=up)
    far_b = send(high[:, n:], perm=down)
    half = group // 2
    q_sum, kv_sum = pl.pallas_call(
        functools.partial(project_kernel, half, part),
        out_shape=(jax.ShapeDtypeStruct((rows, width), f32), jax.ShapeDtypeStruct((rows, 2 * HD), f32)),
        in_specs=[smem()] + [anywhere()] * (3 + half),
        out_specs=(vmem(),) * 2,
        scratch_shapes=[
            pltpu.VMEM((half, rows, part), bf16),
            pltpu.VMEM((half, part, width), bf16),
            pltpu.VMEM((half, part, 2 * HD), bf16),
            pltpu.SemaphoreType.DMA((4 * half,)),
        ],
        compiler_params=pltpu.CompilerParams(vmem_limit_bytes=50 << 20),
        cost_estimate=cost(1 << 34, 0),
        name="project",
    )(place, w_query, w_key, w_value, hidden, low, high, other)
    far_a, far_b, other, x_side = after(kv_sum)((far_a, far_b, other, x_side))
    other_low = send(other, perm=up)
    other_high = send(other, perm=down)
    other_far_a = send(far_a, perm=flip)
    other_far_b = send(far_b, perm=flip)
    core = cross(jnp.concatenate([column, x_side], axis=0), 1)
    packed = (packed, *y_side, x_side, core)

    rest = [far_a, far_b, other_low, other_high, other_far_a, other_far_b]
    value = pl.pallas_call(
        functools.partial(value_kernel, half, half, part),
        out_shape=jax.ShapeDtypeStruct((rows, HD), bf16),
        in_specs=[smem()] + [anywhere()] * (2 + len(rest)),
        out_specs=vmem(),
        scratch_shapes=[
            pltpu.VMEM((rows, half * part), bf16),
            pltpu.VMEM((half, part, HD), bf16),
            pltpu.VMEM((rows, HD), f32),
            pltpu.SemaphoreType.DMA((half + len(rest) + 1,)),
        ],
        compiler_params=pltpu.CompilerParams(vmem_limit_bytes=50 << 20),
        cost_estimate=cost(0, 0),
        name="value",
    )(place, w_value, kv_sum, *rest)

    def prep(near, book, *pieces):
        few = ranks // 2
        shapes = [(few, rows, HD)] * 4
        kinds = [bf16, f32, f32, bf16]
        return pl.pallas_call(
            functools.partial(prep_kernel, near, rows, few, levels),
            out_shape=[jax.ShapeDtypeStruct(size, kind) for size, kind in zip(shapes, kinds)]
            + [jax.ShapeDtypeStruct((heads, HD, rows), bf16)] * near,
            in_specs=[vmem()] + [anywhere()] * len(pieces),
            out_specs=[anywhere()] * 4 + [vmem()] * near,
            scratch_shapes=[pltpu.VMEM((few * (rows + TAIL), HD), bf16)]
            + [pltpu.VMEM(size, kind) for size, kind in zip(shapes, kinds)]
            + [pltpu.SemaphoreType.DMA((few + 1,)), pltpu.SemaphoreType.DMA((4,))]
            + [pltpu.VMEM((rows, width), bf16)] * near,
            compiler_params=pltpu.CompilerParams(vmem_limit_bytes=58 << 20),
            cost_estimate=cost(1 << 34 if near else 1 << 32, 0),
            name="prep",
        )(book, *pieces)

    *near, cot_t = prep(True, after(kv_sum)(book), *packed[:5], cotangent)
    distant = prep(False, after(value)(book), packed[5])
    keys = distant[0]

    count = heads * 3 // 8
    totals = []

    def second(pair):
        pair, ready = lax.optimization_barrier((pair, place))
        found = pl.pallas_call(
            functools.partial(
                stats_kernel, count, heads, rows, levels, levels / total, half, half, part
            ),
            out_shape=(
                jax.ShapeDtypeStruct((heads, rows, HD), bf16),
                jax.ShapeDtypeStruct((heads, HD, rows), bf16),
                jax.ShapeDtypeStruct((count, rows), f32),
                jax.ShapeDtypeStruct((levels, HD), f32),
            ),
            in_specs=[smem()] * 2 + [vmem()] * 3 + [anywhere()] * (8 + len(rest)),
            out_specs=(vmem(),) * 4,
            scratch_shapes=[pltpu.VMEM((count, rows), f32)] * 2
            + [pltpu.VMEM((rows, HD), f32)] * 2
            + [
                pltpu.VMEM((ranks // 2, 2, rows, HD), bf16),
                pltpu.VMEM((rows, half * part), bf16),
                pltpu.VMEM((half, part, width), bf16),
                pltpu.VMEM((half, part, HD), bf16),
                pltpu.VMEM((rows, width), f32),
                pltpu.VMEM((rows, HD), f32),
                pltpu.SemaphoreType.DMA((len(rest),)),
                pltpu.SemaphoreType.DMA((2 * half,)),
                pltpu.SemaphoreType.DMA((6,)),
            ],
            compiler_params=pltpu.CompilerParams(vmem_limit_bytes=50 << 20),
            cost_estimate=cost(1 << 34, 0),
            name="stats",
        )(
            ready, info, early, key_codes, book, near[1], near[2], near[0], distant[0],
            q_sum, kv_sum, w_query, w_key, *rest,
        )
        totals.extend(found)
        return pair

    values = everyone(value, after(keys), second, lambda v: after(totals[2])(v))
    q_rot, q_t, log_total_0, init = totals
    late, _ = lax.optimization_barrier((q_t, values[2:5]))
    log_total_1 = pl.pallas_call(
        functools.partial(late_stats_kernel, count, heads - count, rows),
        out_shape=jax.ShapeDtypeStruct((heads - count, rows), f32),
        in_specs=[smem()] + [vmem()] * 2 + [anywhere()] * 2,
        out_specs=vmem(),
        scratch_shapes=[pltpu.VMEM((heads - count, rows), f32)] * 2
        + [pltpu.VMEM((ranks // 2, 2, rows, HD), bf16), pltpu.SemaphoreType.DMA((2,))],
        compiler_params=pltpu.CompilerParams(vmem_limit_bytes=32 << 20),
        cost_estimate=cost(1 << 34, 0),
        name="stats_late",
    )(info, early, late, near[0], distant[0])

    most = total // BLOCK
    attention_out, local = pl.pallas_call(
        functools.partial(grad_kernel, heads, rows, levels),
        out_shape=(
            jax.ShapeDtypeStruct((rows, width), bf16),
            jax.ShapeDtypeStruct((levels, HD), f32),
        ),
        in_specs=[smem()] + [vmem()] * 8 + [anywhere()] * 14,
        out_specs=(vmem(),) * 2,
        scratch_shapes=[
            pltpu.VMEM((min(most, 7), heads, BLOCK, rows), f32),
            pltpu.VMEM((heads, rows, HD), f32),
            pltpu.VMEM((heads, rows), f32),
            pltpu.VMEM((levels, 8, HD), f32),
            pltpu.VMEM((total, HD), bf16),
            pltpu.VMEM((ranks // 2, 2, rows, HD), bf16),
            pltpu.VMEM((ranks // 2, 2, rows, HD), f32),
            pltpu.VMEM((ranks // 2, 2, rows, HD), f32),
            pltpu.VMEM((ranks // 2, 2, rows, HD), bf16),
            pltpu.VMEM((BLOCK, HD), f32),
            pltpu.SemaphoreType.DMA((24,)),
        ],
        compiler_params=pltpu.CompilerParams(vmem_limit_bytes=44 << 20),
        cost_estimate=cost(8 * rows * width * total, 8 << 20),
        name="grad",
    )(
        info, q_rot, q_t, log_total_0, log_total_1, early, cotangent, cot_t, init,
        *[table for both in zip(near, distant) for table in both], *values,
    )
    for d in (1, 2, 4, 12):
        local = local + cross(local, d)
    return (attention_out, local.T)


def solution(mesh):
    placed = (
        P("tokens", "tensor"),
        P(None, "tensor"),
        P(None, "tensor"),
        P(None, "tensor"),
        P("tokens", "tensor"),
        P("tensor", None),
        P("tokens"),
        P("tokens", "tensor"),
    )
    return jax.shard_map(
        shards,
        mesh=mesh,
        in_specs=placed,
        out_specs=(P("tokens", "tensor"), P("tensor", None)),
        check_vma=False,
    )
```
